32 devices in a mesh: seq: 16 (over z, y, x), head: 2 (over core).
Axes of the slice: x: 2, y: 2, z: 4, core: 2. Of those that a mesh axis runs over, the one named last changes fastest.
Arguments:
- queries: bfloat16 [8192, 8, 512], P('seq', 'head'), may hold values from -8 to 8
- token_keys: bfloat16 [8192, 8, 512], P('seq', 'head'), may hold values from -8 to 8
- token_values: bfloat16 [8192, 8, 512], P('seq', 'head'), may hold values from -8 to 8
- fast_weights: bfloat16 [512, 8, 3, 512], P(None, 'head'), may hold values from -0.25 to 0.25
- learn_rate: float32 [8], P('head'), may hold values from 1 to 10
- out_gain: float32 [8, 512], P('head'), may hold values from 0.5 to 1.5
- group_lengths: int32 [2], replicated, may hold values from 1 to 6144, 8192 in all
- slot_order: int32 [8192], P('seq'), may hold values from 0 to 8191, as said below
Outputs:
- balanced_out: bfloat16 [8192, 8, 512], P('seq', 'head')
The draws below stay inside these ranges and needn't reach their ends.
Inputs may be any that keep to these rules, and one draw needn't show every extreme that they name: slot_order is a permutation of the positions; slot j, with r = j % 512, holds a position of the block [e * 512, (e + 1) * 512) with e = r // 32. `group_lengths`: the two lengths sum to 8192; each lies between 2048 and 6144.
All inputs are finite; a program needn't handle non-finite values.
Results may differ from the reference program's by a relative error of at most 0.0075.
Values may be sent and summed in bfloat16 or wider, within the bound.
No kernel may reach another device: no remote copies, remote signals or barrier semaphores. Data moves between devices by JAX's collectives and lax.ppermute only.
A program may use at most 192 MiB of HBM per device.

```python
import math
import jax
import jax.numpy as jnp
import numpy as np
from jax import lax

HEADS = 8
HEAD_DIM = 512
FAST_HIDDEN = 512
WINDOW = 2048
TOK_DEV = 512
TOKENS = 8192


def paired_rows(key):
    array_shape = (TOKENS, HEADS, HEAD_DIM)
    query_source = jax.random.fold_in(key, 101)
    key_source = jax.random.fold_in(key, 102)
    query_rows = jax.random.truncated_normal(query_source, -6.0, 6.0, array_shape, jnp.float32)
    key_rows = jax.random.truncated_normal(key_source, -6.0, 6.0, array_shape, jnp.float32)
    return (query_rows.astype(jnp.bfloat16), key_rows.astype(jnp.bfloat16))


def draw_queries(key, part):
    return paired_rows(key)[0]


def draw_token_keys(key, part):
    return paired_rows(key)[1]


def draw_token_values(key, part):
    array_shape = (TOKENS, HEADS, HEAD_DIM)
    head_pos = jnp.arange(HEADS, dtype=jnp.float32) / max(HEADS - 1, 1)
    scales = 0.6 * 3.0 ** head_pos
    base = jax.random.truncated_normal(key, -4.0, 4.0, array_shape, jnp.float32)
    return (base * scales[None, :, None]).astype(jnp.bfloat16)


def draw_slot_order(key, part):
    source_count = TOKENS // TOK_DEV
    seg_rows = TOK_DEV // source_count
    block_keys = jax.random.split(key, source_count)
    shuffled = jax.vmap(lambda block_key: jax.random.permutation(block_key, TOK_DEV))(block_keys)
    placed = shuffled.astype(jnp.int32) + (jnp.arange(source_count, dtype=jnp.int32) * TOK_DEV)[:, None]
    placed = placed.reshape(source_count, source_count, seg_rows)
    return jnp.transpose(placed, (1, 0, 2)).reshape(TOKENS).astype(jnp.int32)


def levels(stream_key, extent, cuts, smallest, high):
    def one(axis_at, parts):
        draws = jax.random.uniform(jax.random.fold_in(jax.random.fold_in(stream_key, 6), axis_at), (parts,), jnp.float32, smallest / len(cuts), high / len(cuts))
        return jnp.repeat(jnp.exp(draws), extent[axis_at] // parts).reshape((-1,) + (1,) * (len(extent) - axis_at - 1))

    factor_of = one(*cuts[0])
    for cut in cuts[1:]:
        factor_of = factor_of * one(*cut)
    return factor_of


def split_up(count, total, most, skew):
    loads = [(1 << 20) // math.isqrt(grade ** skew) + 1 for grade in range(2, count + 1)]
    surplus, given = total - most - (count - 1), [1] * (count - 1)
    while surplus > 0:
        free = [i for i in range(count - 1) if given[i] < most]
        mass, remaining = sum([loads[i] for i in free]), surplus
        for i in free:
            extra = min(most - given[i], max(1, remaining * loads[i] // mass), surplus)
            given[i] = given[i] + extra
            surplus = surplus - extra
    return np.array([most] + given)


def uneven_parts(key, count, total, limit, slope):
    if count == 2:
        one = jax.random.randint(key, (), max(1, total - limit), min(limit, total - 1) + 1)
        return jnp.stack([one, total - one])
    tallies = jnp.asarray(split_up(count, total, limit, slope), jnp.int32)
    couples = (count - 1) // 2
    donor, taker = tallies[1:1 + 2 * couples:2], tallies[2:2 + 2 * couples:2]
    room = jnp.minimum(donor - 1, limit - taker)
    shifted = jax.random.randint(jax.random.fold_in(key, 1), (couples,), 0, 1 << 20) % (room + 1)
    tallies = tallies.at[1:1 + 2 * couples:2].set(donor - shifted).at[2:2 + 2 * couples:2].set(taker + shifted)
    return tallies[jax.random.permutation(jax.random.fold_in(key, 2), count)]


def noise(own_key, extent, deviation, most, cuts=(), kind=jnp.bfloat16):
    drawn = jax.random.normal(own_key, extent, jnp.float32) * deviation
    if len(cuts) > 0:
        drawn = levels(own_key, extent, cuts, -0.22, 0.18) * drawn
    return jnp.clip(drawn, min=-most, max=most).astype(kind)


def setup_inputs(seed: int = 0) -> dict:
    keys = jax.random.split(jax.random.key(seed), 9)
    queries = draw_queries(jax.random.fold_in(keys[8], 71), 0)
    token_keys = draw_token_keys(jax.random.fold_in(keys[8], 71), 0)
    token_values = draw_token_values(jax.random.fold_in(keys[8], 71), 0)
    fast_weights = noise(keys[3], (FAST_HIDDEN, HEADS, 3, HEAD_DIM), HEAD_DIM ** -0.5, 0.25, ((1, 2),))
    learn_rate = jnp.clip(jnp.exp(math.log(10.0) - 2.3025851 * jax.random.uniform(keys[4], (HEADS,), jnp.float32) ** levels(keys[4], (HEADS,), ((0, 2),), -0.2, 0.2)), 1.0, 10.0)
    out_gain = jnp.clip(1.0 + 0.1 * jax.random.normal(keys[5], (HEADS, HEAD_DIM), jnp.float32), 0.5, 1.5)
    group_lengths = uneven_parts(keys[6], 2, TOKENS, TOKENS * 3 // 4, 0).astype(jnp.int32)
    slot_order = draw_slot_order(jax.random.fold_in(keys[8], 71), 0)
    return {"queries": queries, "token_keys": token_keys, "token_values": token_values, "fast_weights": fast_weights, "learn_rate": learn_rate, "out_gain": out_gain, "group_lengths": group_lengths, "slot_order": slot_order}


eps = 1e-06

def head_attention(query_head, key_head, value_head):
    block_rows = 512
    padded_keys = jnp.concatenate([jnp.zeros((WINDOW, HEAD_DIM), key_head.dtype), key_head], axis=0)
    padded_values = jnp.concatenate([jnp.zeros((WINDOW, HEAD_DIM), value_head.dtype), value_head], axis=0)
    score_scale = 1.0 / math.sqrt(HEAD_DIM)

    def attend(block_index):
        first_row = block_index * block_rows
        query_rows = lax.dynamic_slice_in_dim(query_head, first_row, block_rows, 0)
        key_rows = lax.dynamic_slice_in_dim(padded_keys, first_row, WINDOW + block_rows, 0)
        value_rows = lax.dynamic_slice_in_dim(padded_values, first_row, WINDOW + block_rows, 0)
        scores = jnp.dot(query_rows, key_rows.T, preferred_element_type=jnp.float32) * score_scale
        query_pos = first_row + jnp.arange(block_rows, dtype=jnp.int32)[:, None]
        key_pos = first_row - WINDOW + jnp.arange(WINDOW + block_rows, dtype=jnp.int32)[None, :]
        allowed = (key_pos <= query_pos) & (key_pos > query_pos - WINDOW) & (key_pos >= 0)
        scores = jnp.where(allowed, scores, -jnp.inf)
        row_max = lax.optimization_barrier(jnp.max(scores, axis=-1, keepdims=True))
        expo = jnp.exp(scores - row_max)
        prob_rows = (expo / lax.optimization_barrier(jnp.sum(expo, axis=-1, keepdims=True))).astype(jnp.bfloat16)
        return jnp.dot(prob_rows, value_rows, preferred_element_type=jnp.float32).astype(jnp.bfloat16)
    blocks = lax.map(attend, jnp.arange(TOKENS // block_rows, dtype=jnp.int32))
    return blocks.reshape(TOKENS, HEAD_DIM)

def swiglu_rows(inputs, weights):
    gate_pre = jnp.dot(inputs, weights[:, 0, :].T, preferred_element_type=jnp.float32)
    up_pre = jnp.dot(inputs, weights[:, 1, :].T, preferred_element_type=jnp.float32)
    hidden_act = (jax.nn.silu(gate_pre) * up_pre).astype(jnp.bfloat16)
    return jnp.dot(hidden_act, weights[:, 2, :], preferred_element_type=jnp.float32).astype(jnp.bfloat16)

def head_fast(query_head, key_head, value_head, weight_head, rate_value, first_len):
    member = jnp.arange(TOKENS, dtype=jnp.int32) < first_len
    group_count = first_len.astype(jnp.float32)
    gate_pre = jnp.dot(key_head, weight_head[:, 0, :].T, preferred_element_type=jnp.float32)
    up_pre = jnp.dot(key_head, weight_head[:, 1, :].T, preferred_element_type=jnp.float32)
    activation = (jax.nn.silu(gate_pre) * up_pre).astype(jnp.bfloat16)
    masked_values = jnp.where(member[:, None], value_head, jnp.zeros_like(value_head))
    back_act = jnp.dot(masked_values, weight_head[:, 2, :].T, preferred_element_type=jnp.float32)
    sig_gate = jax.nn.sigmoid(gate_pre)
    grad_up = (back_act * gate_pre * sig_gate).astype(jnp.bfloat16)
    grad_gate = (back_act * up_pre * sig_gate * (1.0 + gate_pre * (1.0 - sig_gate))).astype(jnp.bfloat16)
    term_gate = jnp.dot(grad_gate.T, key_head, preferred_element_type=jnp.float32)
    term_up = jnp.dot(grad_up.T, key_head, preferred_element_type=jnp.float32)
    term_down = jnp.dot(activation.T, masked_values, preferred_element_type=jnp.float32)
    summed = jnp.stack([term_gate, term_up, term_down], axis=1)
    previous = weight_head.astype(jnp.float32)
    updated = previous + rate_value / group_count * summed
    old_norm = jnp.sqrt(lax.optimization_barrier(jnp.sum(previous * previous, axis=-1, keepdims=True)) + eps)
    new_norm = jnp.sqrt(lax.optimization_barrier(jnp.sum(updated * updated, axis=-1, keepdims=True)) + eps)
    new_weights = (updated * (old_norm / new_norm)).astype(jnp.bfloat16)
    first_out = swiglu_rows(query_head, weight_head)
    second_out = swiglu_rows(query_head, new_weights)
    return jnp.where(member[:, None], first_out, second_out)

def reference(queries, token_keys, token_values, fast_weights, learn_rate, out_gain, group_lengths, slot_order):
    first_len = group_lengths[0]
    head_queries = jnp.swapaxes(queries, 0, 1)
    head_keys = jnp.swapaxes(token_keys, 0, 1)
    head_values = jnp.swapaxes(token_values, 0, 1)
    attention = lax.map(lambda packed: head_attention(packed[0], packed[1], packed[2]), (head_queries, head_keys, head_values))
    head_weights = jnp.transpose(fast_weights, (1, 0, 2, 3))
    fast_out = lax.map(lambda packed: head_fast(packed[0], packed[1], packed[2], packed[3], packed[4], first_len), (head_queries, head_keys, head_values, head_weights, learn_rate))
    summed_rows = jnp.swapaxes(attention.astype(jnp.float32) + fast_out.astype(jnp.float32), 0, 1)
    power = lax.optimization_barrier(jnp.mean(summed_rows * summed_rows, axis=(1, 2)))
    normed = summed_rows * lax.rsqrt(power + eps)[:, None, None] * out_gain[None, :, :]
    return jnp.take(normed, slot_order.astype(jnp.int32), axis=0).astype(jnp.bfloat16)
```

```python
import functools
import math

import jax
import jax.numpy as jnp
from jax import lax
from jax.experimental import pallas as pl
from jax.experimental.pallas import tpu as pltpu
from jax.sharding import PartitionSpec as P

WINDOW = 2048
NEG = -1e30
VMEM_BYTES = 58 * 1024 * 1024

eps = 1e-06

NT = (((1,), (1,)), ((), ()))
TN = (((0,), (0,)), ((), ()))
NN = (((1,), (0,)), ((), ()))


def dot(left, right, dims):
    return lax.dot_general(left, right, dims, preferred_element_type=jnp.float32)


def swap_pairs(count, distance):
    return [(index, index ^ distance) for index in range(count)]


def plane_pairs(count, steps):
    return [(index, index + steps) for index in range(count - steps)]


def spread_heads(value, member, count, order):
    group = value.shape[1]
    by_head = jnp.transpose(value, (1, 0, 2))
    pieces = [None] * group
    for distance in order:
        piece = lax.dynamic_index_in_dim(by_head, member ^ distance, 0, keepdims=False)
        if distance:
            piece = lax.ppermute(piece, "seq", swap_pairs(count, distance))
        pieces[distance] = piece
    return pieces


def grad_kernel(group, tok, info_ref, w_ref, *refs):
    k_any, v_any = refs[:group], refs[group : 2 * group]
    out_ref, kbuf, vbuf, acc, sems = refs[2 * group :]
    plane, member, first_len = info_ref[0], info_ref[1], info_ref[2]
    copies = []
    for d in range(group):
        pair = (
            pltpu.make_async_copy(k_any[d], kbuf.at[d], sems.at[0, d]),
            pltpu.make_async_copy(v_any[d], vbuf.at[d], sems.at[1, d]),
        )
        for copy in pair:
            copy.start()
        copies.append(pair)
    acc[...] = jnp.zeros_like(acc)
    hidden = w_ref.shape[1]
    part = min(256, hidden)
    for d in range(group):
        for copy in copies[d]:
            copy.wait()
        first_tok = (plane * group + (member ^ d)) * tok

        @pl.when(first_tok < first_len)
        def _():
            keys = kbuf[d]
            token = first_tok + lax.broadcasted_iota(jnp.int32, (tok, 1), 0)
            values = jnp.where(token < first_len, vbuf[d].astype(jnp.float32), 0.0)
            values = values.astype(jnp.bfloat16)
            for f in range(0, hidden, part):
                rows = pl.ds(f, part)
                gate = dot(keys, w_ref[0, rows, :], NT)
                up = dot(keys, w_ref[1, rows, :], NT)
                back = dot(values, w_ref[2, rows, :], NT)
                sig = jax.nn.sigmoid(gate)
                silu = gate * sig
                act = (silu * up).astype(jnp.bfloat16)
                grad_up = (back * silu).astype(jnp.bfloat16)
                grad_gate = (back * up * sig * (1.0 + gate * (1.0 - sig))).astype(jnp.bfloat16)
                acc[0, rows, :] += dot(grad_gate, keys, TN)
                acc[1, rows, :] += dot(grad_up, keys, TN)
                acc[2, rows, :] += dot(act, values, TN)

    out_ref[...] = acc[...].astype(out_ref.dtype)


def weight_sums(info, weights, keys, values):
    group = len(keys)
    tok, width = keys[0].shape
    rows, hidden, _ = weights.shape
    flops = 2 * 6 * group * tok * hidden * width
    return pl.pallas_call(
        functools.partial(grad_kernel, group, tok),
        out_shape=jax.ShapeDtypeStruct(weights.shape, jnp.bfloat16),
        in_specs=[
            pl.BlockSpec(memory_space=pltpu.SMEM),
            pl.BlockSpec(memory_space=pltpu.VMEM),
        ]
        + [pl.BlockSpec(memory_space=pl.ANY)] * (2 * group),
        out_specs=pl.BlockSpec(memory_space=pltpu.VMEM),
        scratch_shapes=[
            pltpu.VMEM((group, tok, width), jnp.bfloat16),
            pltpu.VMEM((group, tok, width), jnp.bfloat16),
            pltpu.VMEM(weights.shape, jnp.float32),
            pltpu.SemaphoreType.DMA((2, group)),
        ],
        compiler_params=pltpu.CompilerParams(vmem_limit_bytes=VMEM_BYTES),
        cost_estimate=pl.CostEstimate(
            flops=flops,
            bytes_accessed=2 * (2 * group * tok * width + 2 * rows * hidden * width),
            transcendentals=group * tok * hidden,
        ),
        name="weight_sums",
    )(info, weights, *keys, *values)


def attend_kernel(group, tok, slots, block, info_ref, *refs):
    count = group * slots
    q_any, k_any, v_any = refs[:group], refs[group : group + count], refs[group + count : group + 2 * count]
    out_ref, qbuf, kbuf, vbuf, sems = refs[group + 2 * count :]
    plane, member = info_ref[0], info_ref[1]
    width = qbuf.shape[-1]
    copies = []
    for d in range(group):
        place = pl.ds(pl.multiple_of((member ^ d) * tok, tok), tok)
        copies.append(pltpu.make_async_copy(q_any[d], qbuf.at[place], sems.at[0, d]))
    for s in range(slots):
        for d in range(group):
            place = pl.ds(pl.multiple_of((s * group + (member ^ d)) * tok, tok), tok)
            at = s * group + d
            copies.append(pltpu.make_async_copy(k_any[at], kbuf.at[place], sems.at[1, at]))
            copies.append(pltpu.make_async_copy(v_any[at], vbuf.at[place], sems.at[2, at]))
    for copy in copies:
        copy.start()
    for copy in copies:
        copy.wait()
    behind = (slots - 1) * group * tok
    span = behind + block
    scale = math.log2(math.e) / math.sqrt(width)
    first_key = jnp.maximum(behind - plane * group * tok, 0)
    row = lax.broadcasted_iota(jnp.int32, (block, span), 0)
    col = lax.broadcasted_iota(jnp.int32, (block, span), 1)
    band = (col > row + (behind - WINDOW)) & (col <= row + behind)

    def one(step, carry):
        first_row = pl.multiple_of(step * block, block)
        rows = qbuf[pl.ds(first_row, block), :]
        keys = kbuf[pl.ds(first_row, span), :]
        values = vbuf[pl.ds(first_row, span), :]
        scores = dot(rows, keys, NT)
        scores = jnp.where(band & (col >= first_key - first_row), scores, NEG)
        top = jnp.max(scores, axis=1, keepdims=True)
        expo = jnp.exp2((scores - top) * scale)
        total = jnp.sum(expo, axis=1, keepdims=True)
        mixed = dot(expo.astype(jnp.bfloat16), values, NN) / total
        out_ref[pl.ds(first_row, block), :] = mixed.astype(out_ref.dtype)
        return carry

    lax.fori_loop(0, group * tok // block, one, 0)


def window_attention(info, queries, keys, values):
    group = len(queries)
    slots = len(keys) // group
    tok, width = queries[0].shape
    block = min(256, tok)
    span = (slots - 1) * group * tok + block
    total = group * tok
    return pl.pallas_call(
        functools.partial(attend_kernel, group, tok, slots, block),
        out_shape=jax.ShapeDtypeStruct((total, width), jnp.bfloat16),
        in_specs=[pl.BlockSpec(memory_space=pltpu.SMEM)]
        + [pl.BlockSpec(memory_space=pl.ANY)] * (group + 2 * len(keys)),
        out_specs=pl.BlockSpec(memory_space=pltpu.VMEM),
        scratch_shapes=[
            pltpu.VMEM((total, width), jnp.bfloat16),
            pltpu.VMEM((slots * total, width), jnp.bfloat16),
            pltpu.VMEM((slots * total, width), jnp.bfloat16),
            pltpu.SemaphoreType.DMA((3, slots * group)),
        ],
        compiler_params=pltpu.CompilerParams(vmem_limit_bytes=VMEM_BYTES),
        cost_estimate=pl.CostEstimate(
            flops=4 * total * span * width,
            bytes_accessed=2 * width * total * (2 + 2 * slots),
            transcendentals=total * span,
        ),
        name="window_attention",
    )(info, *queries, *keys, *values)


def finish_kernel(group, tok, count, info_ref, rate_ref, w_ref, sum_ref, att_ref, place_ref, *refs):
    q_refs = refs[:group]
    out_ref, new_w, rows_buf = refs[group:]
    plane, member, first_len = info_ref[0], info_ref[1], info_ref[2]
    step = rate_ref[0] / first_len.astype(jnp.float32)
    hidden = w_ref.shape[1]
    for c in range(w_ref.shape[0]):
        previous = w_ref[c].astype(jnp.float32)
        updated = previous + step * sum_ref[c].astype(jnp.float32)
        old_norm = jnp.sqrt(jnp.sum(previous * previous, axis=1, keepdims=True) + eps)
        new_norm = jnp.sqrt(jnp.sum(updated * updated, axis=1, keepdims=True) + eps)
        new_w[c] = (updated * (old_norm / new_norm)).astype(new_w.dtype)

    def apply(rows, weights):
        gate = dot(rows, weights[0], NT)
        up = dot(rows, weights[1], NT)
        act = (gate * jax.nn.sigmoid(gate) * up).astype(jnp.bfloat16)
        return dot(act, weights[2], NN)

    seg = tok // count
    for d in range(group):
        other = member ^ d
        first_tok = (plane * group + other) * tok
        place = pl.ds(pl.multiple_of(other * tok, tok), tok)

        @pl.when(first_tok < first_len)
        def _():
            rows_buf[...] = apply(q_refs[d][...], w_ref)

        @pl.when(first_tok + tok > first_len)
        def _():
            token = first_tok + lax.broadcasted_iota(jnp.int32, (tok, 1), 0)
            rows_buf[...] = jnp.where(token < first_len, rows_buf[...], apply(q_refs[d][...], new_w))

        rows = (rows_buf[...] + att_ref[place, :].astype(jnp.float32)).astype(jnp.bfloat16)
        wanted = place_ref[other]
        pick = (wanted == lax.broadcasted_iota(jnp.int32, (tok, tok), 1)).astype(jnp.bfloat16)
        sorted_rows = dot(pick, rows, NN).reshape(count, seg, rows.shape[-1])
        out_ref[:, other, :, :] = sorted_rows.astype(out_ref.dtype)


def finish_rows(info, rate, weights, sums, attention, places, queries, count):
    group = len(queries)
    tok, width = queries[0].shape
    hidden = weights.shape[1]
    seg = tok // count
    return pl.pallas_call(
        functools.partial(finish_kernel, group, tok, count),
        out_shape=jax.ShapeDtypeStruct((count, group, seg, width), jnp.bfloat16),
        in_specs=[pl.BlockSpec(memory_space=pltpu.SMEM)] * 2
        + [pl.BlockSpec(memory_space=pltpu.VMEM)] * (4 + group),
        out_specs=pl.BlockSpec(memory_space=pltpu.VMEM),
        scratch_shapes=[
            pltpu.VMEM(weights.shape, jnp.bfloat16),
            pltpu.VMEM((tok, width), jnp.float32),
        ],
        compiler_params=pltpu.CompilerParams(vmem_limit_bytes=VMEM_BYTES),
        cost_estimate=pl.CostEstimate(
            flops=2 * group * tok * width * (3 * hidden + tok),
            bytes_accessed=2 * (3 * group * tok * width + 2 * 3 * hidden * width),
            transcendentals=group * tok * hidden,
        ),
        name="finish_rows",
    )(info, rate, weights, sums, attention, places, *queries)


def total_over_planes(own, group, count):
    planes = count // group
    if planes > 8:
        groups = [[plane * group + m for plane in range(planes)] for m in range(group)]
        return lax.psum(own, "seq", axis_index_groups=groups)
    sums = [own[c] for c in range(own.shape[0])]
    for hop in range(1, planes):
        pairs = [((hop - 1) * group + m, hop * group + m) for m in range(group)]
        for c in range(len(sums)):
            came = lax.ppermute(sums[c], "seq", pairs)
            sums[c] = (sums[c].astype(jnp.float32) + came.astype(jnp.float32)).astype(own.dtype)
    return jnp.stack(sums)


def per_device(
    queries, token_keys, token_values, fast_weights, learn_rate, out_gain, group_lengths, slot_order
):
    tok, group, width = queries.shape
    count = lax.axis_size("seq")
    seg = tok // count
    planes = count // group
    behind = -(-WINDOW // (group * tok))
    position = lax.axis_index("seq")
    plane, member = position // group, position % group
    first_len = group_lengths[0]
    info = jnp.stack([plane, member, first_len]).astype(jnp.int32)

    order = list(range(group))
    keys = spread_heads(token_keys, member, count, order)
    values = spread_heads(token_values, member, count, order)
    rows = spread_heads(queries, member, count, order)
    all_keys, all_values = [], []
    for back in range(behind, 0, -1):
        pairs = plane_pairs(count, back * group)
        for d in range(group):
            all_keys.append(lax.ppermute(keys[d], "seq", pairs))
            all_values.append(lax.ppermute(values[d], "seq", pairs))
    all_keys, all_values = all_keys + keys, all_values + values

    weights = lax.dynamic_index_in_dim(fast_weights, member, 1, keepdims=False)
    weights = jnp.transpose(weights, (1, 0, 2))
    rate = lax.dynamic_slice_in_dim(learn_rate, member, 1)
    sums = total_over_planes(weight_sums(info, weights, keys, values), group, count)

    asked = lax.all_gather(slot_order, "seq").reshape(count, count, seg)
    asked = lax.dynamic_slice_in_dim(asked, plane * group, group, 1) % tok
    places = jnp.transpose(asked, (1, 0, 2)).reshape(group, tok, 1)

    attention = window_attention(info, rows, all_keys, all_values)
    leaving = finish_rows(info, rate, weights, sums, attention, places, rows, count)
    came = lax.all_to_all(leaving, "seq", split_axis=0, concat_axis=0, tiled=True)
    came = came.reshape(planes, group, group, seg, width).astype(jnp.float32)
    power = lax.psum(jnp.sum(came * came, axis=(1, 4)), "head")
    scale = lax.rsqrt(power / (group * lax.axis_size("head") * width) + eps)
    ordered = jnp.transpose(came * scale[:, None, :, :, None], (0, 2, 3, 1, 4))
    return (ordered.reshape(tok, group, width) * out_gain[None]).astype(jnp.bfloat16)


def solution(mesh):
    return jax.shard_map(
        per_device,
        mesh=mesh,
        in_specs=(
            P("seq", "head", None),
            P("seq", "head", None),
            P("seq", "head", None),
            P(None, "head", None, None),
            P("head"),
            P("head", None),
            P(),
            P("seq"),
        ),
        out_specs=P("seq", "head", None),
        check_vma=False,
    )
```

```python
import functools
import math

import jax
import jax.numpy as jnp
from jax import lax
from jax.experimental import pallas as pl
from jax.experimental.pallas import tpu as pltpu
from jax.sharding import PartitionSpec as P

WINDOW = 2048
NEG = -1e30
MIB = 1024 * 1024

eps = 1e-06

NT = (((1,), (1,)), ((), ()))
TN = (((0,), (0,)), ((), ()))
NN = (((1,), (0,)), ((), ()))

ANY = pl.BlockSpec(memory_space=pl.ANY)
SMEM = pl.BlockSpec(memory_space=pltpu.SMEM)
VMEM = pl.BlockSpec(memory_space=pltpu.VMEM)


def dot(left, right, dims):
    return lax.dot_general(left, right, dims, preferred_element_type=jnp.float32)


def params(mib):
    return pltpu.CompilerParams(vmem_limit_bytes=mib * MIB)


def swap_pairs(count, distance):
    return [(index, index ^ distance) for index in range(count)]


def plane_pairs(count, steps):
    return [(index, index + steps) for index in range(count - steps)]


def split_kernel(total, group, info_ref, *refs):
    x_refs = refs[:total]
    outs = refs[len(refs) - group - 2 : len(refs) - 2]
    buf, sems = refs[-2:]
    member = info_ref[1]
    for t, x_ref in enumerate(x_refs):
        buf[:, t] = jnp.swapaxes(x_ref[...], 0, 1)
    copies = [
        pltpu.make_async_copy(buf.at[member ^ d], outs[d], sems.at[d]) for d in range(group)
    ]
    for copy in copies:
        copy.start()
    for copy in copies:
        copy.wait()


def split_heads(info, arrays, after=()):
    tok, group, width = arrays[0].shape
    total = len(arrays)
    return pl.pallas_call(
        functools.partial(split_kernel, total, group),
        out_shape=[jax.ShapeDtypeStruct((total, tok, width), jnp.bfloat16)] * group,
        in_specs=[SMEM] + [VMEM] * total + [ANY] * len(after),
        out_specs=[ANY] * group,
        scratch_shapes=[
            pltpu.VMEM((group, total, tok, width), jnp.bfloat16),
            pltpu.SemaphoreType.DMA((group,)),
        ],
        compiler_params=params(20),
        cost_estimate=pl.CostEstimate(
            flops=0, bytes_accessed=4 * total * group * tok * width, transcendentals=0
        ),
        name="split_heads",
    )(info, *arrays, *after)


def trade(pieces, count):
    return [
        lax.ppermute(piece, "seq", swap_pairs(count, d)) if d else piece
        for d, piece in enumerate(pieces)
    ]


def grad_kernel(group, tok, info_ref, w_ref, *refs):
    kv_any = refs[:group]
    own, sent, kvbuf, acc, sems, out_sems = (
        refs[group],
        refs[group + 1 : group + 4],
        *refs[group + 4 :],
    )
    plane, member, first_len = info_ref[0], info_ref[1], info_ref[2]
    copies = [pltpu.make_async_copy(kv_any[d], kvbuf.at[d], sems.at[d]) for d in range(group)]
    for copy in copies:
        copy.start()
    acc[...] = jnp.zeros_like(acc)
    hidden = w_ref.shape[1]
    part = min(256, hidden)
    for d in range(group):
        copies[d].wait()
    def piece(d, carry):
        first_tok = (plane * group + (member ^ d)) * tok

        @pl.when(first_tok < first_len)
        def _():
            keys = kvbuf[d, 0]
            token = first_tok + lax.broadcasted_iota(jnp.int32, (tok, 1), 0)
            values = jnp.where(token < first_len, kvbuf[d, 1].astype(jnp.float32), 0.0)
            values = values.astype(jnp.bfloat16)
            for f in range(0, hidden, part):
                rows = pl.ds(f, part)
                gate = dot(keys, w_ref[0, rows, :], NT)
                up = dot(keys, w_ref[1, rows, :], NT)
                back = dot(values, w_ref[2, rows, :], NT)
                sig = jax.nn.sigmoid(gate)
                silu = gate * sig
                act = (silu * up).astype(jnp.bfloat16)
                grad_up = (back * silu).astype(jnp.bfloat16)
                grad_gate = (back * up * sig * (1.0 + gate * (1.0 - sig))).astype(jnp.bfloat16)
                acc[0, rows, :] += dot(grad_gate, keys, TN)
                acc[1, rows, :] += dot(grad_up, keys, TN)
                acc[2, rows, :] += dot(act, values, TN)

        return carry

    lax.fori_loop(0, group, piece, 0)
    keep = pltpu.make_async_copy(acc, own, out_sems.at[0])
    keep.start()
    for c in range(3):
        sent[c][...] = acc[c].astype(sent[c].dtype)
    keep.wait()


def weight_sums(info, weights, pairs):
    group = len(pairs)
    _, tok, width = pairs[0].shape
    rows, hidden, _ = weights.shape
    return pl.pallas_call(
        functools.partial(grad_kernel, group, tok),
        out_shape=[jax.ShapeDtypeStruct(weights.shape, jnp.float32)]
        + [jax.ShapeDtypeStruct((hidden, width), jnp.bfloat16)] * rows,
        in_specs=[SMEM, VMEM] + [ANY] * group,
        out_specs=[ANY] + [VMEM] * rows,
        scratch_shapes=[
            pltpu.VMEM((group, 2, tok, width), jnp.bfloat16),
            pltpu.VMEM(weights.shape, jnp.float32),
            pltpu.SemaphoreType.DMA((group,)),
            pltpu.SemaphoreType.DMA((1,)),
        ],
        compiler_params=params(28),
        cost_estimate=pl.CostEstimate(
            flops=2 * 6 * group * tok * hidden * width,
            bytes_accessed=2 * (2 * group * tok * width + 2 * rows * hidden * width),
            transcendentals=group * tok * hidden,
        ),
        name="weight_sums",
    )(info, weights, *pairs)


def lanes_sum(expo):
    total = expo[:, :128]
    for lane in range(128, expo.shape[1], 128):
        total = total + expo[:, lane : lane + 128]
    return total


def soft_steps(parts, scale, fresh, acc, top, norm):
    scores = [
        dot(rows, keys, NT) if mask is None else jnp.where(mask, dot(rows, keys, NT), NEG)
        for _, rows, keys, _, mask in parts
    ]
    done = []
    for (where, _, _, _, _), score in zip(parts, scores):
        peak = jnp.max(score, axis=1, keepdims=True)
        if fresh:
            decay = None
        else:
            before = top[where, :1]
            peak = jnp.maximum(peak, before)
            decay = jnp.exp2((before - peak) * scale)
        expo = jnp.exp2((score - peak) * scale)
        done.append((peak, decay, lanes_sum(expo), expo.astype(jnp.bfloat16)))
    for (where, _, _, values, _), (peak, decay, total, expo) in zip(parts, done):
        mixed = dot(expo, values, NN)
        wide = (peak.shape[0], 128)
        top[where, :] = jnp.broadcast_to(peak, wide)
        if fresh:
            norm[where, :] = total
            acc[where, :] = mixed
        else:
            norm[where, :] = norm[where, :] * decay + total
            acc[where, :] = acc[where, :] * decay + mixed


def score_scale(width):
    return math.log2(math.e) / math.sqrt(width)


def triangle(rows, cols, first_row, first_col, lower):
    row = first_row + lax.broadcasted_iota(jnp.int32, (rows, cols), 0)
    col = first_col + lax.broadcasted_iota(jnp.int32, (rows, cols), 1)
    return col <= row if lower else col > row


def own_kernel(group, tok, part, info_ref, *refs):
    q_any, kv_any = refs[:group], refs[group : 2 * group]
    acc_ref, top_ref, norm_ref, qbuf, kvbuf, sems = refs[2 * group :]
    member = info_ref[1]
    copies = []
    for d in range(group):
        copies.append(pltpu.make_async_copy(q_any[d], qbuf.at[pl.ds(d, 1)], sems.at[0, d]))
        copies.append(pltpu.make_async_copy(kv_any[d], kvbuf.at[d], sems.at[1, d]))
    for copy in copies:
        copy.start()
    for copy in copies:
        copy.wait()
    scale = score_scale(qbuf.shape[-1])

    def piece(d, carry):
        at = member ^ d
        acc, top, norm = acc_ref.at[d], top_ref.at[d], norm_ref.at[d]
        parts = []
        for r in range(0, tok, part):
            where, keys = pl.ds(r, part), pl.ds(0, r + part)
            mask = triangle(part, r + part, r, 0, True)
            parts.append((where, qbuf[d, where], kvbuf[d, 0, keys], kvbuf[d, 1, keys], mask))
        soft_steps(parts, scale, True, acc, top, norm)

        def earlier(other, carry):
            e = member ^ other
            parts = []
            for r in range(0, tok, part):
                where = pl.ds(r, part)
                parts.append((where, qbuf[d, where], kvbuf[e, 0], kvbuf[e, 1], None))
            soft_steps(parts, scale, False, acc, top, norm)
            return carry

        lax.fori_loop(0, at, earlier, 0)
        return carry

    lax.fori_loop(0, group, piece, 0)


def own_attention(info, queries, pairs):
    group = len(queries)
    _, tok, width = pairs[0].shape
    part = min(256, tok)
    return pl.pallas_call(
        functools.partial(own_kernel, group, tok, part),
        out_shape=[
            jax.ShapeDtypeStruct((group, tok, width), jnp.float32),
            jax.ShapeDtypeStruct((group, tok, 128), jnp.float32),
            jax.ShapeDtypeStruct((group, tok, 128), jnp.float32),
        ],
        in_specs=[SMEM] + [ANY] * (2 * group),
        out_specs=[VMEM] * 3,
        scratch_shapes=[
            pltpu.VMEM((group, tok, width), jnp.bfloat16),
            pltpu.VMEM((group, 2, tok, width), jnp.bfloat16),
            pltpu.SemaphoreType.DMA((2, group)),
        ],
        compiler_params=params(28),
        cost_estimate=pl.CostEstimate(
            flops=2 * group * group * tok * tok * width,
            bytes_accessed=width * group * tok * 10,
            transcendentals=group * group * tok * tok // 2,
        ),
        name="own_attention",
    )(info, *queries, *pairs)


def fast_kernel(group, tok, hops, info_ref, rate_ref, w_ref, own_ref, *refs):
    came, q_any = refs[: 3 * hops], refs[3 * hops : 3 * hops + group]
    out_ref, new_w, qbuf, sems = refs[3 * hops + group :]
    plane, member, first_len = info_ref[0], info_ref[1], info_ref[2]
    copies = [
        pltpu.make_async_copy(q_any[d], qbuf.at[pl.ds(d, 1)], sems.at[d]) for d in range(group)
    ]
    for copy in copies:
        copy.start()
    step = rate_ref[0] / first_len.astype(jnp.float32)
    for c in range(3):
        previous = w_ref[c].astype(jnp.float32)
        summed = own_ref[c]
        for hop in range(hops):
            summed = summed + came[3 * hop + c][...].astype(jnp.float32)
        updated = previous + step * summed
        old_norm = jnp.sqrt(jnp.sum(previous * previous, axis=1, keepdims=True) + eps)
        new_norm = jnp.sqrt(jnp.sum(updated * updated, axis=1, keepdims=True) + eps)
        new_w[c] = (updated * (old_norm / new_norm)).astype(new_w.dtype)
    for copy in copies:
        copy.wait()

    def apply(rows, weights):
        gate = dot(rows, weights[0], NT)
        up = dot(rows, weights[1], NT)
        act = (gate * jax.nn.sigmoid(gate) * up).astype(jnp.bfloat16)
        return dot(act, weights[2], NN).astype(jnp.bfloat16)

    def piece(d, carry):
        first_tok = (plane * group + (member ^ d)) * tok

        @pl.when(first_tok < first_len)
        def _():
            out_ref[d] = apply(qbuf[d], w_ref)

        @pl.when(first_tok + tok > first_len)
        def _():
            token = first_tok + lax.broadcasted_iota(jnp.int32, (tok, 1), 0)
            second = apply(qbuf[d], new_w).astype(jnp.float32)
            first = out_ref[d].astype(jnp.float32)
            out_ref[d] = jnp.where(token < first_len, first, second).astype(jnp.bfloat16)

        return carry

    lax.fori_loop(0, group, piece, 0)


def fast_rows(info, rate, weights, own, came, queries):
    group = len(queries)
    _, tok, width = queries[0].shape
    hidden = weights.shape[1]
    hops = len(came) // 3
    return pl.pallas_call(
        functools.partial(fast_kernel, group, tok, hops),
        out_shape=jax.ShapeDtypeStruct((group, tok, width), jnp.bfloat16),
        in_specs=[SMEM] * 2 + [VMEM] * (2 + 3 * hops) + [ANY] * group,
        out_specs=VMEM,
        scratch_shapes=[
            pltpu.VMEM(weights.shape, jnp.bfloat16),
            pltpu.VMEM((group, tok, width), jnp.bfloat16),
            pltpu.SemaphoreType.DMA((group,)),
        ],
        compiler_params=params(28),
        cost_estimate=pl.CostEstimate(
            flops=2 * 3 * group * tok * width * hidden,
            bytes_accessed=2 * (2 * group * tok * width + 6 * hidden * width),
            transcendentals=group * tok * hidden,
        ),
        name="fast_rows",
    )(info, rate, weights, own, *came, *queries)


def cross_kernel(group, tok, count, behind, part, info_ref, *refs):
    pieces = behind * group
    q_any, refs = refs[:group], refs[group:]
    kv_any, refs = refs[:pieces], refs[pieces:]
    acc_any, top_ref, norm_ref, fast_ref, place_ref, out_ref = refs[:6]
    qbuf, kvbuf, acc_ref, sems, kv_sems = refs[6:]
    plane, member = info_ref[0], info_ref[1]
    kv_copies = [
        pltpu.make_async_copy(kv_any[at], kvbuf.at[at], kv_sems.at[at]) for at in range(pieces)
    ]
    copies = []
    for d in range(group):
        copies.append(pltpu.make_async_copy(q_any[d], qbuf.at[pl.ds(d, 1)], sems.at[0, d]))
        copies.append(pltpu.make_async_copy(acc_any.at[d], acc_ref.at[d], sems.at[1, d]))
    for copy in kv_copies + copies:
        copy.start()
    for copy in kv_copies + copies:
        copy.wait()
    scale = score_scale(qbuf.shape[-1])
    seg = tok // count
    valid = jnp.maximum(behind - plane, 0) * group

    def at_piece(order):
        return order // group * group + (member ^ (order % group))

    def piece(d, carry):
        at = member ^ d
        acc, top, norm = acc_ref.at[d], top_ref.at[d], norm_ref.at[d]

        @pl.when(at >= valid)
        def _():
            parts = []
            for r in range(0, tok, part):
                where, keys = pl.ds(r, part), pl.ds(r, tok - r)
                mask = triangle(part, tok - r, r, r, False)
                parts.append((where, qbuf[d, where], kvbuf[d, 0, keys], kvbuf[d, 1, keys], mask))
            soft_steps(parts, scale, False, acc, top, norm)

        def later(other, carry):
            e = at_piece(other)
            parts = []
            for r in range(0, tok, part):
                where = pl.ds(r, part)
                parts.append((where, qbuf[d, where], kvbuf[e, 0], kvbuf[e, 1], None))
            soft_steps(parts, scale, False, acc, top, norm)
            return carry

        lax.fori_loop(jnp.maximum(at + 1, valid), pieces, later, 0)
        total = jnp.sum(norm[...], axis=1, keepdims=True)
        mixed = (acc[...] / total).astype(jnp.bfloat16)
        rows = (mixed.astype(jnp.float32) + fast_ref[d].astype(jnp.float32)).astype(jnp.bfloat16)
        pick = place_ref[at] == lax.broadcasted_iota(jnp.int32, (tok, tok), 1)
        sorted_rows = dot(pick.astype(jnp.bfloat16), rows, NN)
        out_ref[:, at] = sorted_rows.reshape(count, seg, rows.shape[-1]).astype(out_ref.dtype)
        return carry

    lax.fori_loop(0, group, piece, 0)


def cross_rows(info, queries, earlier, state, fast, places, count):
    group = len(queries)
    _, tok, width = queries[0].shape
    behind = len(earlier) // group
    part = min(256, tok)
    return pl.pallas_call(
        functools.partial(cross_kernel, group, tok, count, behind, part),
        out_shape=jax.ShapeDtypeStruct((count, group, tok // count, width), jnp.bfloat16),
        in_specs=[SMEM] + [ANY] * (group + len(earlier) + 1) + [VMEM] * 4,
        out_specs=VMEM,
        scratch_shapes=[
            pltpu.VMEM((group, tok, width), jnp.bfloat16),
            pltpu.VMEM((len(earlier), 2, tok, width), jnp.bfloat16),
            pltpu.VMEM((group, tok, width), jnp.float32),
            pltpu.SemaphoreType.DMA((2, group)),
            pltpu.SemaphoreType.DMA((len(earlier),)),
        ],
        compiler_params=params(36),
        cost_estimate=pl.CostEstimate(
            flops=2 * group * group * tok * tok * width,
            bytes_accessed=width * group * tok * 16,
            transcendentals=group * group * tok * tok // 2,
        ),
        name="cross_rows",
    )(info, *queries, *earlier, *state, fast, places)


def norm_kernel(came_ref, scale_ref, gain_ref, out_ref):
    group = out_ref.shape[1]
    for h in range(group):
        pass
    scaled = came_ref[0].astype(jnp.float32) * scale_ref[...] * gain_ref[...]
    out_ref[...] = jnp.swapaxes(scaled.astype(out_ref.dtype), 0, 1)


def norm_rows(came, scale, gain):
    planes, group, rows, width = came.shape
    return pl.pallas_call(
        norm_kernel,
        grid=(planes,),
        out_shape=jax.ShapeDtypeStruct((planes * rows, group, width), jnp.bfloat16),
        in_specs=[
            pl.BlockSpec((1, group, rows, width), lambda z: (z, 0, 0, 0)),
            pl.BlockSpec((1, rows, 1), lambda z: (z, 0, 0)),
            pl.BlockSpec((group, 1, width), lambda z: (0, 0, 0)),
        ],
        out_specs=pl.BlockSpec((rows, group, width), lambda z: (z, 0, 0)),
        compiler_params=params(20),
        name="norm_rows",
    )(came, scale, gain)


def forward_sums(own, sent, group, count):
    planes = count // group
    if planes > 8:
        groups = [[plane * group + m for plane in range(planes)] for m in range(group)]
        whole = lax.psum(own.astype(jnp.bfloat16), "seq", axis_index_groups=groups)
        return whole.astype(jnp.float32), []
    came = []
    for hop in range(1, planes):
        pairs = [((hop - 1) * group + m, hop * group + m) for m in range(group)]
        if hop > 1:
            sent = [
                (own[c] + came[-3 + c].astype(jnp.float32)).astype(jnp.bfloat16) for c in range(3)
            ]
        came.extend([lax.ppermute(sent[c], "seq", pairs) for c in range(3)])
    return own, came


def asked_places(slot_order, plane, member, group, count):
    tok = slot_order.shape[0]
    seg, planes = tok // count, count // group
    wanted = slot_order.reshape(planes, group, seg) % tok
    if planes > 8:
        asked = lax.all_gather(wanted.reshape(tok), "seq").reshape(count, count, seg)
        asked = lax.dynamic_slice_in_dim(asked, plane * group, group, 1)
        return jnp.transpose(asked, (1, 0, 2)).reshape(group, tok, 1)
    column = jnp.zeros_like(wanted)
    for step in range(planes):
        target = (plane + step) % planes
        part = lax.dynamic_index_in_dim(wanted, target, 0, keepdims=True)
        if step:
            pairs = [(index, (index + step * group) % count) for index in range(count)]
            part = lax.ppermute(part, "seq", pairs)
        source = (plane - step) % planes
        column = lax.dynamic_update_slice_in_dim(column, part, source, 0)
    whole = jnp.zeros((planes, group, group, seg), jnp.int32)
    for d in range(group):
        part = lax.ppermute(column, "seq", swap_pairs(count, d)) if d else column
        whole = lax.dynamic_update_slice_in_dim(whole, part[:, None], member ^ d, 1)
    return jnp.transpose(whole, (2, 0, 1, 3)).reshape(group, tok, 1)


def per_device(
    queries, token_keys, token_values, fast_weights, learn_rate, out_gain, group_lengths, slot_order
):
    tok, group, width = queries.shape
    count = lax.axis_size("seq")
    seg = tok // count
    planes = count // group
    behind = WINDOW // (group * tok)
    position = lax.axis_index("seq")
    plane, member = position // group, position % group
    info = jnp.stack([plane, member, group_lengths[0]]).astype(jnp.int32)

    mine = split_heads(info, [token_keys, token_values])
    pairs = trade(mine, count)
    earlier = []
    for back in range(behind, 0, -1):
        shift = plane_pairs(count, back * group)
        earlier.extend([lax.ppermute(pair, "seq", shift) for pair in pairs])
    asked = trade(split_heads(info, [queries], pairs[1:2]), count)

    weights = lax.dynamic_index_in_dim(fast_weights, member, 1, keepdims=False)
    weights = jnp.transpose(weights, (1, 0, 2))
    rate = lax.dynamic_slice_in_dim(learn_rate, member, 1)
    own, *sent = weight_sums(info, weights, pairs)
    own, came = forward_sums(own, sent, group, count)
    state = own_attention(info, asked, pairs)
    places = asked_places(slot_order, plane, member, group, count)
    fast = fast_rows(info, rate, weights, own, came, asked)
    leaving = cross_rows(info, asked, earlier, state, fast, places, count)

    came = lax.all_to_all(leaving, "seq", split_axis=0, concat_axis=0, tiled=True)
    came = came.reshape(planes, group, group * seg, width)
    wide = came.astype(jnp.float32)
    power = lax.psum(jnp.sum(wide * wide, axis=(1, 3)), "head")
    scale = lax.rsqrt(power / (group * lax.axis_size("head") * width) + eps)
    return norm_rows(came, scale[:, :, None], out_gain[:, None, :])


def solution(mesh):
    return jax.shard_map(
        per_device,
        mesh=mesh,
        in_specs=(
            P("seq", "head", None),
            P("seq", "head", None),
            P("seq", "head", None),
            P(None, "head", None, None),
            P("head"),
            P("head", None),
            P(),
            P("seq"),
        ),
        out_specs=P("seq", "head", None),
        check_vma=False,
    )
```

```python
import functools
import math

import jax
import jax.numpy as jnp
from jax import lax
from jax.experimental import pallas as pl
from jax.experimental.pallas import tpu as pltpu
from jax.sharding import PartitionSpec as P

WINDOW = 2048
NEG = -1e30
MIB = 1024 * 1024

eps = 1e-06

NT = (((1,), (1,)), ((), ()))
TN = (((0,), (0,)), ((), ()))
NN = (((1,), (0,)), ((), ()))

ANY = pl.BlockSpec(memory_space=pl.ANY)
SMEM = pl.BlockSpec(memory_space=pltpu.SMEM)
VMEM = pl.BlockSpec(memory_space=pltpu.VMEM)


def dot(left, right, dims):
    return lax.dot_general(left, right, dims, preferred_element_type=jnp.float32)


def params(mib):
    return pltpu.CompilerParams(vmem_limit_bytes=mib * MIB)


def swap_pairs(count, distance):
    return [(index, index ^ distance) for index in range(count)]


def plane_pairs(count, steps):
    return [(index, index + steps) for index in range(count - steps)]


def split_kernel(total, group, info_ref, *refs):
    x_refs = refs[:total]
    outs = refs[len(refs) - group - 2 : len(refs) - 2]
    buf, sems = refs[-2:]
    member = info_ref[1]
    for t, x_ref in enumerate(x_refs):
        buf[:, t] = jnp.swapaxes(x_ref[...], 0, 1)
    copies = [
        pltpu.make_async_copy(buf.at[member ^ d], outs[d], sems.at[d]) for d in range(group)
    ]
    for copy in copies:
        copy.start()
    for copy in copies:
        copy.wait()


def split_heads(info, arrays, after=()):
    tok, group, width = arrays[0].shape
    total = len(arrays)
    return pl.pallas_call(
        functools.partial(split_kernel, total, group),
        out_shape=[jax.ShapeDtypeStruct((total, tok, width), jnp.bfloat16)] * group,
        in_specs=[SMEM] + [VMEM] * total + [ANY] * len(after),
        out_specs=[ANY] * group,
        scratch_shapes=[
            pltpu.VMEM((group, total, tok, width), jnp.bfloat16),
            pltpu.SemaphoreType.DMA((group,)),
        ],
        compiler_params=params(20),
        cost_estimate=pl.CostEstimate(
            flops=0, bytes_accessed=4 * total * group * tok * width, transcendentals=0
        ),
        name="split_heads",
    )(info, *arrays, *after)


def trade(pieces, count):
    return [
        lax.ppermute(piece, "seq", swap_pairs(count, d)) if d else piece
        for d, piece in enumerate(pieces)
    ]


def grad_kernel(group, tok, first, last, carried, info_ref, w_ref, *refs):
    pieces = last - first
    kv_any, refs = refs[:pieces], refs[pieces:]
    kvbuf, acc, sems, acc_sem = refs[-4:]
    plane, member, first_len = info_ref[0], info_ref[1], info_ref[2]
    copies = [pltpu.make_async_copy(kv_any[n], kvbuf.at[n], sems.at[n]) for n in range(pieces)]
    for copy in copies:
        copy.start()
    if carried:
        load = pltpu.make_async_copy(refs[0], acc, acc_sem.at[0])
        load.start()
        load.wait()
    else:
        acc[...] = jnp.zeros_like(acc)
    hidden = w_ref.shape[1]
    part = min(256, hidden)
    for copy in copies:
        copy.wait()

    def piece(n, carry):
        first_tok = (plane * group + (member ^ (first + n))) * tok

        @pl.when(first_tok < first_len)
        def _():
            keys = kvbuf[n, 0]
            token = first_tok + lax.broadcasted_iota(jnp.int32, (tok, 1), 0)
            values = jnp.where(token < first_len, kvbuf[n, 1].astype(jnp.float32), 0.0)
            values = values.astype(jnp.bfloat16)
            for f in range(0, hidden, part):
                rows = pl.ds(f, part)
                gate = dot(keys, w_ref[0, rows, :], NT)
                up = dot(keys, w_ref[1, rows, :], NT)
                back = dot(values, w_ref[2, rows, :], NT)
                sig = jax.nn.sigmoid(gate)
                silu = gate * sig
                act = (silu * up).astype(jnp.bfloat16)
                grad_up = (back * silu).astype(jnp.bfloat16)
                grad_gate = (back * up * sig * (1.0 + gate * (1.0 - sig))).astype(jnp.bfloat16)
                acc[0, rows, :] += dot(grad_gate, keys, TN)
                acc[1, rows, :] += dot(grad_up, keys, TN)
                acc[2, rows, :] += dot(act, values, TN)

        return carry

    lax.fori_loop(0, pieces, piece, 0)
    whole = last == group
    outs = refs[len(refs) - 4 - (4 if whole else 1) : len(refs) - 4]
    keep = pltpu.make_async_copy(acc, outs[0], acc_sem.at[1])
    keep.start()
    for c, sent in enumerate(outs[1:]):
        sent[...] = acc[c].astype(sent.dtype)
    keep.wait()


def weight_sums(info, weights, pairs, first, last, carried=(), after=()):
    group = len(pairs)
    _, tok, width = pairs[0].shape
    rows, hidden, _ = weights.shape
    pieces = last - first
    sent = rows if last == group else 0
    return pl.pallas_call(
        functools.partial(grad_kernel, group, tok, first, last, len(carried)),
        out_shape=[jax.ShapeDtypeStruct(weights.shape, jnp.float32)]
        + [jax.ShapeDtypeStruct((hidden, width), jnp.bfloat16)] * sent,
        in_specs=[SMEM, VMEM] + [ANY] * (pieces + len(carried) + len(after)),
        out_specs=[ANY] + [VMEM] * sent,
        scratch_shapes=[
            pltpu.VMEM((pieces, 2, tok, width), jnp.bfloat16),
            pltpu.VMEM(weights.shape, jnp.float32),
            pltpu.SemaphoreType.DMA((pieces,)),
            pltpu.SemaphoreType.DMA((2,)),
        ],
        compiler_params=params(28),
        cost_estimate=pl.CostEstimate(
            flops=2 * 6 * pieces * tok * hidden * width,
            bytes_accessed=2 * (2 * pieces * tok * width + 2 * rows * hidden * width),
            transcendentals=pieces * tok * hidden,
        ),
        name="weight_sums",
    )(info, weights, *pairs[first:last], *carried, *after)


def lanes_sum(expo):
    total = expo[:, :128]
    for lane in range(128, expo.shape[1], 128):
        total = total + expo[:, lane : lane + 128]
    return total


def soft_steps(parts, scale, fresh, acc, top, norm):
    scores = [
        dot(rows, keys, NT) if mask is None else jnp.where(mask, dot(rows, keys, NT), NEG)
        for _, rows, keys, _, mask in parts
    ]
    done = []
    for (where, _, _, _, _), score in zip(parts, scores):
        peak = jnp.max(score, axis=1, keepdims=True)
        if fresh:
            decay = None
        else:
            before = top[where, :1]
            peak = jnp.maximum(peak, before)
            decay = jnp.exp2((before - peak) * scale)
        expo = jnp.exp2((score - peak) * scale)
        done.append((peak, decay, lanes_sum(expo), expo.astype(jnp.bfloat16)))
    for (where, _, _, values, _), (peak, decay, total, expo) in zip(parts, done):
        mixed = dot(expo, values, NN)
        wide = (peak.shape[0], 128)
        top[where, :] = jnp.broadcast_to(peak, wide)
        if fresh:
            norm[where, :] = total
            acc[where, :] = mixed
        else:
            norm[where, :] = norm[where, :] * decay + total
            acc[where, :] = acc[where, :] * decay + mixed


def soft_close(scale, acc, top, norm, out_ref, level_ref):
    total = jnp.sum(norm[...], axis=1, keepdims=True)
    out_ref[...] = (acc[...] / jnp.maximum(total, 1e-30)).astype(out_ref.dtype)
    level = top[...] * scale + jnp.log2(jnp.maximum(total, 1e-30))
    level_ref[...] = jnp.transpose(level)[:8]


def as_column(rows):
    return jnp.transpose(jnp.concatenate([rows] * 16, axis=0))[:, :1]


def score_scale(width):
    return math.log2(math.e) / math.sqrt(width)


def triangle(rows, cols, first_row, first_col, lower):
    row = first_row + lax.broadcasted_iota(jnp.int32, (rows, cols), 0)
    col = first_col + lax.broadcasted_iota(jnp.int32, (rows, cols), 1)
    return col <= row if lower else col > row


def own_kernel(group, tok, part, info_ref, *refs):
    q_any, kv_any = refs[:group], refs[group : 2 * group]
    out_ref, level_ref, acc, top, norm, qbuf, kvbuf, sems = refs[-8:]
    member = info_ref[1]
    copies = []
    for d in range(group):
        copies.append(pltpu.make_async_copy(q_any[d], qbuf.at[pl.ds(d, 1)], sems.at[0, d]))
        copies.append(pltpu.make_async_copy(kv_any[d], kvbuf.at[d], sems.at[1, d]))
    for copy in copies:
        copy.start()
    for copy in copies:
        copy.wait()
    scale = score_scale(qbuf.shape[-1])

    def piece(d, carry):
        parts = []
        for r in range(0, tok, part):
            where, keys = pl.ds(r, part), pl.ds(0, r + part)
            mask = triangle(part, r + part, r, 0, True)
            parts.append((where, qbuf[d, where], kvbuf[d, 0, keys], kvbuf[d, 1, keys], mask))
        soft_steps(parts, scale, True, acc, top, norm)

        def earlier(other, carry):
            e = member ^ other
            parts = []
            for r in range(0, tok, part):
                where = pl.ds(r, part)
                parts.append((where, qbuf[d, where], kvbuf[e, 0], kvbuf[e, 1], None))
            soft_steps(parts, scale, False, acc, top, norm)
            return carry

        lax.fori_loop(0, member ^ d, earlier, 0)
        soft_close(scale, acc, top, norm, out_ref.at[d], level_ref.at[d])
        return carry

    lax.fori_loop(0, group, piece, 0)


def soft_shapes(group, tok, width):
    return [
        jax.ShapeDtypeStruct((group, tok, width), jnp.bfloat16),
        jax.ShapeDtypeStruct((group, 8, tok), jnp.float32),
    ]


def soft_scratch(tok, width):
    return [
        pltpu.VMEM((tok, width), jnp.float32),
        pltpu.VMEM((tok, 128), jnp.float32),
        pltpu.VMEM((tok, 128), jnp.float32),
    ]


def soft_cost(group, tok, width):
    return pl.CostEstimate(
        flops=2 * group * group * tok * tok * width,
        bytes_accessed=width * group * tok * 8,
        transcendentals=group * group * tok * tok // 2,
    )


def own_attention(info, queries, pairs, after=()):
    group = len(queries)
    _, tok, width = pairs[0].shape
    part = min(256, tok)
    return pl.pallas_call(
        functools.partial(own_kernel, group, tok, part),
        out_shape=soft_shapes(group, tok, width),
        in_specs=[SMEM] + [ANY] * (2 * group + len(after)),
        out_specs=[VMEM] * 2,
        scratch_shapes=soft_scratch(tok, width)
        + [
            pltpu.VMEM((group, tok, width), jnp.bfloat16),
            pltpu.VMEM((group, 2, tok, width), jnp.bfloat16),
            pltpu.SemaphoreType.DMA((2, group)),
        ],
        compiler_params=params(28),
        cost_estimate=soft_cost(group, tok, width),
        name="own_attention",
    )(info, *queries, *pairs, *after)


def pick_copy(flag, first, second, into, sem):
    if second is None:
        copy = pltpu.make_async_copy(first, into, sem)
        copy.start()
        return copy

    @pl.when(flag == 0)
    def _():
        pltpu.make_async_copy(first, into, sem).start()

    @pl.when(flag != 0)
    def _():
        pltpu.make_async_copy(second, into, sem).start()

    return pltpu.make_async_copy(first, into, sem)


def cross_kernel(group, tok, behind, part, lending, info_ref, *refs):
    pieces = behind * group
    q_any, refs = refs[:group], refs[group:]
    kv_any, refs = refs[:pieces], refs[pieces:]
    lent_q, lent_kv = [None] * group, [None] * pieces
    if lending:
        lent_q, lent_kv, refs = refs[:group], refs[group : 2 * group], refs[2 * group :]
    out_ref, level_ref, acc, top, norm, qbuf, kvbuf, sems, kv_sems = refs[-9:]
    plane, member, lends, planes = info_ref[0], info_ref[1], info_ref[3], info_ref[4]
    copies = [
        pick_copy(lends, kv_any[at], lent_kv[at], kvbuf.at[at], kv_sems.at[at])
        for at in range(pieces)
    ]
    for d in range(group):
        copies.append(pick_copy(lends, q_any[d], lent_q[d], qbuf.at[pl.ds(d, 1)], sems.at[d]))
    for copy in copies:
        copy.wait()
    scale = score_scale(qbuf.shape[-1])
    valid = jnp.maximum(behind - plane, 0) * group
    if lending:
        valid = jnp.where(lends == 0, valid, jnp.where(plane + 1 < planes, 0, pieces))

    def piece(d, carry):
        at = member ^ d

        @pl.when(at >= valid)
        def _():
            parts = []
            for r in range(0, tok, part):
                where, keys = pl.ds(r, part), pl.ds(r, tok - r)
                mask = triangle(part, tok - r, r, r, False)
                parts.append((where, qbuf[d, where], kvbuf[d, 0, keys], kvbuf[d, 1, keys], mask))
            soft_steps(parts, scale, True, acc, top, norm)

        @pl.when(at < valid)
        def _():
            acc[...] = jnp.zeros_like(acc)
            norm[...] = jnp.zeros_like(norm)
            top[...] = jnp.full_like(top, NEG)

        def later(other, carry):
            e = other // group * group + (member ^ (other % group))
            parts = []
            for r in range(0, tok, part):
                where = pl.ds(r, part)
                parts.append((where, qbuf[d, where], kvbuf[e, 0], kvbuf[e, 1], None))
            soft_steps(parts, scale, False, acc, top, norm)
            return carry

        lax.fori_loop(jnp.maximum(at + 1, valid), pieces, later, 0)
        soft_close(scale, acc, top, norm, out_ref.at[d], level_ref.at[d])
        return carry

    lax.fori_loop(0, group, piece, 0)


def cross_attention(info, queries, earlier, lent, after=()):
    group = len(queries)
    _, tok, width = queries[0].shape
    behind = len(earlier) // group
    part = min(256, tok)
    return pl.pallas_call(
        functools.partial(cross_kernel, group, tok, behind, part, len(lent)),
        out_shape=soft_shapes(group, tok, width),
        in_specs=[SMEM] + [ANY] * (group + len(earlier) + len(lent) + len(after)),
        out_specs=[VMEM] * 2,
        scratch_shapes=soft_scratch(tok, width)
        + [
            pltpu.VMEM((group, tok, width), jnp.bfloat16),
            pltpu.VMEM((len(earlier), 2, tok, width), jnp.bfloat16),
            pltpu.SemaphoreType.DMA((group,)),
            pltpu.SemaphoreType.DMA((len(earlier),)),
        ],
        compiler_params=params(28),
        cost_estimate=soft_cost(group, tok, width),
        name="cross_attention",
    )(info, *queries, *earlier, *lent, *after)


def finish_kernel(group, tok, count, hops, lending, info_ref, rate_ref, w_ref, place_ref, *refs):
    own_any, refs = refs[0], refs[1:]
    came, refs = refs[: 3 * hops], refs[3 * hops :]
    q_any, refs = refs[:group], refs[group:]
    own_rows, own_level, cross_any, cross_level = refs[:4]
    lent_any, lent_level = refs[4:6] if lending else (None, None)
    out_ref, new_w, sums, cbuf, qbuf, obuf, xbuf, lbuf, sems, q_sems = refs[-10:]
    plane, member, first_len, lends = info_ref[0], info_ref[1], info_ref[2], info_ref[3]
    own_copy = pltpu.make_async_copy(own_any, sums, sems.at[0])
    own_copy.start()

    def came_copy(hop, c):
        return pltpu.make_async_copy(came[3 * hop + c], cbuf.at[c], sems.at[1 + c])

    for hop in range(hops):

        @pl.when(plane == hop + 1)
        def _():
            for c in range(3):
                came_copy(hop, c).start()

    if hops:

        @pl.when((plane == 0) | (plane > hops))
        def _():
            cbuf[...] = jnp.zeros_like(cbuf)

    level_copies = [
        pltpu.make_async_copy(own_level, lbuf.at[0], sems.at[4]),
        pick_copy(lends, cross_level, lent_level, lbuf.at[1], sems.at[5]),
    ]
    level_copies[0].start()
    q_copies = [
        pltpu.make_async_copy(q_any[d], qbuf.at[pl.ds(d, 1)], q_sems.at[d]) for d in range(group)
    ]
    for copy in q_copies:
        copy.start()
    row_copies = [
        pltpu.make_async_copy(own_rows, obuf, sems.at[6]),
        pick_copy(lends, cross_any, lent_any, xbuf, sems.at[7]),
    ]
    row_copies[0].start()

    own_copy.wait()
    if hops:

        @pl.when((plane > 0) & (plane <= hops))
        def _():
            for c in range(3):
                came_copy(0, c).wait()

    step = rate_ref[0] / first_len.astype(jnp.float32)

    @pl.when((plane + 1) * group * tok > first_len)
    def _():
        for c in range(3):
            previous = w_ref[c].astype(jnp.float32)
            summed = sums[c]
            if hops:
                summed = summed + cbuf[c].astype(jnp.float32)
            updated = previous + step * summed
            old_norm = jnp.sqrt(jnp.sum(previous * previous, axis=1, keepdims=True) + eps)
            new_norm = jnp.sqrt(jnp.sum(updated * updated, axis=1, keepdims=True) + eps)
            new_w[c] = (updated * (old_norm / new_norm)).astype(new_w.dtype)

    for copy in q_copies + level_copies + row_copies:
        copy.wait()

    def apply(rows, weights):
        gate = dot(rows, weights[0], NT)
        up = dot(rows, weights[1], NT)
        act = (gate * jax.nn.sigmoid(gate) * up).astype(jnp.bfloat16)
        return dot(act, weights[2], NN)

    seg = tok // count

    def piece(d, carry):
        at = member ^ d
        first_tok = (plane * group + at) * tok
        own_log, cross_log = as_column(lbuf[0, d]), as_column(lbuf[1, d])
        cross_log = jnp.where(plane > 0, cross_log, NEG)
        own_part = 1.0 / (1.0 + jnp.exp2(cross_log - own_log))
        cross_part = 1.0 / (1.0 + jnp.exp2(own_log - cross_log))
        mixed = obuf[d].astype(jnp.float32) * own_part + xbuf[d].astype(jnp.float32) * cross_part
        mixed = mixed.astype(jnp.bfloat16).astype(jnp.float32)

        def leave(fast):
            rows = (mixed + fast).astype(jnp.bfloat16)
            pick = as_column(place_ref[at]).astype(jnp.int32)
            pick = pick == lax.broadcasted_iota(jnp.int32, (tok, tok), 1)
            sorted_rows = dot(pick.astype(jnp.bfloat16), rows, NN)
            out_ref[:, at] = sorted_rows.reshape(count, seg, rows.shape[-1]).astype(out_ref.dtype)

        @pl.when(first_tok + tok <= first_len)
        def _():
            leave(apply(qbuf[d], w_ref))

        @pl.when(first_tok >= first_len)
        def _():
            leave(apply(qbuf[d], new_w))

        @pl.when((first_tok < first_len) & (first_tok + tok > first_len))
        def _():
            token = first_tok + lax.broadcasted_iota(jnp.int32, (tok, 1), 0)
            leave(jnp.where(token < first_len, apply(qbuf[d], w_ref), apply(qbuf[d], new_w)))

        return carry

    lax.fori_loop(0, group, piece, 0)


def finish_rows(info, rate, weights, places, own, came, queries, own_part, cross_part, lent, count):
    group = len(queries)
    _, tok, width = queries[0].shape
    hidden = weights.shape[1]
    hops = len(came) // 3
    return pl.pallas_call(
        functools.partial(finish_kernel, group, tok, count, hops, len(lent)),
        out_shape=jax.ShapeDtypeStruct((count, group, tok // count, width), jnp.bfloat16),
        in_specs=[SMEM] * 2 + [VMEM] * 2 + [ANY] * (1 + 3 * hops + group + 4 + len(lent)),
        out_specs=VMEM,
        scratch_shapes=[
            pltpu.VMEM(weights.shape, jnp.bfloat16),
            pltpu.VMEM(weights.shape, jnp.float32),
            pltpu.VMEM(weights.shape, jnp.bfloat16),
            pltpu.VMEM((group, tok, width), jnp.bfloat16),
            pltpu.VMEM((group, tok, width), jnp.bfloat16),
            pltpu.VMEM((group, tok, width), jnp.bfloat16),
            pltpu.VMEM((2, group, 8, tok), jnp.float32),
            pltpu.SemaphoreType.DMA((8,)),
            pltpu.SemaphoreType.DMA((group,)),
        ],
        compiler_params=params(36),
        cost_estimate=pl.CostEstimate(
            flops=2 * group * tok * width * (3 * hidden + tok),
            bytes_accessed=2 * (4 * group * tok * width + 6 * hidden * width),
            transcendentals=group * tok * hidden,
        ),
        name="finish_rows",
    )(info, rate, weights, places, own, *came, *queries, *own_part, *cross_part, *lent)


def norm_kernel(came_ref, scale_ref, gain_ref, out_ref):
    scaled = came_ref[0].astype(jnp.float32) * scale_ref[...] * gain_ref[...]
    out_ref[...] = jnp.swapaxes(scaled.astype(out_ref.dtype), 0, 1)


def norm_rows(came, scale, gain):
    planes, group, rows, width = came.shape
    return pl.pallas_call(
        norm_kernel,
        grid=(planes,),
        out_shape=jax.ShapeDtypeStruct((planes * rows, group, width), jnp.bfloat16),
        in_specs=[
            pl.BlockSpec((1, group, rows, width), lambda z: (z, 0, 0, 0)),
            pl.BlockSpec((1, rows, 1), lambda z: (z, 0, 0)),
            pl.BlockSpec((group, 1, width), lambda z: (0, 0, 0)),
        ],
        out_specs=pl.BlockSpec((rows, group, width), lambda z: (z, 0, 0)),
        compiler_params=params(20),
        name="norm_rows",
    )(came, scale, gain)


def forward_sums(own, sent, group, count):
    planes = count // group
    if planes > 8:
        groups = [[plane * group + m for plane in range(planes)] for m in range(group)]
        whole = lax.psum(own.astype(jnp.bfloat16), "seq", axis_index_groups=groups)
        return whole.astype(jnp.float32), []
    came = []
    for hop in range(1, planes):
        pairs = [((hop - 1) * group + m, hop * group + m) for m in range(group)]
        if hop > 1:
            sent = [
                (own[c] + came[-3 + c].astype(jnp.float32)).astype(jnp.bfloat16) for c in range(3)
            ]
        came.extend([lax.ppermute(sent[c], "seq", pairs) for c in range(3)])
    return own, came


def as_places(asked, group, tok):
    places = jnp.transpose(asked, (1, 0, 2)).reshape(group, 1, tok).astype(jnp.float32)
    return jnp.broadcast_to(places, (group, 8, tok))


def asked_places(slot_order, plane, member, group, count):
    tok = slot_order.shape[0]
    seg, planes = tok // count, count // group
    wanted = slot_order.reshape(planes, group, seg) % tok
    if planes > 8:
        asked = lax.all_gather(wanted.reshape(tok), "seq").reshape(count, count, seg)
        asked = lax.dynamic_slice_in_dim(asked, plane * group, group, 1)
        return as_places(asked, group, tok)
    column = jnp.zeros_like(wanted)
    for step in range(planes):
        target = (plane + step) % planes
        part = lax.dynamic_index_in_dim(wanted, target, 0, keepdims=True)
        if step:
            pairs = [(index, (index + step * group) % count) for index in range(count)]
            part = lax.ppermute(part, "seq", pairs)
        source = (plane - step) % planes
        column = lax.dynamic_update_slice_in_dim(column, part, source, 0)
    whole = jnp.zeros((planes, group, group, seg), jnp.int32)
    for d in range(group):
        part = lax.ppermute(column, "seq", swap_pairs(count, d)) if d else column
        whole = lax.dynamic_update_slice_in_dim(whole, part[:, None], member ^ d, 1)
    return as_places(whole.reshape(count, group, seg), group, tok)


def per_device(
    queries, token_keys, token_values, fast_weights, learn_rate, out_gain, group_lengths, slot_order
):
    tok, group, width = queries.shape
    count = lax.axis_size("seq")
    seg = tok // count
    planes = count // group
    behind = WINDOW // (group * tok)
    sides = lax.axis_size("head")
    lending = behind == 1 and sides % 2 == 0
    position = lax.axis_index("seq")
    plane, member = position // group, position % group
    lends = lax.axis_index("head") % 2 if lending else jnp.int32(0)
    info = jnp.stack([plane, member, group_lengths[0], lends, jnp.int32(planes)])
    info = info.astype(jnp.int32)

    def across(value, steps, odd):
        pairs = plane_pairs(count, steps)
        if not lending:
            return lax.ppermute(value, "seq", pairs)
        both = [(a * sides + h, b * sides + h) for a, b in pairs for h in range(odd, sides, 2)]
        return lax.ppermute(value, ("seq", "head"), both)

    def back_across(value, odd):
        pairs = [(b, a) for a, b in plane_pairs(count, group)]
        both = [(a * sides + h, b * sides + h) for a, b in pairs for h in range(odd, sides, 2)]
        return lax.ppermute(value, ("seq", "head"), both)

    mine = split_heads(info, [token_keys, token_values])
    pairs = trade(mine, count)
    earlier = []
    for back in range(behind, 0, -1):
        earlier.extend([across(pair, back * group, 0) for pair in pairs])
    asked = trade(split_heads(info, [queries], pairs[1:2]), count)
    lent = [back_across(piece, 1) for piece in asked] + pairs if lending else []

    weights = lax.dynamic_index_in_dim(fast_weights, member, 1, keepdims=False)
    weights = jnp.transpose(weights, (1, 0, 2))
    rate = lax.dynamic_slice_in_dim(learn_rate, member, 1)
    half = group // 2
    carried = weight_sums(info, weights, pairs, 0, half) if half else []
    own, *sent = weight_sums(info, weights, pairs, half, group, carried, earlier[:half])
    own, came = forward_sums(own, sent, group, count)
    own_part = own_attention(info, asked, pairs, earlier[half:])
    cross_part = cross_attention(info, asked, earlier, lent, came[:3])
    lent_part = [across(value, group, 1) for value in cross_part] if lending else []
    places = asked_places(slot_order, plane, member, group, count)
    leaving = finish_rows(
        info, rate, weights, places, own, came, asked, own_part, cross_part, lent_part, count
    )

    came = lax.all_to_all(leaving, "seq", split_axis=0, concat_axis=0, tiled=True)
    came = came.reshape(planes, group, group * seg, width)
    wide = came.astype(jnp.float32)
    power = lax.psum(jnp.sum(wide * wide, axis=(1, 3)), "head")
    scale = lax.rsqrt(power / (group * lax.axis_size("head") * width) + eps)
    return norm_rows(came, scale[:, :, None], out_gain[:, None, :])


def solution(mesh):
    return jax.shard_map(
        per_device,
        mesh=mesh,
        in_specs=(
            P("seq", "head", None),
            P("seq", "head", None),
            P("seq", "head", None),
            P(None, "head", None, None),
            P("head"),
            P("head", None),
            P(),
            P("seq"),
        ),
        out_specs=P("seq", "head", None),
        check_vma=False,
    )
```

```python
import functools
import math

import jax
import jax.numpy as jnp
from jax import lax
from jax.experimental import pallas as pl
from jax.experimental.pallas import tpu as pltpu
from jax.sharding import PartitionSpec as P

WINDOW = 2048
NEG = -1e30
MIB = 1024 * 1024

eps = 1e-06

NT = (((1,), (1,)), ((), ()))
TN = (((0,), (0,)), ((), ()))
NN = (((1,), (0,)), ((), ()))

ANY = pl.BlockSpec(memory_space=pl.ANY)
SMEM = pl.BlockSpec(memory_space=pltpu.SMEM)
VMEM = pl.BlockSpec(memory_space=pltpu.VMEM)


def dot(left, right, dims):
    return lax.dot_general(left, right, dims, preferred_element_type=jnp.float32)


def params(mib):
    return pltpu.CompilerParams(vmem_limit_bytes=mib * MIB)


def swap_pairs(count, distance):
    return [(index, index ^ distance) for index in range(count)]


def plane_pairs(count, steps):
    return [(index, index + steps) for index in range(count - steps)]


def split_kernel(total, group, info_ref, *refs):
    x_refs = refs[:total]
    outs = refs[len(refs) - group - 2 : len(refs) - 2]
    buf, sems = refs[-2:]
    member = info_ref[1]
    for t, x_ref in enumerate(x_refs):
        buf[:, t] = jnp.swapaxes(x_ref[...], 0, 1)
    copies = [
        pltpu.make_async_copy(buf.at[member ^ d], outs[d], sems.at[d]) for d in range(group)
    ]
    for copy in copies:
        copy.start()
    for copy in copies:
        copy.wait()


def split_heads(info, arrays, after=()):
    tok, group, width = arrays[0].shape
    total = len(arrays)
    return pl.pallas_call(
        functools.partial(split_kernel, total, group),
        out_shape=[jax.ShapeDtypeStruct((total, tok, width), jnp.bfloat16)] * group,
        in_specs=[SMEM] + [VMEM] * total + [ANY] * len(after),
        out_specs=[ANY] * group,
        scratch_shapes=[
            pltpu.VMEM((group, total, tok, width), jnp.bfloat16),
            pltpu.SemaphoreType.DMA((group,)),
        ],
        compiler_params=params(20),
        cost_estimate=pl.CostEstimate(
            flops=0, bytes_accessed=4 * total * group * tok * width, transcendentals=0
        ),
        name="split_heads",
    )(info, *arrays, *after)


def trade(pieces, count):
    return [
        lax.ppermute(piece, "seq", swap_pairs(count, d)) if d else piece
        for d, piece in enumerate(pieces)
    ]


def grad_kernel(group, tok, first, last, carried, info_ref, w_ref, *refs):
    pieces = last - first
    kv_any, refs = refs[:pieces], refs[pieces:]
    kvbuf, acc, sems, acc_sem = refs[-4:]
    plane, member, first_len = info_ref[0], info_ref[1], info_ref[2]
    copies = [pltpu.make_async_copy(kv_any[n], kvbuf.at[n], sems.at[n]) for n in range(pieces)]
    for copy in copies:
        copy.start()
    if carried:
        load = pltpu.make_async_copy(refs[0], acc, acc_sem.at[0])
        load.start()
        load.wait()
    else:
        acc[...] = jnp.zeros_like(acc)
    hidden = w_ref.shape[1]
    part = min(256, hidden)
    for copy in copies:
        copy.wait()

    def piece(n, carry):
        first_tok = (plane * group + (member ^ (first + n))) * tok

        @pl.when(first_tok < first_len)
        def _():
            keys = kvbuf[n, 0]
            token = first_tok + lax.broadcasted_iota(jnp.int32, (tok, 1), 0)
            values = jnp.where(token < first_len, kvbuf[n, 1].astype(jnp.float32), 0.0)
            values = values.astype(jnp.bfloat16)
            for f in range(0, hidden, part):
                rows = pl.ds(f, part)
                gate = dot(keys, w_ref[0, rows, :], NT)
                up = dot(keys, w_ref[1, rows, :], NT)
                back = dot(values, w_ref[2, rows, :], NT)
                sig = jax.nn.sigmoid(gate)
                silu = gate * sig
                act = (silu * up).astype(jnp.bfloat16)
                grad_up = (back * silu).astype(jnp.bfloat16)
                grad_gate = (back * up * sig * (1.0 + gate * (1.0 - sig))).astype(jnp.bfloat16)
                acc[0, rows, :] += dot(grad_gate, keys, TN)
                acc[1, rows, :] += dot(grad_up, keys, TN)
                acc[2, rows, :] += dot(act, values, TN)

        return carry

    lax.fori_loop(0, pieces, piece, 0)
    whole = last == group
    outs = refs[len(refs) - 4 - (5 if whole else 1) : len(refs) - 4]
    keep = pltpu.make_async_copy(acc, outs[0], acc_sem.at[1])
    keep.start()
    if whole:
        onward = pltpu.make_async_copy(kvbuf, outs[1], acc_sem.at[0])
        onward.start()
    for c, sent in enumerate(outs[2:]):
        sent[...] = acc[c].astype(sent.dtype)
    keep.wait()
    if whole:
        onward.wait()


def weight_sums(info, weights, pairs, first, last, carried=(), after=()):
    group = len(pairs)
    _, tok, width = pairs[0].shape
    rows, hidden, _ = weights.shape
    pieces = last - first
    whole = last == group
    stacked = (pieces, 2, tok, width)
    return pl.pallas_call(
        functools.partial(grad_kernel, group, tok, first, last, len(carried)),
        out_shape=[jax.ShapeDtypeStruct(weights.shape, jnp.float32)]
        + [jax.ShapeDtypeStruct(stacked, jnp.bfloat16)] * whole
        + [jax.ShapeDtypeStruct((hidden, width), jnp.bfloat16)] * (rows * whole),
        in_specs=[SMEM, VMEM] + [ANY] * (pieces + len(carried) + len(after)),
        out_specs=[ANY] + [ANY] * whole + [VMEM] * (rows * whole),
        scratch_shapes=[
            pltpu.VMEM((pieces, 2, tok, width), jnp.bfloat16),
            pltpu.VMEM(weights.shape, jnp.float32),
            pltpu.SemaphoreType.DMA((pieces,)),
            pltpu.SemaphoreType.DMA((2,)),
        ],
        compiler_params=params(28),
        cost_estimate=pl.CostEstimate(
            flops=2 * 6 * pieces * tok * hidden * width,
            bytes_accessed=2 * (2 * pieces * tok * width + 2 * rows * hidden * width),
            transcendentals=pieces * tok * hidden,
        ),
        name="weight_sums",
    )(info, weights, *pairs[first:last], *carried, *after)


def lanes_sum(expo):
    total = expo[:, :128]
    for lane in range(128, expo.shape[1], 128):
        total = total + expo[:, lane : lane + 128]
    return total


def soft_steps(parts, scale, fresh, acc, top, norm):
    scores = [
        dot(rows, keys, NT) if mask is None else jnp.where(mask, dot(rows, keys, NT), NEG)
        for _, rows, keys, _, mask in parts
    ]
    done = []
    for (where, _, _, _, _), score in zip(parts, scores):
        peak = jnp.max(score, axis=1, keepdims=True)
        if fresh:
            decay = None
        else:
            before = top[where, :1]
            peak = jnp.maximum(peak, before)
            decay = jnp.exp2((before - peak) * scale)
        expo = jnp.exp2((score - peak) * scale)
        done.append((peak, decay, lanes_sum(expo), expo.astype(jnp.bfloat16)))
    for (where, _, _, values, _), (peak, decay, total, expo) in zip(parts, done):
        mixed = dot(expo, values, NN)
        wide = (peak.shape[0], 128)
        top[where, :] = jnp.broadcast_to(peak, wide)
        if fresh:
            norm[where, :] = total
            acc[where, :] = mixed
        else:
            norm[where, :] = norm[where, :] * decay + total
            acc[where, :] = acc[where, :] * decay + mixed


def soft_close(scale, acc, top, norm, out_ref, level_ref):
    total = jnp.sum(norm[...], axis=1, keepdims=True)
    out_ref[...] = (acc[...] / jnp.maximum(total, 1e-30)).astype(out_ref.dtype)
    level = top[...] * scale + jnp.log2(jnp.maximum(total, 1e-30))
    level_ref[...] = jnp.transpose(level)[:8]


def as_column(rows):
    return jnp.transpose(jnp.concatenate([rows] * 16, axis=0))[:, :1]


def score_scale(width):
    return math.log2(math.e) / math.sqrt(width)


def triangle(rows, cols, first_row, first_col, lower):
    row = first_row + lax.broadcasted_iota(jnp.int32, (rows, cols), 0)
    col = first_col + lax.broadcasted_iota(jnp.int32, (rows, cols), 1)
    return col <= row if lower else col > row


def own_kernel(group, tok, part, info_ref, *refs):
    q_any, kv_any = refs[:group], refs[group : 2 * group]
    out_ref, level_ref, acc, top, norm, qbuf, kvbuf, sems = refs[-8:]
    member = info_ref[1]
    copies = []
    for d in range(group):
        copies.append(pltpu.make_async_copy(q_any[d], qbuf.at[pl.ds(d, 1)], sems.at[0, d]))
        copies.append(pltpu.make_async_copy(kv_any[d], kvbuf.at[d], sems.at[1, d]))
    for copy in copies:
        copy.start()
    for copy in copies:
        copy.wait()
    scale = score_scale(qbuf.shape[-1])

    def piece(d, carry):
        parts = []
        for r in range(0, tok, part):
            where, keys = pl.ds(r, part), pl.ds(0, r + part)
            mask = triangle(part, r + part, r, 0, True)
            parts.append((where, qbuf[d, where], kvbuf[d, 0, keys], kvbuf[d, 1, keys], mask))
        soft_steps(parts, scale, True, acc, top, norm)

        def earlier(other, carry):
            e = member ^ other
            parts = []
            for r in range(0, tok, part):
                where = pl.ds(r, part)
                parts.append((where, qbuf[d, where], kvbuf[e, 0], kvbuf[e, 1], None))
            soft_steps(parts, scale, False, acc, top, norm)
            return carry

        lax.fori_loop(0, member ^ d, earlier, 0)
        soft_close(scale, acc, top, norm, out_ref.at[d], level_ref.at[d])
        return carry

    lax.fori_loop(0, group, piece, 0)


def soft_shapes(group, tok, width):
    return [
        jax.ShapeDtypeStruct((group, tok, width), jnp.bfloat16),
        jax.ShapeDtypeStruct((group, 8, tok), jnp.float32),
    ]


def soft_scratch(tok, width):
    return [
        pltpu.VMEM((tok, width), jnp.float32),
        pltpu.VMEM((tok, 128), jnp.float32),
        pltpu.VMEM((tok, 128), jnp.float32),
    ]


def soft_cost(group, tok, width):
    return pl.CostEstimate(
        flops=2 * group * group * tok * tok * width,
        bytes_accessed=width * group * tok * 8,
        transcendentals=group * group * tok * tok // 2,
    )


def own_attention(info, queries, pairs, after=()):
    group = len(queries)
    _, tok, width = pairs[0].shape
    part = min(256, tok)
    return pl.pallas_call(
        functools.partial(own_kernel, group, tok, part),
        out_shape=soft_shapes(group, tok, width),
        in_specs=[SMEM] + [ANY] * (2 * group + len(after)),
        out_specs=[VMEM] * 2,
        scratch_shapes=soft_scratch(tok, width)
        + [
            pltpu.VMEM((group, tok, width), jnp.bfloat16),
            pltpu.VMEM((group, 2, tok, width), jnp.bfloat16),
            pltpu.SemaphoreType.DMA((2, group)),
        ],
        compiler_params=params(28),
        cost_estimate=soft_cost(group, tok, width),
        name="own_attention",
    )(info, *queries, *pairs, *after)


def pick_copy(flag, first, second, into, sem):
    if second is None:
        copy = pltpu.make_async_copy(first, into, sem)
        copy.start()
        return copy

    @pl.when(flag == 0)
    def _():
        pltpu.make_async_copy(first, into, sem).start()

    @pl.when(flag != 0)
    def _():
        pltpu.make_async_copy(second, into, sem).start()

    return pltpu.make_async_copy(first, into, sem)


def cross_kernel(group, tok, behind, part, lending, whole, info_ref, *refs):
    pieces = behind * group
    q_any, refs = refs[:group], refs[group:]
    kv_any = []
    for size in whole:
        kv_any.extend(refs[0].at[n] if size > 1 else refs[0] for n in range(size))
        refs = refs[1:]
    lent_q, lent_kv = [None] * group, [None] * pieces
    if lending:
        lent_q, lent_kv, refs = refs[:group], refs[group : 2 * group], refs[2 * group :]
    out_ref, level_ref, acc, top, norm, qbuf, kvbuf, sems, kv_sems = refs[-9:]
    plane, member, lends, planes = info_ref[0], info_ref[1], info_ref[3], info_ref[4]
    copies = [
        pick_copy(lends, kv_any[at], lent_kv[at], kvbuf.at[at], kv_sems.at[at])
        for at in range(pieces)
    ]
    for d in range(group):
        copies.append(pick_copy(lends, q_any[d], lent_q[d], qbuf.at[pl.ds(d, 1)], sems.at[d]))
    for copy in copies:
        copy.wait()
    scale = score_scale(qbuf.shape[-1])
    valid = jnp.maximum(behind - plane, 0) * group
    if lending:
        valid = jnp.where(lends == 0, valid, jnp.where(plane + 1 < planes, 0, pieces))

    def piece(d, carry):
        at = member ^ d

        @pl.when(at >= valid)
        def _():
            parts = []
            for r in range(0, tok, part):
                where, keys = pl.ds(r, part), pl.ds(r, tok - r)
                mask = triangle(part, tok - r, r, r, False)
                parts.append((where, qbuf[d, where], kvbuf[d, 0, keys], kvbuf[d, 1, keys], mask))
            soft_steps(parts, scale, True, acc, top, norm)

        @pl.when(at < valid)
        def _():
            acc[...] = jnp.zeros_like(acc)
            norm[...] = jnp.zeros_like(norm)
            top[...] = jnp.full_like(top, NEG)

        def later(other, carry):
            e = other // group * group + (member ^ (other % group))
            parts = []
            for r in range(0, tok, part):
                where = pl.ds(r, part)
                parts.append((where, qbuf[d, where], kvbuf[e, 0], kvbuf[e, 1], None))
            soft_steps(parts, scale, False, acc, top, norm)
            return carry

        lax.fori_loop(jnp.maximum(at + 1, valid), pieces, later, 0)
        soft_close(scale, acc, top, norm, out_ref.at[d], level_ref.at[d])
        return carry

    lax.fori_loop(0, group, piece, 0)


def cross_attention(info, queries, earlier, lent, after=()):
    group = len(queries)
    _, tok, width = queries[0].shape
    whole = [array.shape[0] if array.ndim == 4 else 1 for array in earlier]
    behind = sum(whole) // group
    part = min(256, tok)
    return pl.pallas_call(
        functools.partial(cross_kernel, group, tok, behind, part, len(lent), whole),
        out_shape=soft_shapes(group, tok, width),
        in_specs=[SMEM] + [ANY] * (group + len(earlier) + len(lent) + len(after)),
        out_specs=[VMEM] * 2,
        scratch_shapes=soft_scratch(tok, width)
        + [
            pltpu.VMEM((group, tok, width), jnp.bfloat16),
            pltpu.VMEM((behind * group, 2, tok, width), jnp.bfloat16),
            pltpu.SemaphoreType.DMA((group,)),
            pltpu.SemaphoreType.DMA((behind * group,)),
        ],
        compiler_params=params(28),
        cost_estimate=soft_cost(group, tok, width),
        name="cross_attention",
    )(info, *queries, *earlier, *lent, *after)


def finish_kernel(group, tok, count, hops, lending, info_ref, rate_ref, w_ref, place_ref, *refs):
    own_any, refs = refs[0], refs[1:]
    came, refs = refs[: 3 * hops], refs[3 * hops :]
    q_any, refs = refs[:group], refs[group:]
    own_rows, own_level, cross_any, cross_level = refs[:4]
    lent_any, lent_level = refs[4:6] if lending else (None, None)
    out_ref, new_w, sums, cbuf, qbuf, obuf, xbuf, lbuf, sems, q_sems = refs[-10:]
    plane, member, first_len, lends = info_ref[0], info_ref[1], info_ref[2], info_ref[3]
    own_copy = pltpu.make_async_copy(own_any, sums, sems.at[0])
    own_copy.start()

    def came_copy(hop, c):
        return pltpu.make_async_copy(came[3 * hop + c], cbuf.at[c], sems.at[1 + c])

    for hop in range(hops):

        @pl.when(plane == hop + 1)
        def _():
            for c in range(3):
                came_copy(hop, c).start()

    if hops:

        @pl.when((plane == 0) | (plane > hops))
        def _():
            cbuf[...] = jnp.zeros_like(cbuf)

    level_copies = [
        pltpu.make_async_copy(own_level, lbuf.at[0], sems.at[4]),
        pick_copy(lends, cross_level, lent_level, lbuf.at[1], sems.at[5]),
    ]
    level_copies[0].start()
    q_copies = [
        pltpu.make_async_copy(q_any[d], qbuf.at[pl.ds(d, 1)], q_sems.at[d]) for d in range(group)
    ]
    for copy in q_copies:
        copy.start()
    row_copies = [
        pltpu.make_async_copy(own_rows, obuf, sems.at[6]),
        pick_copy(lends, cross_any, lent_any, xbuf, sems.at[7]),
    ]
    row_copies[0].start()

    own_copy.wait()
    if hops:

        @pl.when((plane > 0) & (plane <= hops))
        def _():
            for c in range(3):
                came_copy(0, c).wait()

    step = rate_ref[0] / first_len.astype(jnp.float32)

    @pl.when((plane + 1) * group * tok > first_len)
    def _():
        for c in range(3):
            previous = w_ref[c].astype(jnp.float32)
            summed = sums[c]
            if hops:
                summed = summed + cbuf[c].astype(jnp.float32)
            updated = previous + step * summed
            old_norm = jnp.sqrt(jnp.sum(previous * previous, axis=1, keepdims=True) + eps)
            new_norm = jnp.sqrt(jnp.sum(updated * updated, axis=1, keepdims=True) + eps)
            new_w[c] = (updated * (old_norm / new_norm)).astype(new_w.dtype)

    for copy in q_copies + level_copies + row_copies:
        copy.wait()

    def apply(rows, weights):
        gate = dot(rows, weights[0], NT)
        up = dot(rows, weights[1], NT)
        act = (gate * jax.nn.sigmoid(gate) * up).astype(jnp.bfloat16)
        return dot(act, weights[2], NN)

    seg = tok // count

    def piece(d, carry):
        at = member ^ d
        first_tok = (plane * group + at) * tok
        own_log, cross_log = as_column(lbuf[0, d]), as_column(lbuf[1, d])
        cross_log = jnp.where(plane > 0, cross_log, NEG)
        own_part = 1.0 / (1.0 + jnp.exp2(cross_log - own_log))
        cross_part = 1.0 / (1.0 + jnp.exp2(own_log - cross_log))
        mixed = obuf[d].astype(jnp.float32) * own_part + xbuf[d].astype(jnp.float32) * cross_part
        mixed = mixed.astype(jnp.bfloat16).astype(jnp.float32)

        def leave(fast):
            rows = (mixed + fast).astype(jnp.bfloat16)
            pick = as_column(place_ref[at]).astype(jnp.int32)
            pick = pick == lax.broadcasted_iota(jnp.int32, (tok, tok), 1)
            sorted_rows = dot(pick.astype(jnp.bfloat16), rows, NN)
            out_ref[:, at] = sorted_rows.reshape(count, seg, rows.shape[-1]).astype(out_ref.dtype)

        @pl.when(first_tok + tok <= first_len)
        def _():
            leave(apply(qbuf[d], w_ref))

        @pl.when(first_tok >= first_len)
        def _():
            leave(apply(qbuf[d], new_w))

        @pl.when((first_tok < first_len) & (first_tok + tok > first_len))
        def _():
            token = first_tok + lax.broadcasted_iota(jnp.int32, (tok, 1), 0)
            leave(jnp.where(token < first_len, apply(qbuf[d], w_ref), apply(qbuf[d], new_w)))

        return carry

    lax.fori_loop(0, group, piece, 0)


def finish_rows(info, rate, weights, places, own, came, queries, own_part, cross_part, lent, count):
    group = len(queries)
    _, tok, width = queries[0].shape
    hidden = weights.shape[1]
    hops = len(came) // 3
    return pl.pallas_call(
        functools.partial(finish_kernel, group, tok, count, hops, len(lent)),
        out_shape=jax.ShapeDtypeStruct((count, group, tok // count, width), jnp.bfloat16),
        in_specs=[SMEM] * 2 + [VMEM] * 2 + [ANY] * (1 + 3 * hops + group + 4 + len(lent)),
        out_specs=VMEM,
        scratch_shapes=[
            pltpu.VMEM(weights.shape, jnp.bfloat16),
            pltpu.VMEM(weights.shape, jnp.float32),
            pltpu.VMEM(weights.shape, jnp.bfloat16),
            pltpu.VMEM((group, tok, width), jnp.bfloat16),
            pltpu.VMEM((group, tok, width), jnp.bfloat16),
            pltpu.VMEM((group, tok, width), jnp.bfloat16),
            pltpu.VMEM((2, group, 8, tok), jnp.float32),
            pltpu.SemaphoreType.DMA((8,)),
            pltpu.SemaphoreType.DMA((group,)),
        ],
        compiler_params=params(36),
        cost_estimate=pl.CostEstimate(
            flops=2 * group * tok * width * (3 * hidden + tok),
            bytes_accessed=2 * (4 * group * tok * width + 6 * hidden * width),
            transcendentals=group * tok * hidden,
        ),
        name="finish_rows",
    )(info, rate, weights, places, own, *came, *queries, *own_part, *cross_part, *lent)


def norm_kernel(came_ref, scale_ref, gain_ref, out_ref):
    scaled = came_ref[0].astype(jnp.float32) * scale_ref[...] * gain_ref[...]
    out_ref[...] = jnp.swapaxes(scaled.astype(out_ref.dtype), 0, 1)


def norm_rows(came, scale, gain):
    planes, group, rows, width = came.shape
    return pl.pallas_call(
        norm_kernel,
        grid=(planes,),
        out_shape=jax.ShapeDtypeStruct((planes * rows, group, width), jnp.bfloat16),
        in_specs=[
            pl.BlockSpec((1, group, rows, width), lambda z: (z, 0, 0, 0)),
            pl.BlockSpec((1, rows, 1), lambda z: (z, 0, 0)),
            pl.BlockSpec((group, 1, width), lambda z: (0, 0, 0)),
        ],
        out_specs=pl.BlockSpec((rows, group, width), lambda z: (z, 0, 0)),
        compiler_params=params(20),
        name="norm_rows",
    )(came, scale, gain)


def add_kernel(c, own_any, came_ref, out_ref, buf, sem):
    copy = pltpu.make_async_copy(own_any.at[c], buf, sem.at[0])
    copy.start()
    copy.wait()
    out_ref[...] = (buf[...] + came_ref[...].astype(jnp.float32)).astype(out_ref.dtype)


def hop_add(own, came, c):
    return pl.pallas_call(
        functools.partial(add_kernel, c),
        out_shape=jax.ShapeDtypeStruct(came.shape, came.dtype),
        in_specs=[ANY, VMEM],
        out_specs=VMEM,
        scratch_shapes=[pltpu.VMEM(came.shape, jnp.float32), pltpu.SemaphoreType.DMA((1,))],
        compiler_params=params(8),
        cost_estimate=pl.CostEstimate(
            flops=came.size, bytes_accessed=8 * came.size, transcendentals=0
        ),
        name="hop_add",
    )(own, came)


def forward_sums(own, sent, group, count):
    planes = count // group
    if planes > 8:
        groups = [[plane * group + m for plane in range(planes)] for m in range(group)]
        whole = lax.psum(own.astype(jnp.bfloat16), "seq", axis_index_groups=groups)
        return whole.astype(jnp.float32), [], []
    came, added = [], []
    for hop in range(1, planes):
        pairs = [((hop - 1) * group + m, hop * group + m) for m in range(group)]
        if hop > 1:
            sent = [hop_add(own, came[-3 + c], c) for c in range(3)]
            added.extend(sent)
        came.extend([lax.ppermute(sent[c], "seq", pairs) for c in range(3)])
    return own, came, added


def as_places(asked, group, tok):
    places = jnp.transpose(asked, (1, 0, 2)).reshape(group, 1, tok).astype(jnp.float32)
    return jnp.broadcast_to(places, (group, 8, tok))


def asked_places(slot_order, plane, member, group, count):
    tok = slot_order.shape[0]
    seg, planes = tok // count, count // group
    wanted = slot_order.reshape(planes, group, seg) % tok
    if planes > 8:
        asked = lax.all_gather(wanted.reshape(tok), "seq").reshape(count, count, seg)
        asked = lax.dynamic_slice_in_dim(asked, plane * group, group, 1)
        return as_places(asked, group, tok)
    column = jnp.zeros_like(wanted)
    for step in range(planes):
        target = (plane + step) % planes
        part = lax.dynamic_index_in_dim(wanted, target, 0, keepdims=True)
        if step:
            pairs = [(index, (index + step * group) % count) for index in range(count)]
            part = lax.ppermute(part, "seq", pairs)
        source = (plane - step) % planes
        column = lax.dynamic_update_slice_in_dim(column, part, source, 0)
    whole = jnp.zeros((planes, group, group, seg), jnp.int32)
    for d in range(group):
        part = lax.ppermute(column, "seq", swap_pairs(count, d)) if d else column
        whole = lax.dynamic_update_slice_in_dim(whole, part[:, None], member ^ d, 1)
    return as_places(whole.reshape(count, group, seg), group, tok)


def per_device(
    queries, token_keys, token_values, fast_weights, learn_rate, out_gain, group_lengths, slot_order
):
    tok, group, width = queries.shape
    count = lax.axis_size("seq")
    seg = tok // count
    planes = count // group
    behind = WINDOW // (group * tok)
    sides = lax.axis_size("head")
    lending = behind == 1 and sides % 2 == 0
    position = lax.axis_index("seq")
    plane, member = position // group, position % group
    lends = lax.axis_index("head") % 2 if lending else jnp.int32(0)
    info = jnp.stack([plane, member, group_lengths[0], lends, jnp.int32(planes)])
    info = info.astype(jnp.int32)

    def across(value, steps, odd):
        pairs = plane_pairs(count, steps)
        if not lending:
            return lax.ppermute(value, "seq", pairs)
        both = [(a * sides + h, b * sides + h) for a, b in pairs for h in range(odd, sides, 2)]
        return lax.ppermute(value, ("seq", "head"), both)

    def back_across(value, odd):
        pairs = [(b, a) for a, b in plane_pairs(count, group)]
        both = [(a * sides + h, b * sides + h) for a, b in pairs for h in range(odd, sides, 2)]
        return lax.ppermute(value, ("seq", "head"), both)

    mine = split_heads(info, [token_keys, token_values])
    pairs = trade(mine, count)
    weights = lax.dynamic_index_in_dim(fast_weights, member, 1, keepdims=False)
    weights = jnp.transpose(weights, (1, 0, 2))
    rate = lax.dynamic_slice_in_dim(learn_rate, member, 1)
    places = asked_places(slot_order, plane, member, group, count)

    half = group // 2
    carried, near = [], []
    if half:
        carried = weight_sums(info, weights, pairs, 0, half)
        near = [[across(pair, back * group, 0) for pair in pairs[:half]] for back in range(behind, 0, -1)]
    waits = [array for arrays in near for array in arrays] + [places]
    own, onward, *sent = weight_sums(info, weights, pairs, half, group, carried, waits)
    onward = onward if group - half > 1 else onward[0]
    earlier = []
    for n, back in enumerate(range(behind, 0, -1)):
        earlier.extend((near[n] if half else []) + [across(onward, back * group, 0)])
    asked = trade(split_heads(info, [queries], [own]), count)
    lent = [back_across(piece, 1) for piece in asked] + pairs if lending else []

    own, came, added = forward_sums(own, sent, group, count)
    own_part = own_attention(info, asked, pairs, added[:1])
    cross_part = cross_attention(info, asked, earlier, lent, list(own_part[:1]) + added[1:4])
    lent_part = [across(value, group, 1) for value in cross_part] if lending else []
    leaving = finish_rows(
        info, rate, weights, places, own, came, asked, own_part, cross_part, lent_part, count
    )

    came = lax.all_to_all(leaving, "seq", split_axis=0, concat_axis=0, tiled=True)
    came = came.reshape(planes, group, group * seg, width)
    wide = came.astype(jnp.float32)
    power = lax.psum(jnp.sum(wide * wide, axis=(1, 3)), "head")
    scale = lax.rsqrt(power / (group * lax.axis_size("head") * width) + eps)
    return norm_rows(came, scale[:, :, None], out_gain[:, None, :])


def solution(mesh):
    return jax.shard_map(
        per_device,
        mesh=mesh,
        in_specs=(
            P("seq", "head", None),
            P("seq", "head", None),
            P("seq", "head", None),
            P(None, "head", None, None),
            P("head"),
            P("head", None),
            P(),
            P("seq"),
        ),
        out_specs=P("seq", "head", None),
        check_vma=False,
    )
```

```python
import functools
import math

import jax
import jax.numpy as jnp
from jax import lax
from jax.experimental import pallas as pl
from jax.experimental.pallas import tpu as pltpu
from jax.sharding import PartitionSpec as P

WINDOW = 2048
NEG = -1e30
MIB = 1024 * 1024

eps = 1e-06

NT = (((1,), (1,)), ((), ()))
TN = (((0,), (0,)), ((), ()))
NN = (((1,), (0,)), ((), ()))

ANY = pl.BlockSpec(memory_space=pl.ANY)
SMEM = pl.BlockSpec(memory_space=pltpu.SMEM)
VMEM = pl.BlockSpec(memory_space=pltpu.VMEM)


def dot(left, right, dims):
    return lax.dot_general(left, right, dims, preferred_element_type=jnp.float32)


def params(mib):
    return pltpu.CompilerParams(vmem_limit_bytes=mib * MIB)


def swap_pairs(count, distance):
    return [(index, index ^ distance) for index in range(count)]


def plane_pairs(count, steps):
    return [(index, index + steps) for index in range(count - steps)]


def split_kernel(total, group, info_ref, *refs):
    x_refs = refs[:total]
    outs = refs[len(refs) - group - 2 : len(refs) - 2]
    buf, sems = refs[-2:]
    member = info_ref[1]
    for t, x_ref in enumerate(x_refs):
        buf[:, t] = jnp.swapaxes(x_ref[...], 0, 1)
    copies = [
        pltpu.make_async_copy(buf.at[member ^ d], outs[d], sems.at[d]) for d in range(group)
    ]
    for copy in copies:
        copy.start()
    for copy in copies:
        copy.wait()


def split_heads(info, arrays, after=()):
    tok, group, width = arrays[0].shape
    total = len(arrays)
    return pl.pallas_call(
        functools.partial(split_kernel, total, group),
        out_shape=[jax.ShapeDtypeStruct((total, tok, width), jnp.bfloat16)] * group,
        in_specs=[SMEM] + [VMEM] * total + [ANY] * len(after),
        out_specs=[ANY] * group,
        scratch_shapes=[
            pltpu.VMEM((group, total, tok, width), jnp.bfloat16),
            pltpu.SemaphoreType.DMA((group,)),
        ],
        compiler_params=params(20),
        name="split_heads",
    )(info, *arrays, *after)


def trade(pieces, count):
    return [
        lax.ppermute(piece, "seq", swap_pairs(count, d)) if d else piece
        for d, piece in enumerate(pieces)
    ]


def grad_kernel(group, tok, first, last, carried, info_ref, w_ref, *refs):
    pieces = last - first
    kv_any, refs = refs[:pieces], refs[pieces:]
    kvbuf, acc, sems, acc_sem = refs[-4:]
    plane, member, first_len = info_ref[0], info_ref[1], info_ref[2]
    copies = [pltpu.make_async_copy(kv_any[n], kvbuf.at[n], sems.at[n]) for n in range(pieces)]
    for copy in copies:
        copy.start()
    if carried:
        load = pltpu.make_async_copy(refs[0], acc, acc_sem.at[0])
        load.start()
        load.wait()
    else:
        acc[...] = jnp.zeros_like(acc)
    hidden = w_ref.shape[1]
    part = min(256, hidden)
    for copy in copies:
        copy.wait()

    def piece(n, carry):
        first_tok = (plane * group + (member ^ (first + n))) * tok

        @pl.when(first_tok < first_len)
        def _():
            keys = kvbuf[n, 0]
            token = first_tok + lax.broadcasted_iota(jnp.int32, (tok, 1), 0)
            values = jnp.where(token < first_len, kvbuf[n, 1].astype(jnp.float32), 0.0)
            values = values.astype(jnp.bfloat16)
            for f in range(0, hidden, part):
                rows = pl.ds(f, part)
                gate = dot(keys, w_ref[0, rows, :], NT)
                up = dot(keys, w_ref[1, rows, :], NT)
                back = dot(values, w_ref[2, rows, :], NT)
                sig = jax.nn.sigmoid(gate)
                silu = gate * sig
                act = (silu * up).astype(jnp.bfloat16)
                grad_up = (back * silu).astype(jnp.bfloat16)
                grad_gate = (back * up * sig * (1.0 + gate * (1.0 - sig))).astype(jnp.bfloat16)
                acc[0, rows, :] += dot(grad_gate, keys, TN)
                acc[1, rows, :] += dot(grad_up, keys, TN)
                acc[2, rows, :] += dot(act, values, TN)

        return carry

    lax.fori_loop(0, pieces, piece, 0)
    whole = last == group
    outs = refs[len(refs) - 4 - (4 if whole else 1) : len(refs) - 4]
    keep = pltpu.make_async_copy(acc, outs[0], acc_sem.at[1])
    keep.start()
    for c, sent in enumerate(outs[1:]):
        sent[...] = acc[c].astype(sent.dtype)
    keep.wait()


def weight_sums(info, weights, pairs, first, last, carried=(), after=()):
    group = len(pairs)
    _, tok, width = pairs[0].shape
    rows, hidden, _ = weights.shape
    pieces = last - first
    whole = last == group
    return pl.pallas_call(
        functools.partial(grad_kernel, group, tok, first, last, len(carried)),
        out_shape=[jax.ShapeDtypeStruct(weights.shape, jnp.float32)]
        + [jax.ShapeDtypeStruct((hidden, width), jnp.bfloat16)] * (rows * whole),
        in_specs=[SMEM, VMEM] + [ANY] * (pieces + len(carried) + len(after)),
        out_specs=[ANY] + [VMEM] * (rows * whole),
        scratch_shapes=[
            pltpu.VMEM((pieces, 2, tok, width), jnp.bfloat16),
            pltpu.VMEM(weights.shape, jnp.float32),
            pltpu.SemaphoreType.DMA((pieces,)),
            pltpu.SemaphoreType.DMA((2,)),
        ],
        compiler_params=params(28),
        name="weight_sums",
    )(info, weights, *pairs[first:last], *carried, *after)


def lanes_sum(expo):
    total = expo[:, :128]
    for lane in range(128, expo.shape[1], 128):
        total = total + expo[:, lane : lane + 128]
    return total


def soft_steps(parts, scale, fresh, acc, top, norm):
    scores = [
        dot(rows, keys, NT) if mask is None else jnp.where(mask, dot(rows, keys, NT), NEG)
        for _, rows, keys, _, mask in parts
    ]
    done = []
    for (where, _, _, _, _), score in zip(parts, scores):
        peak = jnp.max(score, axis=1, keepdims=True)
        if fresh:
            decay = None
        else:
            before = top[where, :1]
            peak = jnp.maximum(peak, before)
            decay = jnp.exp2((before - peak) * scale)
        expo = jnp.exp2((score - peak) * scale)
        done.append((peak, decay, lanes_sum(expo), expo.astype(jnp.bfloat16)))
    for (where, _, _, values, _), (peak, decay, total, expo) in zip(parts, done):
        mixed = dot(expo, values, NN)
        wide = (peak.shape[0], 128)
        top[where, :] = jnp.broadcast_to(peak, wide)
        if fresh:
            norm[where, :] = total
            acc[where, :] = mixed
        else:
            norm[where, :] = norm[where, :] * decay + total
            acc[where, :] = acc[where, :] * decay + mixed


def soft_close(scale, acc, top, norm, out_ref, level_ref):
    total = jnp.sum(norm[...], axis=1, keepdims=True)
    out_ref[...] = (acc[...] / jnp.maximum(total, 1e-30)).astype(out_ref.dtype)
    level = top[...] * scale + jnp.log2(jnp.maximum(total, 1e-30))
    level_ref[...] = jnp.transpose(level)[:8]


def as_column(rows):
    return jnp.transpose(jnp.concatenate([rows] * 16, axis=0))[:, :1]


def score_scale(width):
    return math.log2(math.e) / math.sqrt(width)


def triangle(rows, cols, first_row, first_col, lower):
    row = first_row + lax.broadcasted_iota(jnp.int32, (rows, cols), 0)
    col = first_col + lax.broadcasted_iota(jnp.int32, (rows, cols), 1)
    return col <= row if lower else col > row


def own_kernel(group, tok, part, first, last, info_ref, *refs):
    count = last - first
    q_any, kv_any = refs[:count], refs[count : count + group]
    out_ref, level_ref, onward, acc, top, norm, qbuf, kvbuf, sems, on_sem = refs[-10:]
    member = info_ref[1]
    copies = []
    for n in range(count):
        copies.append(pltpu.make_async_copy(q_any[n], qbuf.at[pl.ds(n, 1)], sems.at[0, n]))
    for d in range(group):
        copies.append(pltpu.make_async_copy(kv_any[d], kvbuf.at[d], sems.at[1, d]))
    for copy in copies:
        copy.start()
    for copy in copies:
        copy.wait()
    pass_on = pltpu.make_async_copy(kvbuf.at[group - 1], onward, on_sem.at[0])
    pass_on.start()
    scale = score_scale(qbuf.shape[-1])

    def piece(n, carry):
        d = first + n
        parts = []
        for r in range(0, tok, part):
            where, keys = pl.ds(r, part), pl.ds(0, r + part)
            mask = triangle(part, r + part, r, 0, True)
            parts.append((where, qbuf[n, where], kvbuf[d, 0, keys], kvbuf[d, 1, keys], mask))
        soft_steps(parts, scale, True, acc, top, norm)

        def earlier(other, carry):
            e = member ^ other
            parts = []
            for r in range(0, tok, part):
                where = pl.ds(r, part)
                parts.append((where, qbuf[n, where], kvbuf[e, 0], kvbuf[e, 1], None))
            soft_steps(parts, scale, False, acc, top, norm)
            return carry

        lax.fori_loop(0, member ^ d, earlier, 0)
        soft_close(scale, acc, top, norm, out_ref.at[n], level_ref.at[n])
        return carry

    lax.fori_loop(0, count, piece, 0)
    pass_on.wait()


def soft_shapes(group, tok, width):
    return [
        jax.ShapeDtypeStruct((group, tok, width), jnp.bfloat16),
        jax.ShapeDtypeStruct((group, 8, tok), jnp.float32),
    ]


def soft_scratch(tok, width):
    return [
        pltpu.VMEM((tok, width), jnp.float32),
        pltpu.VMEM((tok, 128), jnp.float32),
        pltpu.VMEM((tok, 128), jnp.float32),
    ]


def own_attention(info, queries, pairs, first, last, after=()):
    group = len(queries)
    _, tok, width = pairs[0].shape
    part = min(256, tok)
    count = last - first
    return pl.pallas_call(
        functools.partial(own_kernel, group, tok, part, first, last),
        out_shape=soft_shapes(count, tok, width)
        + [jax.ShapeDtypeStruct(pairs[0].shape, jnp.bfloat16)],
        in_specs=[SMEM] + [ANY] * (count + group + len(after)),
        out_specs=[VMEM] * 2 + [ANY],
        scratch_shapes=soft_scratch(tok, width)
        + [
            pltpu.VMEM((count, tok, width), jnp.bfloat16),
            pltpu.VMEM((group, 2, tok, width), jnp.bfloat16),
            pltpu.SemaphoreType.DMA((2, group)),
            pltpu.SemaphoreType.DMA((1,)),
        ],
        compiler_params=params(28),
        name="own_attention",
    )(info, *queries[first:last], *pairs, *after)


def pick_copy(flag, first, second, into, sem):
    if second is None:
        copy = pltpu.make_async_copy(first, into, sem)
        copy.start()
        return copy

    @pl.when(flag == 0)
    def _():
        pltpu.make_async_copy(first, into, sem).start()

    @pl.when(flag != 0)
    def _():
        pltpu.make_async_copy(second, into, sem).start()

    return pltpu.make_async_copy(first, into, sem)


def cross_kernel(group, tok, behind, part, lending, info_ref, *refs):
    pieces = behind * group
    q_any, refs = refs[:group], refs[group:]
    kv_any, refs = refs[:pieces], refs[pieces:]
    lent_q, lent_kv = [None] * group, [None] * pieces
    if lending:
        lent_q, lent_kv, refs = refs[:group], refs[group : 2 * group], refs[2 * group :]
    out_ref, level_ref, acc, top, norm, qbuf, kvbuf, sems, kv_sems = refs[-9:]
    plane, member, lends, planes = info_ref[0], info_ref[1], info_ref[3], info_ref[4]
    copies = [
        pick_copy(lends, kv_any[at], lent_kv[at], kvbuf.at[at], kv_sems.at[at])
        for at in range(pieces)
    ]
    for d in range(group):
        copies.append(pick_copy(lends, q_any[d], lent_q[d], qbuf.at[pl.ds(d, 1)], sems.at[d]))
    for copy in copies:
        copy.wait()
    scale = score_scale(qbuf.shape[-1])
    valid = jnp.maximum(behind - plane, 0) * group
    if lending:
        valid = jnp.where(lends == 0, valid, jnp.where(plane + 1 < planes, 0, pieces))

    def piece(d, carry):
        at = member ^ d

        @pl.when(at >= valid)
        def _():
            parts = []
            for r in range(0, tok, part):
                where, keys = pl.ds(r, part), pl.ds(r, tok - r)
                mask = triangle(part, tok - r, r, r, False)
                parts.append((where, qbuf[d, where], kvbuf[d, 0, keys], kvbuf[d, 1, keys], mask))
            soft_steps(parts, scale, True, acc, top, norm)

        @pl.when(at < valid)
        def _():
            acc[...] = jnp.zeros_like(acc)
            norm[...] = jnp.zeros_like(norm)
            top[...] = jnp.full_like(top, NEG)

        def later(other, carry):
            e = other // group * group + (member ^ (other % group))
            parts = []
            for r in range(0, tok, part):
                where = pl.ds(r, part)
                parts.append((where, qbuf[d, where], kvbuf[e, 0], kvbuf[e, 1], None))
            soft_steps(parts, scale, False, acc, top, norm)
            return carry

        lax.fori_loop(jnp.maximum(at + 1, valid), pieces, later, 0)
        soft_close(scale, acc, top, norm, out_ref.at[d], level_ref.at[d])
        return carry

    lax.fori_loop(0, group, piece, 0)


def cross_attention(info, queries, earlier, lent, after=()):
    group = len(queries)
    _, tok, width = queries[0].shape
    behind = len(earlier) // group
    part = min(256, tok)
    return pl.pallas_call(
        functools.partial(cross_kernel, group, tok, behind, part, len(lent)),
        out_shape=soft_shapes(group, tok, width),
        in_specs=[SMEM] + [ANY] * (group + len(earlier) + len(lent) + len(after)),
        out_specs=[VMEM] * 2,
        scratch_shapes=soft_scratch(tok, width)
        + [
            pltpu.VMEM((group, tok, width), jnp.bfloat16),
            pltpu.VMEM((behind * group, 2, tok, width), jnp.bfloat16),
            pltpu.SemaphoreType.DMA((group,)),
            pltpu.SemaphoreType.DMA((behind * group,)),
        ],
        compiler_params=params(28),
        name="cross_attention",
    )(info, *queries, *earlier, *lent, *after)


def finish_kernel(group, tok, count, hops, lending, cuts, info_ref, rate_ref, w_ref, place_ref, *refs):
    own_any, refs = refs[0], refs[1:]
    came, refs = refs[: 3 * hops], refs[3 * hops :]
    q_any, refs = refs[:group], refs[group:]
    own_parts, refs = refs[: 2 * len(cuts)], refs[2 * len(cuts) :]
    cross_any, cross_level = refs[:2]
    lent_any, lent_level = refs[2:4] if lending else (None, None)
    out_ref, new_w, sums, cbuf, qbuf, obuf, xbuf, lbuf, sems, q_sems, own_sems = refs[-11:]
    plane, member, first_len, lends = info_ref[0], info_ref[1], info_ref[2], info_ref[3]
    own_copy = pltpu.make_async_copy(own_any, sums, sems.at[0])
    own_copy.start()

    def came_copy(hop, c):
        return pltpu.make_async_copy(came[3 * hop + c], cbuf.at[c], sems.at[1 + c])

    for hop in range(hops):

        @pl.when(plane == hop + 1)
        def _():
            for c in range(3):
                came_copy(hop, c).start()

    if hops:

        @pl.when((plane == 0) | (plane > hops))
        def _():
            cbuf[...] = jnp.zeros_like(cbuf)

    level_copies = [pick_copy(lends, cross_level, lent_level, lbuf.at[1], sems.at[5])]
    row_copies = [pick_copy(lends, cross_any, lent_any, xbuf, sems.at[7])]
    for n, (first, last) in enumerate(cuts):
        into = pl.ds(first, last - first)
        rows, level = own_parts[2 * n], own_parts[2 * n + 1]
        row_copies.append(pltpu.make_async_copy(rows, obuf.at[into], own_sems.at[0, n]))
        level_copies.append(pltpu.make_async_copy(level, lbuf.at[0, into], own_sems.at[1, n]))
        row_copies[-1].start()
        level_copies[-1].start()
    q_copies = [
        pltpu.make_async_copy(q_any[d], qbuf.at[pl.ds(d, 1)], q_sems.at[d]) for d in range(group)
    ]
    for copy in q_copies:
        copy.start()
    own_copy.wait()
    if hops:

        @pl.when((plane > 0) & (plane <= hops))
        def _():
            for c in range(3):
                came_copy(0, c).wait()

    step = rate_ref[0] / first_len.astype(jnp.float32)

    @pl.when((plane + 1) * group * tok > first_len)
    def _():
        for c in range(3):
            previous = w_ref[c].astype(jnp.float32)
            summed = sums[c]
            if hops:
                summed = summed + cbuf[c].astype(jnp.float32)
            updated = previous + step * summed
            old_norm = jnp.sqrt(jnp.sum(previous * previous, axis=1, keepdims=True) + eps)
            new_norm = jnp.sqrt(jnp.sum(updated * updated, axis=1, keepdims=True) + eps)
            new_w[c] = (updated * (old_norm / new_norm)).astype(new_w.dtype)

    for copy in q_copies + level_copies + row_copies:
        copy.wait()

    def apply(rows, weights):
        gate = dot(rows, weights[0], NT)
        up = dot(rows, weights[1], NT)
        act = (gate * jax.nn.sigmoid(gate) * up).astype(jnp.bfloat16)
        return dot(act, weights[2], NN)

    seg = tok // count

    def piece(d, carry):
        at = member ^ d
        first_tok = (plane * group + at) * tok
        own_log, cross_log = as_column(lbuf[0, d]), as_column(lbuf[1, d])
        cross_log = jnp.where(plane > 0, cross_log, NEG)
        own_part = 1.0 / (1.0 + jnp.exp2(cross_log - own_log))
        cross_part = 1.0 / (1.0 + jnp.exp2(own_log - cross_log))
        mixed = obuf[d].astype(jnp.float32) * own_part + xbuf[d].astype(jnp.float32) * cross_part
        mixed = mixed.astype(jnp.bfloat16).astype(jnp.float32)

        def leave(fast):
            rows = (mixed + fast).astype(jnp.bfloat16)
            pick = as_column(place_ref[at]).astype(jnp.int32)
            pick = pick == lax.broadcasted_iota(jnp.int32, (tok, tok), 1)
            sorted_rows = dot(pick.astype(jnp.bfloat16), rows, NN)
            out_ref[:, at] = sorted_rows.reshape(count, seg, rows.shape[-1]).astype(out_ref.dtype)

        @pl.when(first_tok + tok <= first_len)
        def _():
            leave(apply(qbuf[d], w_ref))

        @pl.when(first_tok >= first_len)
        def _():
            leave(apply(qbuf[d], new_w))

        @pl.when((first_tok < first_len) & (first_tok + tok > first_len))
        def _():
            token = first_tok + lax.broadcasted_iota(jnp.int32, (tok, 1), 0)
            leave(jnp.where(token < first_len, apply(qbuf[d], w_ref), apply(qbuf[d], new_w)))

        return carry

    lax.fori_loop(0, group, piece, 0)


def finish_rows(
    info, rate, weights, places, own, came, queries, cuts, own_parts, cross_part, lent, count
):
    group = len(queries)
    _, tok, width = queries[0].shape
    hidden = weights.shape[1]
    hops = len(came) // 3
    return pl.pallas_call(
        functools.partial(finish_kernel, group, tok, count, hops, len(lent), cuts),
        out_shape=jax.ShapeDtypeStruct((count, group, tok // count, width), jnp.bfloat16),
        in_specs=[SMEM] * 2 + [VMEM] * 2 + [ANY] * (
            1 + 3 * hops + group + len(own_parts) + 2 + len(lent)
        ),
        out_specs=VMEM,
        scratch_shapes=[
            pltpu.VMEM(weights.shape, jnp.bfloat16),
            pltpu.VMEM(weights.shape, jnp.float32),
            pltpu.VMEM(weights.shape, jnp.bfloat16),
            pltpu.VMEM((group, tok, width), jnp.bfloat16),
            pltpu.VMEM((group, tok, width), jnp.bfloat16),
            pltpu.VMEM((group, tok, width), jnp.bfloat16),
            pltpu.VMEM((2, group, 8, tok), jnp.float32),
            pltpu.SemaphoreType.DMA((8,)),
            pltpu.SemaphoreType.DMA((group,)),
            pltpu.SemaphoreType.DMA((2, len(cuts))),
        ],
        compiler_params=params(36),
        name="finish_rows",
    )(info, rate, weights, places, own, *came, *queries, *own_parts, *cross_part, *lent)


def norm_kernel(came_ref, scale_ref, gain_ref, out_ref):
    scaled = came_ref[0].astype(jnp.float32) * scale_ref[...] * gain_ref[...]
    out_ref[...] = jnp.swapaxes(scaled.astype(out_ref.dtype), 0, 1)


def norm_rows(came, scale, gain):
    planes, group, rows, width = came.shape
    return pl.pallas_call(
        norm_kernel,
        grid=(planes,),
        out_shape=jax.ShapeDtypeStruct((planes * rows, group, width), jnp.bfloat16),
        in_specs=[
            pl.BlockSpec((1, group, rows, width), lambda z: (z, 0, 0, 0)),
            pl.BlockSpec((1, rows, 1), lambda z: (z, 0, 0)),
            pl.BlockSpec((group, 1, width), lambda z: (0, 0, 0)),
        ],
        out_specs=pl.BlockSpec((rows, group, width), lambda z: (z, 0, 0)),
        compiler_params=params(20),
        name="norm_rows",
    )(came, scale, gain)


def add_kernel(c, own_any, came_ref, *refs):
    out_ref, buf, sem = refs[-3:]
    copy = pltpu.make_async_copy(own_any.at[c], buf, sem.at[0])
    copy.start()
    copy.wait()
    out_ref[...] = (buf[...] + came_ref[...].astype(jnp.float32)).astype(out_ref.dtype)


def hop_add(own, came, c, after=()):
    return pl.pallas_call(
        functools.partial(add_kernel, c),
        out_shape=jax.ShapeDtypeStruct(came.shape, came.dtype),
        in_specs=[ANY, VMEM] + [ANY] * len(after),
        out_specs=VMEM,
        scratch_shapes=[pltpu.VMEM(came.shape, jnp.float32), pltpu.SemaphoreType.DMA((1,))],
        compiler_params=params(8),
        name="hop_add",
    )(own, came, *after)


def pass_kernel(x_any, *refs):
    out_any, sem = refs[-2:]
    copy = pltpu.make_async_copy(x_any, out_any, sem.at[0])
    copy.start()
    copy.wait()


def pass_after(value, after):
    return pl.pallas_call(
        pass_kernel,
        out_shape=jax.ShapeDtypeStruct(value.shape, value.dtype),
        in_specs=[ANY] * (1 + len(after)),
        out_specs=ANY,
        scratch_shapes=[pltpu.SemaphoreType.DMA((1,))],
        name="pass_after",
    )(value, *after)


def as_places(asked, group, tok):
    places = jnp.transpose(asked, (1, 0, 2)).reshape(group, 1, tok).astype(jnp.float32)
    return jnp.broadcast_to(places, (group, 8, tok))


def asked_places(slot_order, group, count):
    tok = slot_order.shape[0]
    seg, planes = tok // count, count // group
    wanted = (slot_order % tok).reshape(planes, 1, group * seg)
    wanted = jnp.broadcast_to(wanted, (planes, group, group * seg))
    wanted = wanted.reshape(count, group * seg)
    asked = lax.all_to_all(wanted, "seq", split_axis=0, concat_axis=0, tiled=True)
    return as_places(asked.reshape(count, group, seg), group, tok)


def per_device(
    queries, token_keys, token_values, fast_weights, learn_rate, out_gain, group_lengths, slot_order
):
    tok, group, width = queries.shape
    count = lax.axis_size("seq")
    seg = tok // count
    planes = count // group
    behind = WINDOW // (group * tok)
    sides = lax.axis_size("head")
    lending = behind == 1 and sides % 2 == 0
    position = lax.axis_index("seq")
    plane, member = position // group, position % group
    lends = lax.axis_index("head") % 2 if lending else jnp.int32(0)
    info = jnp.stack([plane, member, group_lengths[0], lends, jnp.int32(planes)])
    info = info.astype(jnp.int32)

    def across(value, steps, odd):
        pairs = plane_pairs(count, steps)
        if not lending:
            return lax.ppermute(value, "seq", pairs)
        both = [(a * sides + h, b * sides + h) for a, b in pairs for h in range(odd, sides, 2)]
        return lax.ppermute(value, ("seq", "head"), both)

    def back_across(value, odd):
        pairs = [(b, a) for a, b in plane_pairs(count, group)]
        both = [(a * sides + h, b * sides + h) for a, b in pairs for h in range(odd, sides, 2)]
        return lax.ppermute(value, ("seq", "head"), both)

    mine = split_heads(info, [token_keys, token_values])
    weights = lax.dynamic_index_in_dim(fast_weights, member, 1, keepdims=False)
    weights = jnp.transpose(weights, (1, 0, 2))
    rate = lax.dynamic_slice_in_dim(learn_rate, member, 1)
    places = asked_places(slot_order, group, count)

    last = group - 1
    pairs = trade(mine[:last] or mine, count)
    if last:
        late = pass_after(mine[last], pairs[1:])
        pairs = pairs + [lax.ppermute(late, "seq", swap_pairs(count, last))]
    shifts = [back * group for back in range(behind, 0, -1)]
    near = [[across(pair, shift, 0) for pair in pairs[:last]] for shift in shifts]
    carried = weight_sums(info, weights, pairs, 0, last) if last else []
    waits = [array for arrays in near for array in arrays[:2]] + [places]
    own, *sent = weight_sums(info, weights, pairs, last, group, carried, waits)
    asked = trade(split_heads(info, [queries], [own]), count)
    lent = [back_across(piece, 1) for piece in asked] + pairs if lending else []

    chained = planes <= 8
    hops = planes - 1 if chained else 0
    came = {}

    def hop(step, c, value):
        sources = [(step - 1) * group + m for m in range(group)]
        came[step, c] = lax.ppermute(value, "seq", [(a, a + group) for a in sources])

    if chained:
        for c in range(3 if hops else 0):
            hop(1, c, sent[c])
    else:
        groups = [[z * group + m for z in range(planes)] for m in range(group)]
        own = lax.psum(own.astype(jnp.bfloat16), "seq", axis_index_groups=groups)
        own = own.astype(jnp.float32)
    adds = [(step, c) for step in range(2, hops + 1) for c in range(3)]
    adds.sort(key=lambda add: (sum(add), add))
    cuts = [cut for cut in ((0, 1), (1, last), (max(1, last), group)) if cut[1] > cut[0]]
    work = [("own", cuts[0])]
    for n in range(max(len(adds), len(cuts) - 1)):
        work.extend([("add", add) for add in adds[n : n + 1]])
        work.extend([("own", cut) for cut in cuts[n + 1 : n + 2]])
    work.insert(len(work) - 1 if adds else len(work), ("cross", None))
    own_parts, cross_part, token, earlier = [], None, [own], []
    for kind, what in work:
        if kind == "add":
            added = hop_add(own, came[what[0] - 1, what[1]], what[1], token)
            hop(*what, added)
            token = [added]
        elif kind == "own":
            begun = len(own_parts) // 2
            ready = lent[cuts[begun - 1][0] : cuts[begun - 1][1]] if lending and begun else []
            rows, level, onward = own_attention(info, asked, pairs, *what, token + ready)
            if not own_parts:
                for arrays, shift in zip(near, shifts):
                    earlier.extend(arrays + [across(onward, shift, 0)])
            own_parts.extend([rows, level])
            token = [rows]
        else:
            cross_part = cross_attention(info, asked, earlier, lent, token)
            token = [cross_part[0]]
    lent_part = [across(value, group, 1) for value in cross_part] if lending else []
    arrived = [came[step, c] for step in range(1, hops + 1) for c in range(3)]
    leaving = finish_rows(
        info, rate, weights, places, own, arrived, asked, cuts, own_parts, cross_part, lent_part, count
    )

    came = lax.all_to_all(leaving, "seq", split_axis=0, concat_axis=0, tiled=True)
    came = came.reshape(planes, group, group * seg, width)
    wide = came.astype(jnp.float32)
    power = lax.psum(jnp.sum(wide * wide, axis=(1, 3)), "head")
    scale = lax.rsqrt(power / (group * lax.axis_size("head") * width) + eps)
    return norm_rows(came, scale[:, :, None], out_gain[:, None, :])


def solution(mesh):
    return jax.shard_map(
        per_device,
        mesh=mesh,
        in_specs=(
            P("seq", "head", None),
            P("seq", "head", None),
            P("seq", "head", None),
            P(None, "head", None, None),
            P("head"),
            P("head", None),
            P(),
            P("seq"),
        ),
        out_specs=P("seq", "head", None),
        check_vma=False,
    )
```

```python
import functools
import math

import jax
import jax.numpy as jnp
from jax import lax
from jax.experimental import pallas as pl
from jax.experimental.pallas import tpu as pltpu
from jax.sharding import PartitionSpec as P

WINDOW = 2048
NEG = -1e30
MIB = 1024 * 1024

eps = 1e-06

NT = (((1,), (1,)), ((), ()))
TN = (((0,), (0,)), ((), ()))
NN = (((1,), (0,)), ((), ()))

ANY = pl.BlockSpec(memory_space=pl.ANY)
SMEM = pl.BlockSpec(memory_space=pltpu.SMEM)
VMEM = pl.BlockSpec(memory_space=pltpu.VMEM)


def dot(left, right, dims):
    return lax.dot_general(left, right, dims, preferred_element_type=jnp.float32)


def params(mib):
    return pltpu.CompilerParams(vmem_limit_bytes=mib * MIB)


def swap_pairs(count, distance):
    return [(index, index ^ distance) for index in range(count)]


def plane_pairs(count, steps):
    return [(index, index + steps) for index in range(count - steps)]


def split_kernel(total, group, info_ref, *refs):
    x_refs = refs[:total]
    outs = refs[len(refs) - group - 2 : len(refs) - 2]
    buf, sems = refs[-2:]
    member = info_ref[1]
    for t, x_ref in enumerate(x_refs):
        buf[:, t] = jnp.swapaxes(x_ref[...], 0, 1)
    copies = [
        pltpu.make_async_copy(buf.at[member ^ d], outs[d], sems.at[d]) for d in range(group)
    ]
    for copy in copies:
        copy.start()
    for copy in copies:
        copy.wait()


def split_heads(info, arrays, after=()):
    tok, group, width = arrays[0].shape
    total = len(arrays)
    return pl.pallas_call(
        functools.partial(split_kernel, total, group),
        out_shape=[jax.ShapeDtypeStruct((total, tok, width), jnp.bfloat16)] * group,
        in_specs=[SMEM] + [VMEM] * total + [ANY] * len(after),
        out_specs=[ANY] * group,
        scratch_shapes=[
            pltpu.VMEM((group, total, tok, width), jnp.bfloat16),
            pltpu.SemaphoreType.DMA((group,)),
        ],
        compiler_params=params(20),
        name="split_heads",
    )(info, *arrays, *after)


def trade(pieces, count):
    return [
        lax.ppermute(piece, "seq", swap_pairs(count, d)) if d else piece
        for d, piece in enumerate(pieces)
    ]


def grad_kernel(group, tok, first, last, carried, info_ref, w_ref, *refs):
    pieces = last - first
    kv_any, refs = refs[:pieces], refs[pieces:]
    kvbuf, acc, sems, acc_sem = refs[-4:]
    plane, member, first_len = info_ref[0], info_ref[1], info_ref[2]
    copies = [pltpu.make_async_copy(kv_any[n], kvbuf.at[n], sems.at[n]) for n in range(pieces)]
    for copy in copies:
        copy.start()
    if carried:
        load = pltpu.make_async_copy(refs[0], acc, acc_sem.at[0])
        load.start()
        load.wait()
    else:
        acc[...] = jnp.zeros_like(acc)
    hidden = w_ref.shape[1]
    part = min(256, hidden)
    for copy in copies:
        copy.wait()

    def piece(n, carry):
        first_tok = (plane * group + (member ^ (first + n))) * tok

        @pl.when(first_tok < first_len)
        def _():
            keys = kvbuf[n, 0]
            token = first_tok + lax.broadcasted_iota(jnp.int32, (tok, 1), 0)
            values = jnp.where(token < first_len, kvbuf[n, 1].astype(jnp.float32), 0.0)
            values = values.astype(jnp.bfloat16)
            for f in range(0, hidden, part):
                rows = pl.ds(f, part)
                gate = dot(keys, w_ref[0, rows, :], NT)
                up = dot(keys, w_ref[1, rows, :], NT)
                back = dot(values, w_ref[2, rows, :], NT)
                sig = jax.nn.sigmoid(gate)
                silu = gate * sig
                act = (silu * up).astype(jnp.bfloat16)
                grad_up = (back * silu).astype(jnp.bfloat16)
                grad_gate = (back * up * sig * (1.0 + gate * (1.0 - sig))).astype(jnp.bfloat16)
                acc[0, rows, :] += dot(grad_gate, keys, TN)
                acc[1, rows, :] += dot(grad_up, keys, TN)
                acc[2, rows, :] += dot(act, values, TN)

        return carry

    lax.fori_loop(0, pieces, piece, 0)
    whole = last == group
    out = refs[len(refs) - 5]
    if whole:
        out[...] = acc[...].astype(out.dtype)
    else:
        keep = pltpu.make_async_copy(acc, out, acc_sem.at[1])
        keep.start()
        keep.wait()


def weight_sums(info, weights, pairs, first, last, carried=(), after=()):
    group = len(pairs)
    _, tok, width = pairs[0].shape
    pieces = last - first
    whole = last == group
    return pl.pallas_call(
        functools.partial(grad_kernel, group, tok, first, last, len(carried)),
        out_shape=jax.ShapeDtypeStruct(weights.shape, jnp.bfloat16 if whole else jnp.float32),
        in_specs=[SMEM, VMEM] + [ANY] * (pieces + len(carried) + len(after)),
        out_specs=VMEM if whole else ANY,
        scratch_shapes=[
            pltpu.VMEM((pieces, 2, tok, width), jnp.bfloat16),
            pltpu.VMEM(weights.shape, jnp.float32),
            pltpu.SemaphoreType.DMA((pieces,)),
            pltpu.SemaphoreType.DMA((2,)),
        ],
        compiler_params=params(28),
        name="weight_sums",
    )(info, weights, *pairs[first:last], *carried, *after)


def lanes_sum(expo):
    total = expo[:, :128]
    for lane in range(128, expo.shape[1], 128):
        total = total + expo[:, lane : lane + 128]
    return total


def soft_steps(parts, scale, fresh, acc, top, norm):
    scores = [
        dot(rows, keys, NT) if mask is None else jnp.where(mask, dot(rows, keys, NT), NEG)
        for _, rows, keys, _, mask in parts
    ]
    done = []
    for (where, _, _, _, _), score in zip(parts, scores):
        peak = jnp.max(score, axis=1, keepdims=True)
        if fresh:
            decay = None
        else:
            before = top[where, :1]
            peak = jnp.maximum(peak, before)
            decay = jnp.exp2((before - peak) * scale)
        expo = jnp.exp2((score - peak) * scale)
        done.append((peak, decay, lanes_sum(expo), expo.astype(jnp.bfloat16)))
    for (where, _, _, values, _), (peak, decay, total, expo) in zip(parts, done):
        mixed = dot(expo, values, NN)
        wide = (peak.shape[0], 128)
        top[where, :] = jnp.broadcast_to(peak, wide)
        if fresh:
            norm[where, :] = total
            acc[where, :] = mixed
        else:
            norm[where, :] = norm[where, :] * decay + total
            acc[where, :] = acc[where, :] * decay + mixed


def soft_close(scale, acc, top, norm, out_ref, level_ref):
    total = jnp.sum(norm[...], axis=1, keepdims=True)
    out_ref[...] = (acc[...] / jnp.maximum(total, 1e-30)).astype(out_ref.dtype)
    level = top[...] * scale + jnp.log2(jnp.maximum(total, 1e-30))
    level_ref[...] = jnp.transpose(level)[:8]


def as_column(rows):
    return jnp.transpose(jnp.concatenate([rows] * 16, axis=0))[:, :1]


def score_scale(width):
    return math.log2(math.e) / math.sqrt(width)


def triangle(rows, cols, first_row, first_col, lower):
    row = first_row + lax.broadcasted_iota(jnp.int32, (rows, cols), 0)
    col = first_col + lax.broadcasted_iota(jnp.int32, (rows, cols), 1)
    return col <= row if lower else col > row


def own_kernel(group, tok, part, first, last, info_ref, *refs):
    count = last - first
    q_any, kv_any = refs[:count], refs[count : count + group]
    out_ref, level_ref, acc, top, norm, qbuf, kvbuf, sems = refs[-8:]
    member = info_ref[1]
    copies = []
    for n in range(count):
        copies.append(pltpu.make_async_copy(q_any[n], qbuf.at[pl.ds(n, 1)], sems.at[0, n]))
    for d in range(group):
        copies.append(pltpu.make_async_copy(kv_any[d], kvbuf.at[d], sems.at[1, d]))
    for copy in copies:
        copy.start()
    for copy in copies:
        copy.wait()
    scale = score_scale(qbuf.shape[-1])

    def piece(n, carry):
        d = first + n
        parts = []
        for r in range(0, tok, part):
            where, keys = pl.ds(r, part), pl.ds(0, r + part)
            mask = triangle(part, r + part, r, 0, True)
            parts.append((where, qbuf[n, where], kvbuf[d, 0, keys], kvbuf[d, 1, keys], mask))
        soft_steps(parts, scale, True, acc, top, norm)

        def earlier(other, carry):
            e = member ^ other
            parts = []
            for r in range(0, tok, part):
                where = pl.ds(r, part)
                parts.append((where, qbuf[n, where], kvbuf[e, 0], kvbuf[e, 1], None))
            soft_steps(parts, scale, False, acc, top, norm)
            return carry

        lax.fori_loop(0, member ^ d, earlier, 0)
        soft_close(scale, acc, top, norm, out_ref.at[n], level_ref.at[n])
        return carry

    lax.fori_loop(0, count, piece, 0)


def soft_shapes(group, tok, width):
    return [
        jax.ShapeDtypeStruct((group, tok, width), jnp.bfloat16),
        jax.ShapeDtypeStruct((group, 8, tok), jnp.float32),
    ]


def soft_scratch(tok, width):
    return [
        pltpu.VMEM((tok, width), jnp.float32),
        pltpu.VMEM((tok, 128), jnp.float32),
        pltpu.VMEM((tok, 128), jnp.float32),
    ]


def own_attention(info, queries, pairs, first, last, after=()):
    group = len(queries)
    _, tok, width = pairs[0].shape
    part = min(256, tok)
    count = last - first
    return pl.pallas_call(
        functools.partial(own_kernel, group, tok, part, first, last),
        out_shape=soft_shapes(count, tok, width),
        in_specs=[SMEM] + [ANY] * (count + group + len(after)),
        out_specs=[VMEM] * 2,
        scratch_shapes=soft_scratch(tok, width)
        + [
            pltpu.VMEM((count, tok, width), jnp.bfloat16),
            pltpu.VMEM((group, 2, tok, width), jnp.bfloat16),
            pltpu.SemaphoreType.DMA((2, group)),
        ],
        compiler_params=params(28),
        name="own_attention",
    )(info, *queries[first:last], *pairs, *after)


def pick_copy(flag, first, second, into, sem):
    if second is None:
        copy = pltpu.make_async_copy(first, into, sem)
        copy.start()
        return copy

    @pl.when(flag == 0)
    def _():
        pltpu.make_async_copy(first, into, sem).start()

    @pl.when(flag != 0)
    def _():
        pltpu.make_async_copy(second, into, sem).start()

    return pltpu.make_async_copy(first, into, sem)


def cross_kernel(group, tok, behind, part, lending, first, last, info_ref, *refs):
    pieces, count = behind * group, last - first
    q_any, refs = refs[:count], refs[count:]
    kv_any, refs = refs[:pieces], refs[pieces:]
    lent_q, lent_kv = [None] * count, [None] * pieces
    if lending:
        lent_q, lent_kv, refs = refs[:count], refs[count : count + group], refs[count + group :]
    out_ref, level_ref, acc, top, norm, qbuf, kvbuf, sems, kv_sems = refs[-9:]
    plane, member, lends, planes = info_ref[0], info_ref[1], info_ref[3], info_ref[4]
    copies = [
        pick_copy(lends, kv_any[at], lent_kv[at], kvbuf.at[at], kv_sems.at[at])
        for at in range(pieces)
    ]
    for n in range(count):
        copies.append(pick_copy(lends, q_any[n], lent_q[n], qbuf.at[pl.ds(n, 1)], sems.at[n]))
    for copy in copies:
        copy.wait()
    scale = score_scale(qbuf.shape[-1])
    valid = jnp.maximum(behind - plane, 0) * group
    if lending:
        valid = jnp.where(lends == 0, valid, jnp.where(plane + 1 < planes, 0, pieces))

    def piece(n, carry):
        d = first + n
        at = member ^ d

        @pl.when(at >= valid)
        def _():
            parts = []
            for r in range(0, tok, part):
                where, keys = pl.ds(r, part), pl.ds(r, tok - r)
                mask = triangle(part, tok - r, r, r, False)
                parts.append((where, qbuf[n, where], kvbuf[d, 0, keys], kvbuf[d, 1, keys], mask))
            soft_steps(parts, scale, True, acc, top, norm)

        @pl.when(at < valid)
        def _():
            acc[...] = jnp.zeros_like(acc)
            norm[...] = jnp.zeros_like(norm)
            top[...] = jnp.full_like(top, NEG)

        def later(other, carry):
            e = other // group * group + (member ^ (other % group))
            parts = []
            for r in range(0, tok, part):
                where = pl.ds(r, part)
                parts.append((where, qbuf[n, where], kvbuf[e, 0], kvbuf[e, 1], None))
            soft_steps(parts, scale, False, acc, top, norm)
            return carry

        lax.fori_loop(jnp.maximum(at + 1, valid), pieces, later, 0)
        soft_close(scale, acc, top, norm, out_ref.at[n], level_ref.at[n])
        return carry

    lax.fori_loop(0, count, piece, 0)


def cross_attention(info, queries, earlier, lent, pairs, first, last, after=()):
    group = len(queries)
    _, tok, width = queries[0].shape
    behind = len(earlier) // group
    part = min(256, tok)
    count = last - first
    others = lent[first:last] + pairs if lent else []
    return pl.pallas_call(
        functools.partial(cross_kernel, group, tok, behind, part, len(lent), first, last),
        out_shape=soft_shapes(count, tok, width),
        in_specs=[SMEM] + [ANY] * (count + len(earlier) + len(others) + len(after)),
        out_specs=[VMEM] * 2,
        scratch_shapes=soft_scratch(tok, width)
        + [
            pltpu.VMEM((count, tok, width), jnp.bfloat16),
            pltpu.VMEM((behind * group, 2, tok, width), jnp.bfloat16),
            pltpu.SemaphoreType.DMA((count,)),
            pltpu.SemaphoreType.DMA((behind * group,)),
        ],
        compiler_params=params(28),
        name="cross_attention",
    )(info, *queries[first:last], *earlier, *others, *after)


def finish_kernel(
    group, tok, count, lending, cuts, cross_cuts, info_ref, rate_ref, w_ref, place_ref, sum_ref, *refs
):
    q_any, refs = refs[:group], refs[group:]
    own_parts, refs = refs[: 2 * len(cuts)], refs[2 * len(cuts) :]
    cross_parts, refs = refs[: 2 * len(cross_cuts)], refs[2 * len(cross_cuts) :]
    lent_parts = refs[: 2 * len(cross_cuts)] if lending else [None] * 2 * len(cross_cuts)
    out_ref, new_w, qbuf, obuf, xbuf, lbuf, q_sems, own_sems, cross_sems = refs[-9:]
    plane, member, first_len, lends = info_ref[0], info_ref[1], info_ref[2], info_ref[3]
    copies = []
    for d in range(group):
        copies.append(pltpu.make_async_copy(q_any[d], qbuf.at[pl.ds(d, 1)], q_sems.at[d]))
    for n, (first, last) in enumerate(cuts):
        into = pl.ds(first, last - first)
        rows, level = own_parts[2 * n], own_parts[2 * n + 1]
        copies.append(pltpu.make_async_copy(level, lbuf.at[0, into], own_sems.at[1, n]))
        copies.append(pltpu.make_async_copy(rows, obuf.at[into], own_sems.at[0, n]))
    for copy in copies:
        copy.start()
    for n, (first, last) in enumerate(cross_cuts):
        into, rows, level = pl.ds(first, last - first), 2 * n, 2 * n + 1
        copies.append(
            pick_copy(
                lends, cross_parts[level], lent_parts[level], lbuf.at[1, into], cross_sems.at[1, n]
            )
        )
        copies.append(
            pick_copy(lends, cross_parts[rows], lent_parts[rows], xbuf.at[into], cross_sems.at[0, n])
        )

    step = rate_ref[0] / first_len.astype(jnp.float32)

    @pl.when((plane + 1) * group * tok > first_len)
    def _():
        for c in range(3):
            previous = w_ref[c].astype(jnp.float32)
            updated = previous + step * sum_ref[c].astype(jnp.float32)
            old_norm = jnp.sqrt(jnp.sum(previous * previous, axis=1, keepdims=True) + eps)
            new_norm = jnp.sqrt(jnp.sum(updated * updated, axis=1, keepdims=True) + eps)
            new_w[c] = (updated * (old_norm / new_norm)).astype(new_w.dtype)

    for copy in copies:
        copy.wait()

    def apply(rows, weights):
        gate = dot(rows, weights[0], NT)
        up = dot(rows, weights[1], NT)
        act = (gate * jax.nn.sigmoid(gate) * up).astype(jnp.bfloat16)
        return dot(act, weights[2], NN)

    seg = tok // count

    def piece(d, carry):
        at = member ^ d
        first_tok = (plane * group + at) * tok
        own_log, cross_log = as_column(lbuf[0, d]), as_column(lbuf[1, d])
        cross_log = jnp.where(plane > 0, cross_log, NEG)
        own_part = 1.0 / (1.0 + jnp.exp2(cross_log - own_log))
        cross_part = 1.0 / (1.0 + jnp.exp2(own_log - cross_log))
        mixed = obuf[d].astype(jnp.float32) * own_part + xbuf[d].astype(jnp.float32) * cross_part
        mixed = mixed.astype(jnp.bfloat16).astype(jnp.float32)

        def leave(fast):
            rows = (mixed + fast).astype(jnp.bfloat16)
            pick = as_column(place_ref[at]).astype(jnp.int32)
            pick = pick == lax.broadcasted_iota(jnp.int32, (tok, tok), 1)
            sorted_rows = dot(pick.astype(jnp.bfloat16), rows, NN)
            out_ref[:, at] = sorted_rows.reshape(count, seg, rows.shape[-1]).astype(out_ref.dtype)

        @pl.when(first_tok + tok <= first_len)
        def _():
            leave(apply(qbuf[d], w_ref))

        @pl.when(first_tok >= first_len)
        def _():
            leave(apply(qbuf[d], new_w))

        @pl.when((first_tok < first_len) & (first_tok + tok > first_len))
        def _():
            token = first_tok + lax.broadcasted_iota(jnp.int32, (tok, 1), 0)
            leave(jnp.where(token < first_len, apply(qbuf[d], w_ref), apply(qbuf[d], new_w)))

        return carry

    lax.fori_loop(0, group, piece, 0)


def finish_rows(
    info, rate, weights, places, sums, queries, cuts, own_parts, cross_cuts, cross_parts, lent, count
):
    group = len(queries)
    _, tok, width = queries[0].shape
    return pl.pallas_call(
        functools.partial(finish_kernel, group, tok, count, len(lent), cuts, cross_cuts),
        out_shape=jax.ShapeDtypeStruct((count, group, tok // count, width), jnp.bfloat16),
        in_specs=[SMEM] * 2
        + [VMEM] * 3
        + [ANY] * (group + len(own_parts) + len(cross_parts) + len(lent)),
        out_specs=VMEM,
        scratch_shapes=[
            pltpu.VMEM(weights.shape, jnp.bfloat16),
            pltpu.VMEM((group, tok, width), jnp.bfloat16),
            pltpu.VMEM((group, tok, width), jnp.bfloat16),
            pltpu.VMEM((group, tok, width), jnp.bfloat16),
            pltpu.VMEM((2, group, 8, tok), jnp.float32),
            pltpu.SemaphoreType.DMA((group,)),
            pltpu.SemaphoreType.DMA((2, len(cuts))),
            pltpu.SemaphoreType.DMA((2, len(cross_cuts))),
        ],
        compiler_params=params(30),
        name="finish_rows",
    )(info, rate, weights, places, sums, *queries, *own_parts, *cross_parts, *lent)


def norm_kernel(came_ref, scale_ref, gain_ref, out_ref):
    scaled = came_ref[0].astype(jnp.float32) * scale_ref[...] * gain_ref[...]
    out_ref[...] = jnp.swapaxes(scaled.astype(out_ref.dtype), 0, 1)


def norm_rows(came, scale, gain):
    planes, group, rows, width = came.shape
    return pl.pallas_call(
        norm_kernel,
        grid=(planes,),
        out_shape=jax.ShapeDtypeStruct((planes * rows, group, width), jnp.bfloat16),
        in_specs=[
            pl.BlockSpec((1, group, rows, width), lambda z: (z, 0, 0, 0)),
            pl.BlockSpec((1, rows, 1), lambda z: (z, 0, 0)),
            pl.BlockSpec((group, 1, width), lambda z: (0, 0, 0)),
        ],
        out_specs=pl.BlockSpec((rows, group, width), lambda z: (z, 0, 0)),
        compiler_params=params(20),
        name="norm_rows",
    )(came, scale, gain)


def pass_kernel(x_any, *refs):
    out_any, buf, sem = refs[-3:]
    for source, target in ((x_any, buf), (buf, out_any)):
        copy = pltpu.make_async_copy(source, target, sem.at[0])
        copy.start()
        copy.wait()


def pass_after(value, after):
    return pl.pallas_call(
        pass_kernel,
        out_shape=jax.ShapeDtypeStruct(value.shape, value.dtype),
        in_specs=[ANY] * (1 + len(after)),
        out_specs=ANY,
        scratch_shapes=[pltpu.VMEM(value.shape, value.dtype), pltpu.SemaphoreType.DMA((1,))],
        compiler_params=params(8),
        name="pass_after",
    )(value, *after)


def as_places(asked, group, tok):
    places = jnp.transpose(asked, (1, 0, 2)).reshape(group, 1, tok).astype(jnp.float32)
    return jnp.broadcast_to(places, (group, 8, tok))


def asked_places(slot_order, group, count):
    tok = slot_order.shape[0]
    seg, planes = tok // count, count // group
    wanted = (slot_order % tok).reshape(planes, 1, group * seg)
    wanted = jnp.broadcast_to(wanted, (planes, group, group * seg))
    wanted = wanted.reshape(count, group * seg)
    asked = lax.all_to_all(wanted, "seq", split_axis=0, concat_axis=0, tiled=True)
    return as_places(asked.reshape(count, group, seg), group, tok)


def per_device(
    queries, token_keys, token_values, fast_weights, learn_rate, out_gain, group_lengths, slot_order
):
    tok, group, width = queries.shape
    count = lax.axis_size("seq")
    seg = tok // count
    planes = count // group
    behind = WINDOW // (group * tok)
    sides = lax.axis_size("head")
    lending = behind == 1 and sides % 2 == 0
    position = lax.axis_index("seq")
    plane, member = position // group, position % group
    lends = lax.axis_index("head") % 2 if lending else jnp.int32(0)
    info = jnp.stack([plane, member, group_lengths[0], lends, jnp.int32(planes)])
    info = info.astype(jnp.int32)

    def across(value, steps, odd):
        pairs = plane_pairs(count, steps)
        if not lending:
            return lax.ppermute(value, "seq", pairs)
        both = [(a * sides + h, b * sides + h) for a, b in pairs for h in range(odd, sides, 2)]
        return lax.ppermute(value, ("seq", "head"), both)

    def back_across(value, odd):
        pairs = [(b, a) for a, b in plane_pairs(count, group)]
        both = [(a * sides + h, b * sides + h) for a, b in pairs for h in range(odd, sides, 2)]
        return lax.ppermute(value, ("seq", "head"), both)

    mine = split_heads(info, [token_keys, token_values])
    weights = lax.dynamic_index_in_dim(fast_weights, member, 1, keepdims=False)
    weights = jnp.transpose(weights, (1, 0, 2))
    rate = lax.dynamic_slice_in_dim(learn_rate, member, 1)
    places = asked_places(slot_order, group, count)

    last = group - 1
    pairs = trade(mine[:last] or mine, count)
    if last:
        late = pass_after(mine[last], pairs[1:] + [weights, places])
        pairs = pairs + [lax.ppermute(late, "seq", swap_pairs(count, last))]
    shifts = [back * group for back in range(behind, 0, -1)]
    earlier = [across(pair, shift, 0) for shift in shifts for pair in pairs]
    carried = weight_sums(info, weights, pairs, 0, last) if last else None
    waits = earlier[:2] if last else []
    carried = [carried] if last else []
    sums = weight_sums(info, weights, pairs, last, group, carried, waits)
    asked = split_heads(info, [queries], [sums])
    groups = [[z * group + m for z in range(planes)] for m in range(group)]
    sums = lax.psum(sums, "seq", axis_index_groups=groups)
    asked = trade(asked, count)
    lent = [back_across(piece, 1) for piece in asked] if lending else []

    cuts = [cut for cut in ((0, 1), (1, last), (max(1, last), group)) if cut[1] > cut[0]]
    cross_cuts = [(0, group)]
    own_parts, cross_parts, lent_parts, token = [], [], [], []
    for n, (first, end) in enumerate(cuts):
        if n and lending:
            token = token + lent[cuts[n - 1][0] : cuts[n - 1][1]]
        rows, level = own_attention(info, asked, pairs, first, end, token)
        own_parts.extend([rows, level])
        token = [rows] + (earlier[2:3] if n == 0 else [])
    for first, end in cross_cuts:
        rows, level = cross_attention(info, asked, earlier, lent, pairs, first, end, token)
        cross_parts.extend([rows, level])
        token = [rows]
        if lending:
            lent_parts.extend([across(rows, group, 1), across(level, group, 1)])
    leaving = finish_rows(
        info, rate, weights, places, sums, asked, cuts, own_parts, cross_cuts, cross_parts, lent_parts, count
    )

    came = lax.all_to_all(leaving, "seq", split_axis=0, concat_axis=0, tiled=True)
    came = came.reshape(planes, group, group * seg, width)
    wide = came.astype(jnp.float32)
    power = lax.psum(jnp.sum(wide * wide, axis=(1, 3)), "head")
    scale = lax.rsqrt(power / (group * lax.axis_size("head") * width) + eps)
    return norm_rows(came, scale[:, :, None], out_gain[:, None, :])


def solution(mesh):
    return jax.shard_map(
        per_device,
        mesh=mesh,
        in_specs=(
            P("seq", "head", None),
            P("seq", "head", None),
            P("seq", "head", None),
            P(None, "head", None, None),
            P("head"),
            P("head", None),
            P(),
            P("seq"),
        ),
        out_specs=P("seq", "head", None),
        check_vma=False,
    )
```

```python
import functools
import math

import jax
import jax.numpy as jnp
from jax import lax
from jax.experimental import pallas as pl
from jax.experimental.pallas import tpu as pltpu
from jax.sharding import PartitionSpec as P

WINDOW = 2048
NEG = -1e30
MIB = 1024 * 1024

eps = 1e-06

NT = (((1,), (1,)), ((), ()))
TN = (((0,), (0,)), ((), ()))
NN = (((1,), (0,)), ((), ()))

ANY = pl.BlockSpec(memory_space=pl.ANY)
SMEM = pl.BlockSpec(memory_space=pltpu.SMEM)
VMEM = pl.BlockSpec(memory_space=pltpu.VMEM)


def dot(left, right, dims):
    return lax.dot_general(left, right, dims, preferred_element_type=jnp.float32)


def params(mib):
    return pltpu.CompilerParams(vmem_limit_bytes=mib * MIB)


def swap_pairs(count, distance):
    return [(index, index ^ distance) for index in range(count)]


def plane_pairs(count, steps):
    return [(index, index + steps) for index in range(count - steps)]


def run(copies):
    for copy in copies:
        copy.start()
    for copy in copies:
        copy.wait()


def split_kernel(group, total, info_ref, *refs):
    x_any, outs = refs[:total], refs[-4 - group : -4]
    held, buf, in_sems, sems = refs[-4:]
    member = info_ref[1]
    loads = [pltpu.make_async_copy(x_any[t], held.at[t], in_sems.at[t]) for t in range(total)]
    for load in loads:
        load.start()
    copies = []
    for t in range(total):
        loads[t].wait()
        buf[:, t] = jnp.swapaxes(held[t], 0, 1)
        for d in range(group):
            source = buf.at[member ^ d, t]
            copies.append(pltpu.make_async_copy(source, outs[d].at[t], sems.at[t, d]))
            copies[-1].start()
    for copy in copies:
        copy.wait()


def split_heads(info, arrays, after=()):
    tok, group, width = arrays[0].shape
    total = len(arrays)
    return pl.pallas_call(
        functools.partial(split_kernel, group, total),
        out_shape=[jax.ShapeDtypeStruct((total, tok, width), jnp.bfloat16)] * group,
        in_specs=[SMEM] + [ANY] * (total + len(after)),
        out_specs=[ANY] * group,
        scratch_shapes=[
            pltpu.VMEM((total, tok, group, width), jnp.bfloat16),
            pltpu.VMEM((group, total, tok, width), jnp.bfloat16),
            pltpu.SemaphoreType.DMA((total,)),
            pltpu.SemaphoreType.DMA((total, group)),
        ],
        compiler_params=params(60),
        name="split_heads",
    )(info, *arrays, *after)


def trade(pieces, count):
    return [
        lax.ppermute(piece, "seq", swap_pairs(count, d)) if d else piece
        for d, piece in enumerate(pieces)
    ]


def grad_kernel(group, tok, first, last, carried, chunks, info_ref, w_ref, *refs):
    pieces = last - first
    piece_any, refs = refs[:pieces], refs[pieces:]
    kvbuf, acc, sems = refs[-3:]
    *outs, last_piece = refs[-4 - chunks : -3] if last == group else (refs[-4], None)
    onward = [last_piece] if last == group else []
    plane, member, first_len = info_ref[0], info_ref[1], info_ref[2]
    copies = [
        pltpu.make_async_copy(piece_any[n], kvbuf.at[n], sems.at[n]) for n in range(pieces)
    ]
    if carried:
        copies.append(pltpu.make_async_copy(refs[0], acc, sems.at[pieces]))
    run(copies)
    leaving = [pltpu.make_async_copy(kvbuf.at[pieces - 1], to, sems.at[0]) for to in onward]
    for copy in leaving:
        copy.start()
    if not carried:
        acc[...] = jnp.zeros_like(acc)
    hidden = w_ref.shape[1]
    part = min(256, hidden)

    def piece(n, carry):
        first_tok = (plane * group + (member ^ (first + n))) * tok

        @pl.when(first_tok < first_len)
        def _():
            keys = kvbuf[n, 0]
            token = first_tok + lax.broadcasted_iota(jnp.int32, (tok, 1), 0)
            values = jnp.where(token < first_len, kvbuf[n, 1].astype(jnp.float32), 0.0)
            values = values.astype(jnp.bfloat16)
            for f in range(0, hidden, part):
                rows = pl.ds(f, part)
                gate = dot(keys, w_ref[0, rows, :], NT)
                up = dot(keys, w_ref[1, rows, :], NT)
                back = dot(values, w_ref[2, rows, :], NT)
                sig = jax.nn.sigmoid(gate)
                silu = gate * sig
                act = (silu * up).astype(jnp.bfloat16)
                grad_up = (back * silu).astype(jnp.bfloat16)
                grad_gate = (back * up * sig * (1.0 + gate * (1.0 - sig))).astype(jnp.bfloat16)
                acc[0, rows, :] += dot(grad_gate, keys, TN)
                acc[1, rows, :] += dot(grad_up, keys, TN)
                acc[2, rows, :] += dot(act, values, TN)

        return carry

    lax.fori_loop(0, pieces, piece, 0)
    rows = hidden // chunks
    for n, out in enumerate(outs):
        at = pl.multiple_of((plane + n) % chunks * rows, rows)
        out[...] = acc[:, pl.ds(at, rows), :].astype(out.dtype)
    for copy in leaving:
        copy.wait()


def weight_sums(info, weights, pairs, first, last, carried=(), after=(), chunks=1):
    group = len(pairs)
    pieces = last - first
    kind = jnp.bfloat16 if last == group else jnp.float32
    return pl.pallas_call(
        functools.partial(grad_kernel, group, pairs[0].shape[1], first, last, len(carried), chunks),
        out_shape=[jax.ShapeDtypeStruct((3, weights.shape[1] // chunks, weights.shape[2]), kind)] * chunks
        + [jax.ShapeDtypeStruct(pairs[0].shape, jnp.bfloat16)] * (last == group),
        in_specs=[SMEM, VMEM] + [ANY] * (pieces + len(carried) + len(after)),
        out_specs=[VMEM] * chunks + [ANY] * (last == group),
        scratch_shapes=[
            pltpu.VMEM((pieces,) + pairs[0].shape, jnp.bfloat16),
            pltpu.VMEM(weights.shape, jnp.float32),
            pltpu.SemaphoreType.DMA((pieces + 1,)),
        ],
        compiler_params=params(60),
        name="weight_sums",
    )(info, weights, *pairs[first:last], *carried, *after)


def lanes_sum(expo):
    total = expo[:, :128]
    for lane in range(128, expo.shape[1], 128):
        total = total + expo[:, lane : lane + 128]
    return total


def soft_steps(parts, scale, fresh, acc, top, norm):
    scores = [
        dot(rows, keys, NT) if mask is None else jnp.where(mask, dot(rows, keys, NT), NEG)
        for _, rows, keys, _, mask in parts
    ]
    done = []
    for (where, _, _, _, _), score in zip(parts, scores):
        peak = jnp.max(score, axis=1, keepdims=True)
        if fresh:
            decay = None
        else:
            before = top[where, :1]
            peak = jnp.maximum(peak, before)
            decay = jnp.exp2((before - peak) * scale)
        expo = jnp.exp2((score - peak) * scale)
        done.append((peak, decay, lanes_sum(expo), expo.astype(jnp.bfloat16)))
    for (where, _, _, values, _), (peak, decay, total, expo) in zip(parts, done):
        mixed = dot(expo, values, NN)
        wide = (peak.shape[0], 128)
        top[where, :] = jnp.broadcast_to(peak, wide)
        if fresh:
            norm[where, :] = total
            acc[where, :] = mixed
        else:
            norm[where, :] = norm[where, :] * decay + total
            acc[where, :] = acc[where, :] * decay + mixed


def soft_close(scale, acc, top, norm, out_ref, level_ref):
    total = jnp.sum(norm[...], axis=1, keepdims=True)
    out_ref[...] = (acc[...] / jnp.maximum(total, 1e-30)).astype(out_ref.dtype)
    level = top[...] * scale + jnp.log2(jnp.maximum(total, 1e-30))
    level_ref[...] = jnp.transpose(level)[:8]


def as_column(rows):
    return jnp.transpose(jnp.concatenate([rows] * 16, axis=0))[:, :1]


def score_scale(width):
    return math.log2(math.e) / math.sqrt(width)


def triangle(rows, cols, first_row, first_col, lower):
    row = first_row + lax.broadcasted_iota(jnp.int32, (rows, cols), 0)
    col = first_col + lax.broadcasted_iota(jnp.int32, (rows, cols), 1)
    return col <= row if lower else col > row


def own_kernel(group, tok, part, first, last, info_ref, *refs):
    count = last - first
    out_ref, level_ref, acc, top, norm, qbuf, kvbuf, sems = refs[-8:]
    member = info_ref[1]
    copies = [
        pltpu.make_async_copy(refs[n], qbuf.at[pl.ds(n, 1)], sems.at[n]) for n in range(count)
    ]
    for d in range(group):
        copies.append(pltpu.make_async_copy(refs[count + d], kvbuf.at[d], sems.at[count + d]))
    run(copies)
    scale = score_scale(qbuf.shape[-1])

    def piece(n, carry):
        d = first + n
        parts = []
        for r in range(0, tok, part):
            where, keys = pl.ds(r, part), pl.ds(0, r + part)
            mask = triangle(part, r + part, r, 0, True)
            parts.append((where, qbuf[n, where], kvbuf[d, 0, keys], kvbuf[d, 1, keys], mask))
        soft_steps(parts, scale, True, acc, top, norm)

        def earlier(other, carry):
            e = member ^ other
            parts = []
            for r in range(0, tok, part):
                where = pl.ds(r, part)
                parts.append((where, qbuf[n, where], kvbuf[e, 0], kvbuf[e, 1], None))
            soft_steps(parts, scale, False, acc, top, norm)
            return carry

        lax.fori_loop(0, member ^ d, earlier, 0)
        soft_close(scale, acc, top, norm, out_ref.at[n], level_ref.at[n])
        return carry

    lax.fori_loop(0, count, piece, 0)


def soft_shapes(group, tok, width):
    return [
        jax.ShapeDtypeStruct((group, tok, width), jnp.bfloat16),
        jax.ShapeDtypeStruct((group, 8, tok), jnp.float32),
    ]


def soft_scratch(tok, width):
    return [
        pltpu.VMEM((tok, width), jnp.float32),
        pltpu.VMEM((tok, 128), jnp.float32),
        pltpu.VMEM((tok, 128), jnp.float32),
    ]


def own_attention(info, asked, pairs, first, last, after=()):
    group = len(asked)
    _, tok, width = asked[0].shape
    count = last - first
    return pl.pallas_call(
        functools.partial(own_kernel, group, tok, min(256, tok), first, last),
        out_shape=soft_shapes(count, tok, width),
        in_specs=[SMEM] + [ANY] * (count + group + len(after)),
        out_specs=[VMEM] * 2,
        scratch_shapes=soft_scratch(tok, width)
        + [
            pltpu.VMEM((count, tok, width), jnp.bfloat16),
            pltpu.VMEM((group, 2, tok, width), jnp.bfloat16),
            pltpu.SemaphoreType.DMA((count + group,)),
        ],
        compiler_params=params(60),
        name="own_attention",
    )(info, *asked[first:last], *pairs, *after)


def renorm_kernel(terms, info_ref, rate_ref, w_ref, *refs):
    out_ref = refs[-1]
    rows = out_ref.shape[1]
    mine = pl.ds(pl.multiple_of(info_ref[0] * rows, rows), rows)
    step = rate_ref[0] / info_ref[2].astype(jnp.float32)
    for c in range(w_ref.shape[0]):
        previous = w_ref[c, mine, :].astype(jnp.float32)
        summed = refs[0][c].astype(jnp.float32)
        for term in refs[1:terms]:
            summed = summed + term[c].astype(jnp.float32)
        updated = previous + step * summed
        old_norm = jnp.sqrt(jnp.sum(previous * previous, axis=1, keepdims=True) + eps)
        new_norm = jnp.sqrt(jnp.sum(updated * updated, axis=1, keepdims=True) + eps)
        out_ref[c] = (updated * (old_norm / new_norm)).astype(out_ref.dtype)


def renorm(info, rate, weights, sums, after=()):
    return pl.pallas_call(
        functools.partial(renorm_kernel, len(sums)),
        out_shape=jax.ShapeDtypeStruct(sums[0].shape, jnp.bfloat16),
        in_specs=[SMEM] * 2 + [VMEM] * (1 + len(sums)) + [ANY] * len(after),
        out_specs=VMEM,
        compiler_params=params(60),
        name="renorm",
    )(info, rate, weights, *sums, *after)


def cross_kernel(group, tok, behind, part, info_ref, *refs):
    pieces = behind * group
    out_ref, level_ref, acc, top, norm, qbuf, kvbuf, sems = refs[-8:]
    plane, member = info_ref[0], info_ref[1]
    moves = [(refs[d], qbuf.at[pl.ds(d, 1)]) for d in range(group)]
    moves += [(refs[group + at], kvbuf.at[at]) for at in range(pieces)]
    run([pltpu.make_async_copy(*move, sems.at[n]) for n, move in enumerate(moves)])
    scale = score_scale(qbuf.shape[-1])
    valid = jnp.maximum(behind - plane, 0) * group

    def piece(d, carry):
        at = member ^ d

        @pl.when(at >= valid)
        def _():
            parts = []
            for r in range(0, tok, part):
                where, keys = pl.ds(r, part), pl.ds(r, tok - r)
                mask = triangle(part, tok - r, r, r, False)
                parts.append((where, qbuf[d, where], kvbuf[d, 0, keys], kvbuf[d, 1, keys], mask))
            soft_steps(parts, scale, True, acc, top, norm)

        @pl.when(at < valid)
        def _():
            acc[...] = jnp.zeros_like(acc)
            norm[...] = jnp.zeros_like(norm)
            top[...] = jnp.full_like(top, NEG)

        def later(other, carry):
            e = other // group * group + (member ^ (other % group))
            parts = []
            for r in range(0, tok, part):
                where = pl.ds(r, part)
                parts.append((where, qbuf[d, where], kvbuf[e, 0], kvbuf[e, 1], None))
            soft_steps(parts, scale, False, acc, top, norm)
            return carry

        lax.fori_loop(jnp.maximum(at + 1, valid), pieces, later, 0)
        soft_close(scale, acc, top, norm, out_ref.at[d], level_ref.at[d])
        return carry

    lax.fori_loop(0, group, piece, 0)


def cross_attention(info, asked, earlier, after=()):
    group = len(asked)
    _, tok, width = asked[0].shape
    behind = len(earlier) // group
    operands = [*asked, *earlier, *after]
    return pl.pallas_call(
        functools.partial(cross_kernel, group, tok, behind, min(256, tok)),
        out_shape=soft_shapes(group, tok, width),
        in_specs=[SMEM] + [ANY] * len(operands),
        out_specs=[VMEM] * 2,
        scratch_shapes=soft_scratch(tok, width)
        + [
            pltpu.VMEM((group, tok, width), jnp.bfloat16),
            pltpu.VMEM((behind * group, 2, tok, width), jnp.bfloat16),
            pltpu.SemaphoreType.DMA((group + behind * group,)),
        ],
        compiler_params=params(60),
        name="cross_attention",
    )(info, *operands)


def fast_apply(rows, weights):
    gate = dot(rows, weights[0], NT)
    up = dot(rows, weights[1], NT)
    act = (gate * jax.nn.sigmoid(gate) * up).astype(jnp.bfloat16)
    return dot(act, weights[2], NN)


def first_kernel(group, tok, cuts, info_ref, w_any, *refs):
    out_ref, wbuf, qbuf, obuf, xbuf, lbuf, sems = refs[-7:]
    plane, member, first_len = info_ref[0], info_ref[1], info_ref[2]
    moves = [(w_any, wbuf)] + [(refs[d], qbuf.at[pl.ds(d, 1)]) for d in range(group)]
    for n, (first, last) in enumerate(cuts):
        into = pl.ds(first, last - first)
        rows, level = refs[group + 2 * n], refs[group + 2 * n + 1]
        moves += [(rows, obuf.at[into]), (level, lbuf.at[0, into])]
    rows, level = refs[group + 2 * len(cuts)], refs[group + 2 * len(cuts) + 1]
    moves += [(rows, xbuf), (level, lbuf.at[1])]
    run([pltpu.make_async_copy(*move, sems.at[n]) for n, move in enumerate(moves)])

    def piece(d, carry):
        first_tok = (plane * group + (member ^ d)) * tok
        own_log, cross_log = as_column(lbuf[0, d]), as_column(lbuf[1, d])
        own_part = 1.0 / (1.0 + jnp.exp2(cross_log - own_log))
        cross_part = 1.0 / (1.0 + jnp.exp2(own_log - cross_log))
        mixed = obuf[d].astype(jnp.float32) * own_part + xbuf[d].astype(jnp.float32) * cross_part
        out_ref[d] = mixed.astype(out_ref.dtype)

        @pl.when(first_tok < first_len)
        def _():
            token = first_tok + lax.broadcasted_iota(jnp.int32, (tok, 1), 0)
            fast = jnp.where(token < first_len, fast_apply(qbuf[d], wbuf), 0.0)
            out_ref[d] = (out_ref[d].astype(jnp.float32) + fast).astype(out_ref.dtype)

        return carry

    lax.fori_loop(0, group, piece, 0)


def first_rows(info, weights, asked, cuts, parts):
    group = len(asked)
    _, tok, width = asked[0].shape
    operands = [*asked, *parts]
    whole = pltpu.VMEM((group, tok, width), jnp.bfloat16)
    return pl.pallas_call(
        functools.partial(first_kernel, group, tok, cuts),
        out_shape=jax.ShapeDtypeStruct((group, tok, width), jnp.bfloat16),
        in_specs=[SMEM, ANY] + [ANY] * len(operands),
        out_specs=VMEM,
        scratch_shapes=[
            pltpu.VMEM(weights.shape, jnp.bfloat16),
            whole,
            whole,
            whole,
            pltpu.VMEM((2, group, 8, tok), jnp.float32),
            pltpu.SemaphoreType.DMA((len(operands) + 1,)),
        ],
        compiler_params=params(60),
        name="first_rows",
    )(info, weights, *operands)


def finish_kernel(group, tok, count, chunks, info_ref, place_ref, base_any, *refs):
    out_ref, wbuf, qbuf, bbuf, sems = refs[-5:]
    plane, member, first_len = info_ref[0], info_ref[1], info_ref[2]

    def base_copy(d):
        return pltpu.make_async_copy(base_any.at[d], bbuf.at[d], sems.at[group + chunks + d])

    moves = [(refs[d], qbuf.at[pl.ds(d, 1)]) for d in range(group)]
    rows = wbuf.shape[1] // chunks
    for n in range(chunks):
        at = pl.multiple_of((plane + chunks - n) % chunks * rows, rows)
        moves.append((refs[group + n], wbuf.at[:, pl.ds(at, rows), :]))
    copies = [pltpu.make_async_copy(*move, sems.at[n]) for n, move in enumerate(moves)]
    for copy in copies:
        copy.start()
    for d in range(group):
        base_copy(d).start()
    for copy in copies:
        copy.wait()
    seg = tok // count

    def piece(d, carry):
        at = member ^ d
        first_tok = (plane * group + at) * tok
        base_copy(d).wait()

        @pl.when(first_tok + tok > first_len)
        def _():
            token = first_tok + lax.broadcasted_iota(jnp.int32, (tok, 1), 0)
            fast = jnp.where(token < first_len, 0.0, fast_apply(qbuf[d], wbuf))
            bbuf[d] = (bbuf[d].astype(jnp.float32) + fast).astype(bbuf.dtype)

        pick = as_column(place_ref[at]).astype(jnp.int32)
        pick = (pick == lax.broadcasted_iota(jnp.int32, (tok, tok), 1)).astype(jnp.bfloat16)
        sorted_rows = dot(pick, bbuf[d], NN)
        sorted_rows = sorted_rows.reshape(count, seg, sorted_rows.shape[-1])
        out_ref[:, at] = sorted_rows.astype(out_ref.dtype)
        return carry

    lax.fori_loop(0, group, piece, 0)


def finish_rows(info, places, new, base, asked, count):
    group = len(asked)
    _, tok, width = asked[0].shape
    whole = pltpu.VMEM((group, tok, width), jnp.bfloat16)
    return pl.pallas_call(
        functools.partial(finish_kernel, group, tok, count, len(new)),
        out_shape=jax.ShapeDtypeStruct((count, group, tok // count, width), jnp.bfloat16),
        in_specs=[SMEM, VMEM, ANY] + [ANY] * (group + len(new)),
        out_specs=VMEM,
        scratch_shapes=[
            pltpu.VMEM((3, new[0].shape[1] * len(new), width), jnp.bfloat16),
            whole,
            whole,
            pltpu.SemaphoreType.DMA((2 * group + len(new),)),
        ],
        compiler_params=params(60),
        name="finish_rows",
    )(info, places, base, *asked, *new)


def norm_kernel(came_ref, scale_ref, gain_ref, out_ref):
    scaled = came_ref[0].astype(jnp.float32) * scale_ref[...] * gain_ref[...]
    out_ref[...] = jnp.swapaxes(scaled.astype(out_ref.dtype), 0, 1)


def norm_rows(came, scale, gain):
    planes, group, rows, width = came.shape
    return pl.pallas_call(
        norm_kernel,
        grid=(planes,),
        out_shape=jax.ShapeDtypeStruct((planes * rows, group, width), jnp.bfloat16),
        in_specs=[
            pl.BlockSpec((1, group, rows, width), lambda z: (z, 0, 0, 0)),
            pl.BlockSpec((1, rows, 1), lambda z: (z, 0, 0)),
            pl.BlockSpec((group, 1, width), lambda z: (0, 0, 0)),
        ],
        out_specs=pl.BlockSpec((rows, group, width), lambda z: (z, 0, 0)),
        compiler_params=params(20),
        name="norm_rows",
    )(came, scale, gain)


def pass_kernel(count, *refs):
    for n in range(count):
        refs[len(refs) - count + n][...] = refs[n][...]


def pass_after(values, after):
    return pl.pallas_call(
        functools.partial(pass_kernel, len(values)),
        out_shape=[jax.ShapeDtypeStruct(value.shape, value.dtype) for value in values],
        in_specs=[VMEM] * len(values) + [ANY] * len(after),
        out_specs=[VMEM] * len(values),
        compiler_params=params(20),
        name="pass_after",
    )(*values, *after)


def as_places(asked, group, tok):
    places = jnp.transpose(asked, (1, 0, 2)).reshape(group, 1, tok).astype(jnp.float32)
    return jnp.broadcast_to(places, (group, 8, tok))


def asked_places(slot_order, group, count):
    tok = slot_order.shape[0]
    seg, planes = tok // count, count // group
    wanted = (slot_order % tok).reshape(planes, 1, group * seg)
    wanted = jnp.broadcast_to(wanted, (planes, group, group * seg))
    wanted = wanted.reshape(count, group * seg)
    asked = lax.all_to_all(wanted, "seq", split_axis=0, concat_axis=0, tiled=True)
    return as_places(asked.reshape(count, group, seg), group, tok)


def per_device(
    queries, token_keys, token_values, fast_weights, learn_rate, out_gain, group_lengths, slot_order
):
    tok, group, width = queries.shape
    count = lax.axis_size("seq")
    seg = tok // count
    planes = count // group
    behind = WINDOW // (group * tok)
    position = lax.axis_index("seq")
    plane, member = position // group, position % group
    info = jnp.stack([plane, member, group_lengths[0]]).astype(jnp.int32)

    weights = lax.dynamic_index_in_dim(fast_weights, member, 1, keepdims=False)
    weights = jnp.transpose(weights, (1, 0, 2))
    rate = lax.dynamic_slice_in_dim(learn_rate, member, 1)
    places = asked_places(slot_order, group, count)

    last = group - 1
    mine = split_heads(info, [token_keys, token_values])
    pairs = list(mine)
    if last:
        pairs = trade(pairs[:last], count)
        (late,) = pass_after(mine[last:], [*pairs[1:], weights, places])
        pairs = pairs + [lax.ppermute(late, "seq", swap_pairs(count, last))]
    carried = [weight_sums(info, weights, pairs, 0, last)[0]] if last else []
    asked = trade(split_heads(info, [queries], carried), count)
    shifts = [back * group for back in range(behind, 0, -1)]
    sources = [plane_pairs(count, shift) for shift in shifts]
    near = [[lax.ppermute(pair, "seq", source) for pair in pairs[:last]] for source in sources]
    waits = [asked[0], *near[-1][:2]]
    direct = planes <= 8
    chunks = planes if direct else 1
    *sums, onward = weight_sums(info, weights, pairs, last, group, carried, waits, chunks)
    earlier = []
    for source, arrays in zip(sources, near):
        earlier.extend(arrays + [lax.ppermute(onward, "seq", source)])

    groups = [[z * group + m for z in range(planes)] for m in range(group)]
    cuts = [(0, group)]
    parts = list(own_attention(info, asked, pairs, 0, group))

    def turned(value, steps):
        pairs_of_turn = [(index, (index + steps * group) % count) for index in range(count)]
        return lax.ppermute(value, "seq", pairs_of_turn)

    if direct:
        sums = sums[:1] + [turned(sums[step], step) for step in range(1, planes)]
    else:
        sums = [
            lax.psum_scatter(
                sums[0], "seq", scatter_dimension=1, axis_index_groups=groups, tiled=True
            )
        ]
    part = renorm(info, rate, weights, sums, parts[1:] + earlier[min(2, last) :])
    if direct:
        new = [part] + [turned(part, step) for step in range(1, planes)]
    else:
        new = [lax.all_gather(part, "seq", axis_index_groups=groups, axis=1, tiled=True)]
    parts.extend(cross_attention(info, asked, earlier, [part]))
    base = first_rows(info, weights, asked, cuts, parts)
    leaving = finish_rows(info, places, new, base, asked, count)

    came = lax.all_to_all(leaving, "seq", split_axis=0, concat_axis=0, tiled=True)
    came = came.reshape(planes, group, group * seg, width)
    wide = came.astype(jnp.float32)
    power = lax.psum(jnp.sum(wide * wide, axis=(1, 3)), "head")
    scale = lax.rsqrt(power / (group * lax.axis_size("head") * width) + eps)
    return norm_rows(came, scale[:, :, None], out_gain[:, None, :])


def solution(mesh):
    return jax.shard_map(
        per_device,
        mesh=mesh,
        in_specs=(
            P("seq", "head", None),
            P("seq", "head", None),
            P("seq", "head", None),
            P(None, "head", None, None),
            P("head"),
            P("head", None),
            P(),
            P("seq"),
        ),
        out_specs=P("seq", "head", None),
        check_vma=False,
    )
```

```python
import functools
import math

import jax
import jax.numpy as jnp
from jax import lax
from jax.experimental import pallas as pl
from jax.experimental.pallas import tpu as pltpu
from jax.sharding import PartitionSpec as P

WINDOW = 2048
NEG = -1e30
MIB = 1024 * 1024

eps = 1e-06

NT = (((1,), (1,)), ((), ()))
TN = (((0,), (0,)), ((), ()))
NN = (((1,), (0,)), ((), ()))

ANY = pl.BlockSpec(memory_space=pl.ANY)
SMEM = pl.BlockSpec(memory_space=pltpu.SMEM)
VMEM = pl.BlockSpec(memory_space=pltpu.VMEM)


def dot(left, right, dims):
    return lax.dot_general(left, right, dims, preferred_element_type=jnp.float32)


def params(mib):
    return pltpu.CompilerParams(vmem_limit_bytes=mib * MIB)


def swap_pairs(count, distance):
    return [(index, index ^ distance) for index in range(count)]


def plane_pairs(count, steps):
    return [(index, index + steps) for index in range(count - steps)]


def run(copies):
    for copy in copies:
        copy.start()
    for copy in copies:
        copy.wait()


def split_kernel(group, total, info_ref, *refs):
    x_any, outs = refs[:total], refs[-4 - group : -4]
    held, buf, in_sems, sems = refs[-4:]
    member = info_ref[1]
    loads = [pltpu.make_async_copy(x_any[t], held.at[t], in_sems.at[t]) for t in range(total)]
    for load in loads:
        load.start()
    copies = []
    for t in range(total):
        loads[t].wait()
        buf[:, t] = jnp.swapaxes(held[t], 0, 1)
        for d in range(group):
            source = buf.at[member ^ d, t]
            copies.append(pltpu.make_async_copy(source, outs[d].at[t], sems.at[t, d]))
            copies[-1].start()
    for copy in copies:
        copy.wait()


def split_heads(info, arrays, after=()):
    tok, group, width = arrays[0].shape
    total = len(arrays)
    return pl.pallas_call(
        functools.partial(split_kernel, group, total),
        out_shape=[jax.ShapeDtypeStruct((total, tok, width), jnp.bfloat16)] * group,
        in_specs=[SMEM] + [ANY] * (total + len(after)),
        out_specs=[ANY] * group,
        scratch_shapes=[
            pltpu.VMEM((total, tok, group, width), jnp.bfloat16),
            pltpu.VMEM((group, total, tok, width), jnp.bfloat16),
            pltpu.SemaphoreType.DMA((total,)),
            pltpu.SemaphoreType.DMA((total, group)),
        ],
        compiler_params=params(60),
        name="split_heads",
    )(info, *arrays, *after)


def trade(pieces, count):
    return [
        lax.ppermute(piece, "seq", swap_pairs(count, d)) if d else piece
        for d, piece in enumerate(pieces)
    ]


def grad_kernel(group, tok, first, last, carried, chunks, info_ref, w_ref, *refs):
    pieces = last - first
    piece_any, refs = refs[:pieces], refs[pieces:]
    kvbuf, acc, sems = refs[-3:]
    *outs, last_piece = refs[-4 - chunks : -3] if last == group else (refs[-4], None)
    onward = [last_piece] if last == group else []
    plane, member, first_len = info_ref[0], info_ref[1], info_ref[2]
    copies = [
        pltpu.make_async_copy(piece_any[n], kvbuf.at[n], sems.at[n]) for n in range(pieces)
    ]
    if carried:
        copies.append(pltpu.make_async_copy(refs[0], acc, sems.at[pieces]))
    run(copies)
    leaving = [pltpu.make_async_copy(kvbuf.at[pieces - 1], to, sems.at[0]) for to in onward]
    for copy in leaving:
        copy.start()
    if not carried:
        acc[...] = jnp.zeros_like(acc)
    hidden = w_ref.shape[1]
    part = min(256, hidden)

    def piece(n, carry):
        first_tok = (plane * group + (member ^ (first + n))) * tok

        @pl.when(first_tok < first_len)
        def _():
            keys = kvbuf[n, 0]
            token = first_tok + lax.broadcasted_iota(jnp.int32, (tok, 1), 0)
            values = jnp.where(token < first_len, kvbuf[n, 1].astype(jnp.float32), 0.0)
            values = values.astype(jnp.bfloat16)
            for f in range(0, hidden, part):
                rows = pl.ds(f, part)
                gate = dot(keys, w_ref[0, rows, :], NT)
                up = dot(keys, w_ref[1, rows, :], NT)
                back = dot(values, w_ref[2, rows, :], NT)
                sig = jax.nn.sigmoid(gate)
                silu = gate * sig
                act = (silu * up).astype(jnp.bfloat16)
                grad_up = (back * silu).astype(jnp.bfloat16)
                grad_gate = (back * up * sig * (1.0 + gate * (1.0 - sig))).astype(jnp.bfloat16)
                acc[0, rows, :] += dot(grad_gate, keys, TN)
                acc[1, rows, :] += dot(grad_up, keys, TN)
                acc[2, rows, :] += dot(act, values, TN)

        return carry

    lax.fori_loop(0, pieces, piece, 0)
    rows = hidden // chunks
    for n, out in enumerate(outs):
        at = pl.multiple_of((plane + n) % chunks * rows, rows)
        out[...] = acc[:, pl.ds(at, rows), :].astype(out.dtype)
    for copy in leaving:
        copy.wait()


def weight_sums(info, weights, pairs, first, last, carried=(), after=(), chunks=1):
    group = len(pairs)
    pieces = last - first
    kind = jnp.bfloat16 if last == group else jnp.float32
    return pl.pallas_call(
        functools.partial(grad_kernel, group, pairs[0].shape[1], first, last, len(carried), chunks),
        out_shape=[jax.ShapeDtypeStruct((3, weights.shape[1] // chunks, weights.shape[2]), kind)] * chunks
        + [jax.ShapeDtypeStruct(pairs[0].shape, jnp.bfloat16)] * (last == group),
        in_specs=[SMEM, VMEM] + [ANY] * (pieces + len(carried) + len(after)),
        out_specs=[VMEM] * chunks + [ANY] * (last == group),
        scratch_shapes=[
            pltpu.VMEM((pieces,) + pairs[0].shape, jnp.bfloat16),
            pltpu.VMEM(weights.shape, jnp.float32),
            pltpu.SemaphoreType.DMA((pieces + 1,)),
        ],
        compiler_params=params(60),
        name="weight_sums",
    )(info, weights, *pairs[first:last], *carried, *after)


def lanes_sum(expo):
    total = expo[:, :128]
    for lane in range(128, expo.shape[1], 128):
        total = total + expo[:, lane : lane + 128]
    return total


def soft_steps(parts, scale, fresh, acc, top, norm):
    scores = [
        dot(rows, keys, NT) if mask is None else jnp.where(mask, dot(rows, keys, NT), NEG)
        for _, rows, keys, _, mask in parts
    ]
    done = []
    for (where, _, _, _, _), score in zip(parts, scores):
        peak = jnp.max(score, axis=1, keepdims=True)
        if fresh:
            decay = None
        else:
            before = top[where, :1]
            peak = jnp.maximum(peak, before)
            decay = jnp.exp2((before - peak) * scale)
        expo = jnp.exp2((score - peak) * scale)
        done.append((peak, decay, lanes_sum(expo), expo.astype(jnp.bfloat16)))
    for (where, _, _, values, _), (peak, decay, total, expo) in zip(parts, done):
        mixed = dot(expo, values, NN)
        wide = (peak.shape[0], 128)
        top[where, :] = jnp.broadcast_to(peak, wide)
        if fresh:
            norm[where, :] = total
            acc[where, :] = mixed
        else:
            norm[where, :] = norm[where, :] * decay + total
            acc[where, :] = acc[where, :] * decay + mixed


def soft_close(scale, acc, top, norm, out_ref, level_ref):
    total = jnp.sum(norm[...], axis=1, keepdims=True)
    out_ref[...] = (acc[...] / jnp.maximum(total, 1e-30)).astype(out_ref.dtype)
    level = top[...] * scale + jnp.log2(jnp.maximum(total, 1e-30))
    level_ref[...] = jnp.transpose(level)[:8]


def as_column(rows):
    return jnp.transpose(jnp.concatenate([rows] * 16, axis=0))[:, :1]


def score_scale(width):
    return math.log2(math.e) / math.sqrt(width)


def triangle(rows, cols, first_row, first_col, lower):
    row = first_row + lax.broadcasted_iota(jnp.int32, (rows, cols), 0)
    col = first_col + lax.broadcasted_iota(jnp.int32, (rows, cols), 1)
    return col <= row if lower else col > row


def own_kernel(group, tok, part, first, last, info_ref, *refs):
    count = last - first
    out_ref, level_ref, acc, top, norm, qbuf, kvbuf, sems = refs[-8:]
    member = info_ref[1]
    copies = [
        pltpu.make_async_copy(refs[n], qbuf.at[pl.ds(n, 1)], sems.at[n]) for n in range(count)
    ]
    for d in range(group):
        copies.append(pltpu.make_async_copy(refs[count + d], kvbuf.at[d], sems.at[count + d]))
    run(copies)
    scale = score_scale(qbuf.shape[-1])

    def piece(n, carry):
        d = first + n
        parts = []
        for r in range(0, tok, part):
            where, keys = pl.ds(r, part), pl.ds(0, r + part)
            mask = triangle(part, r + part, r, 0, True)
            parts.append((where, qbuf[n, where], kvbuf[d, 0, keys], kvbuf[d, 1, keys], mask))
        soft_steps(parts, scale, True, acc, top, norm)

        def earlier(other, carry):
            e = member ^ other
            parts = []
            for r in range(0, tok, part):
                where = pl.ds(r, part)
                parts.append((where, qbuf[n, where], kvbuf[e, 0], kvbuf[e, 1], None))
            soft_steps(parts, scale, False, acc, top, norm)
            return carry

        lax.fori_loop(0, member ^ d, earlier, 0)
        soft_close(scale, acc, top, norm, out_ref.at[n], level_ref.at[n])
        return carry

    lax.fori_loop(0, count, piece, 0)


def soft_shapes(group, tok, width):
    return [
        jax.ShapeDtypeStruct((group, tok, width), jnp.bfloat16),
        jax.ShapeDtypeStruct((group, 8, tok), jnp.float32),
    ]


def soft_scratch(tok, width):
    return [
        pltpu.VMEM((tok, width), jnp.float32),
        pltpu.VMEM((tok, 128), jnp.float32),
        pltpu.VMEM((tok, 128), jnp.float32),
    ]


def own_attention(info, asked, pairs, first, last, after=()):
    group = len(asked)
    _, tok, width = asked[0].shape
    count = last - first
    return pl.pallas_call(
        functools.partial(own_kernel, group, tok, min(256, tok), first, last),
        out_shape=soft_shapes(count, tok, width),
        in_specs=[SMEM] + [ANY] * (count + group + len(after)),
        out_specs=[VMEM] * 2,
        scratch_shapes=soft_scratch(tok, width)
        + [
            pltpu.VMEM((count, tok, width), jnp.bfloat16),
            pltpu.VMEM((group, 2, tok, width), jnp.bfloat16),
            pltpu.SemaphoreType.DMA((count + group,)),
        ],
        compiler_params=params(60),
        name="own_attention",
    )(info, *asked[first:last], *pairs, *after)


def renorm_kernel(terms, info_ref, rate_ref, w_ref, *refs):
    out_ref = refs[-1]
    rows = out_ref.shape[1]
    mine = pl.ds(pl.multiple_of(info_ref[0] * rows, rows), rows)
    step = rate_ref[0] / info_ref[2].astype(jnp.float32)
    for c in range(w_ref.shape[0]):
        previous = w_ref[c, mine, :].astype(jnp.float32)
        summed = refs[0][c].astype(jnp.float32)
        for term in refs[1:terms]:
            summed = summed + term[c].astype(jnp.float32)
        updated = previous + step * summed
        old_norm = jnp.sqrt(jnp.sum(previous * previous, axis=1, keepdims=True) + eps)
        new_norm = jnp.sqrt(jnp.sum(updated * updated, axis=1, keepdims=True) + eps)
        out_ref[c] = (updated * (old_norm / new_norm)).astype(out_ref.dtype)


def renorm(info, rate, weights, sums, after=()):
    return pl.pallas_call(
        functools.partial(renorm_kernel, len(sums)),
        out_shape=jax.ShapeDtypeStruct(sums[0].shape, jnp.bfloat16),
        in_specs=[SMEM] * 2 + [VMEM] * (1 + len(sums)) + [ANY] * len(after),
        out_specs=VMEM,
        compiler_params=params(60),
        name="renorm",
    )(info, rate, weights, *sums, *after)


def cross_kernel(group, tok, behind, part, info_ref, *refs):
    pieces = behind * group
    out_ref, level_ref, acc, top, norm, qbuf, kvbuf, sems = refs[-8:]
    plane, member = info_ref[0], info_ref[1]
    moves = [(refs[d], qbuf.at[pl.ds(d, 1)]) for d in range(group)]
    moves += [(refs[group + at], kvbuf.at[at]) for at in range(pieces)]
    run([pltpu.make_async_copy(*move, sems.at[n]) for n, move in enumerate(moves)])
    scale = score_scale(qbuf.shape[-1])
    valid = jnp.maximum(behind - plane, 0) * group

    def piece(d, carry):
        at = member ^ d

        @pl.when(at >= valid)
        def _():
            parts = []
            for r in range(0, tok, part):
                where, keys = pl.ds(r, part), pl.ds(r, tok - r)
                mask = triangle(part, tok - r, r, r, False)
                parts.append((where, qbuf[d, where], kvbuf[d, 0, keys], kvbuf[d, 1, keys], mask))
            soft_steps(parts, scale, True, acc, top, norm)

        @pl.when(at < valid)
        def _():
            acc[...] = jnp.zeros_like(acc)
            norm[...] = jnp.zeros_like(norm)
            top[...] = jnp.full_like(top, NEG)

        def later(other, carry):
            e = other // group * group + (member ^ (other % group))
            parts = []
            for r in range(0, tok, part):
                where = pl.ds(r, part)
                parts.append((where, qbuf[d, where], kvbuf[e, 0], kvbuf[e, 1], None))
            soft_steps(parts, scale, False, acc, top, norm)
            return carry

        lax.fori_loop(jnp.maximum(at + 1, valid), pieces, later, 0)
        soft_close(scale, acc, top, norm, out_ref.at[d], level_ref.at[d])
        return carry

    lax.fori_loop(0, group, piece, 0)


def cross_attention(info, asked, earlier, after=()):
    group = len(asked)
    _, tok, width = asked[0].shape
    behind = len(earlier) // group
    operands = [*asked, *earlier, *after]
    return pl.pallas_call(
        functools.partial(cross_kernel, group, tok, behind, min(256, tok)),
        out_shape=soft_shapes(group, tok, width),
        in_specs=[SMEM] + [ANY] * len(operands),
        out_specs=[VMEM] * 2,
        scratch_shapes=soft_scratch(tok, width)
        + [
            pltpu.VMEM((group, tok, width), jnp.bfloat16),
            pltpu.VMEM((behind * group, 2, tok, width), jnp.bfloat16),
            pltpu.SemaphoreType.DMA((group + behind * group,)),
        ],
        compiler_params=params(60),
        name="cross_attention",
    )(info, *operands)


def fast_apply(rows, weights):
    gate = dot(rows, weights[0], NT)
    up = dot(rows, weights[1], NT)
    act = (gate * jax.nn.sigmoid(gate) * up).astype(jnp.bfloat16)
    return dot(act, weights[2], NN)


def first_kernel(group, tok, cuts, info_ref, w_any, *refs):
    out_ref, wbuf, qbuf, obuf, xbuf, lbuf, sems = refs[-7:]
    plane, member, first_len = info_ref[0], info_ref[1], info_ref[2]
    moves = [(w_any, wbuf)] + [(refs[d], qbuf.at[pl.ds(d, 1)]) for d in range(group)]
    for n, (first, last) in enumerate(cuts):
        into = pl.ds(first, last - first)
        rows, level = refs[group + 2 * n], refs[group + 2 * n + 1]
        moves += [(rows, obuf.at[into]), (level, lbuf.at[0, into])]
    rows, level = refs[group + 2 * len(cuts)], refs[group + 2 * len(cuts) + 1]
    moves += [(rows, xbuf), (level, lbuf.at[1])]
    run([pltpu.make_async_copy(*move, sems.at[n]) for n, move in enumerate(moves)])

    def piece(d, carry):
        first_tok = (plane * group + (member ^ d)) * tok
        own_log, cross_log = as_column(lbuf[0, d]), as_column(lbuf[1, d])
        own_part = 1.0 / (1.0 + jnp.exp2(cross_log - own_log))
        cross_part = 1.0 / (1.0 + jnp.exp2(own_log - cross_log))
        mixed = obuf[d].astype(jnp.float32) * own_part + xbuf[d].astype(jnp.float32) * cross_part
        out_ref[d] = mixed.astype(out_ref.dtype)

        @pl.when(first_tok < first_len)
        def _():
            token = first_tok + lax.broadcasted_iota(jnp.int32, (tok, 1), 0)
            fast = jnp.where(token < first_len, fast_apply(qbuf[d], wbuf), 0.0)
            out_ref[d] = (out_ref[d].astype(jnp.float32) + fast).astype(out_ref.dtype)

        return carry

    lax.fori_loop(0, group, piece, 0)


def first_rows(info, weights, asked, cuts, parts):
    group = len(asked)
    _, tok, width = asked[0].shape
    operands = [*asked, *parts]
    whole = pltpu.VMEM((group, tok, width), jnp.bfloat16)
    return pl.pallas_call(
        functools.partial(first_kernel, group, tok, cuts),
        out_shape=jax.ShapeDtypeStruct((group, tok, width), jnp.bfloat16),
        in_specs=[SMEM, ANY] + [ANY] * len(operands),
        out_specs=VMEM,
        scratch_shapes=[
            pltpu.VMEM(weights.shape, jnp.bfloat16),
            whole,
            whole,
            whole,
            pltpu.VMEM((2, group, 8, tok), jnp.float32),
            pltpu.SemaphoreType.DMA((len(operands) + 1,)),
        ],
        compiler_params=params(60),
        name="first_rows",
    )(info, weights, *operands)


def finish_kernel(group, tok, count, chunks, info_ref, place_ref, base_any, *refs):
    out_ref, wbuf, qbuf, bbuf, sems = refs[-5:]
    plane, member, first_len = info_ref[0], info_ref[1], info_ref[2]

    def base_copy(d):
        return pltpu.make_async_copy(base_any.at[d], bbuf.at[d], sems.at[group + chunks + d])

    moves = [(refs[d], qbuf.at[pl.ds(d, 1)]) for d in range(group)]
    rows = wbuf.shape[1] // chunks
    for n in range(chunks):
        at = pl.multiple_of((plane + chunks - n) % chunks * rows, rows)
        moves.append((refs[group + n], wbuf.at[:, pl.ds(at, rows), :]))
    copies = [pltpu.make_async_copy(*move, sems.at[n]) for n, move in enumerate(moves)]
    for copy in copies:
        copy.start()
    for d in range(group):
        base_copy(d).start()
    for copy in copies:
        copy.wait()
    seg = tok // count

    def piece(d, carry):
        at = member ^ d
        first_tok = (plane * group + at) * tok
        base_copy(d).wait()

        @pl.when(first_tok + tok > first_len)
        def _():
            token = first_tok + lax.broadcasted_iota(jnp.int32, (tok, 1), 0)
            fast = jnp.where(token < first_len, 0.0, fast_apply(qbuf[d], wbuf))
            bbuf[d] = (bbuf[d].astype(jnp.float32) + fast).astype(bbuf.dtype)

        pick = as_column(place_ref[at]).astype(jnp.int32)
        pick = (pick == lax.broadcasted_iota(jnp.int32, (tok, tok), 1)).astype(jnp.bfloat16)
        sorted_rows = dot(pick, bbuf[d], NN)
        sorted_rows = sorted_rows.reshape(count, seg, sorted_rows.shape[-1])
        out_ref[:, at] = sorted_rows.astype(out_ref.dtype)
        return carry

    lax.fori_loop(0, group, piece, 0)


def finish_rows(info, places, new, base, asked, count):
    group = len(asked)
    _, tok, width = asked[0].shape
    whole = pltpu.VMEM((group, tok, width), jnp.bfloat16)
    return pl.pallas_call(
        functools.partial(finish_kernel, group, tok, count, len(new)),
        out_shape=jax.ShapeDtypeStruct((count, group, tok // count, width), jnp.bfloat16),
        in_specs=[SMEM, VMEM, ANY] + [ANY] * (group + len(new)),
        out_specs=VMEM,
        scratch_shapes=[
            pltpu.VMEM((3, new[0].shape[1] * len(new), width), jnp.bfloat16),
            whole,
            whole,
            pltpu.SemaphoreType.DMA((2 * group + len(new),)),
        ],
        compiler_params=params(60),
        name="finish_rows",
    )(info, places, base, *asked, *new)


def norm_kernel(came_ref, scale_ref, gain_ref, out_ref):
    scaled = came_ref[0].astype(jnp.float32) * scale_ref[...] * gain_ref[...]
    out_ref[...] = jnp.swapaxes(scaled.astype(out_ref.dtype), 0, 1)


def norm_rows(came, scale, gain):
    planes, group, rows, width = came.shape
    return pl.pallas_call(
        norm_kernel,
        grid=(planes,),
        out_shape=jax.ShapeDtypeStruct((planes * rows, group, width), jnp.bfloat16),
        in_specs=[
            pl.BlockSpec((1, group, rows, width), lambda z: (z, 0, 0, 0)),
            pl.BlockSpec((1, rows, 1), lambda z: (z, 0, 0)),
            pl.BlockSpec((group, 1, width), lambda z: (0, 0, 0)),
        ],
        out_specs=pl.BlockSpec((rows, group, width), lambda z: (z, 0, 0)),
        compiler_params=params(20),
        name="norm_rows",
    )(came, scale, gain)


def pass_kernel(count, *refs):
    for n in range(count):
        refs[len(refs) - count + n][...] = refs[n][...]


def pass_after(values, after):
    return pl.pallas_call(
        functools.partial(pass_kernel, len(values)),
        out_shape=[jax.ShapeDtypeStruct(value.shape, value.dtype) for value in values],
        in_specs=[VMEM] * len(values) + [ANY] * len(after),
        out_specs=[VMEM] * len(values),
        compiler_params=params(20),
        name="pass_after",
    )(*values, *after)


def as_places(asked, group, tok):
    places = jnp.transpose(asked, (1, 0, 2)).reshape(group, 1, tok).astype(jnp.float32)
    return jnp.broadcast_to(places, (group, 8, tok))


def asked_places(slot_order, group, count):
    tok = slot_order.shape[0]
    seg, planes = tok // count, count // group
    wanted = (slot_order % tok).reshape(planes, 1, group * seg)
    wanted = jnp.broadcast_to(wanted, (planes, group, group * seg))
    wanted = wanted.reshape(count, group * seg)
    asked = lax.all_to_all(wanted, "seq", split_axis=0, concat_axis=0, tiled=True)
    return as_places(asked.reshape(count, group, seg), group, tok)


def per_device(
    queries, token_keys, token_values, fast_weights, learn_rate, out_gain, group_lengths, slot_order
):
    tok, group, width = queries.shape
    count = lax.axis_size("seq")
    seg = tok // count
    planes = count // group
    behind = WINDOW // (group * tok)
    position = lax.axis_index("seq")
    plane, member = position // group, position % group
    info = jnp.stack([plane, member, group_lengths[0]]).astype(jnp.int32)

    weights = lax.dynamic_index_in_dim(fast_weights, member, 1, keepdims=False)
    weights = jnp.transpose(weights, (1, 0, 2))
    rate = lax.dynamic_slice_in_dim(learn_rate, member, 1)
    places = asked_places(slot_order, group, count)

    last = group - 1
    mine = split_heads(info, [token_keys, token_values])
    pairs = list(mine)
    if last:
        pairs = trade(pairs[:last], count)
        (late,) = pass_after(mine[last:], [*pairs[1:], weights, places])
        pairs = pairs + [lax.ppermute(late, "seq", swap_pairs(count, last))]
    carried = [weight_sums(info, weights, pairs, 0, last)[0]] if last else []
    asked = trade(split_heads(info, [queries], carried), count)
    shifts = [back * group for back in range(behind, 0, -1)]
    sources = [plane_pairs(count, shift) for shift in shifts]
    near = [[lax.ppermute(pair, "seq", source) for pair in pairs[:last]] for source in sources]
    waits = [*asked[:3], *near[-1][:2]]
    direct = planes <= 8
    chunks = planes if direct else 1
    *sums, onward = weight_sums(info, weights, pairs, last, group, carried, waits, chunks)
    earlier = []
    for source, arrays in zip(sources, near):
        earlier.extend(arrays + [lax.ppermute(onward, "seq", source)])

    groups = [[z * group + m for z in range(planes)] for m in range(group)]
    cuts = [(0, group)]
    parts = list(own_attention(info, asked, pairs, 0, group))

    def turned(value, steps):
        pairs_of_turn = [(index, (index + steps * group) % count) for index in range(count)]
        return lax.ppermute(value, "seq", pairs_of_turn)

    if direct:
        sums = sums[:1] + [turned(sums[step], step) for step in range(1, planes)]
    else:
        sums = [
            lax.psum_scatter(
                sums[0], "seq", scatter_dimension=1, axis_index_groups=groups, tiled=True
            )
        ]
    part = renorm(info, rate, weights, sums, parts[1:] + earlier[min(2, last) :])
    if direct:
        new = [part] + [turned(part, step) for step in range(1, planes)]
    else:
        new = [lax.all_gather(part, "seq", axis_index_groups=groups, axis=1, tiled=True)]
    parts.extend(cross_attention(info, asked, earlier, [part]))
    base = first_rows(info, weights, asked, cuts, parts)
    leaving = finish_rows(info, places, new, base, asked, count)

    came = lax.all_to_all(leaving, "seq", split_axis=0, concat_axis=0, tiled=True)
    came = came.reshape(planes, group, group * seg, width)
    wide = came.astype(jnp.float32)
    power = lax.psum(jnp.sum(wide * wide, axis=(1, 3)), "head")
    scale = lax.rsqrt(power / (group * lax.axis_size("head") * width) + eps)
    return norm_rows(came, scale[:, :, None], out_gain[:, None, :])


def solution(mesh):
    return jax.shard_map(
        per_device,
        mesh=mesh,
        in_specs=(
            P("seq", "head", None),
            P("seq", "head", None),
            P("seq", "head", None),
            P(None, "head", None, None),
            P("head"),
            P("head", None),
            P(),
            P("seq"),
        ),
        out_specs=P("seq", "head", None),
        check_vma=False,
    )
```

```python
import functools
import math

import jax
import jax.numpy as jnp
from jax import lax
from jax.experimental import pallas as pl
from jax.experimental.pallas import tpu as pltpu
from jax.sharding import PartitionSpec as P

WINDOW = 2048
NEG = -1e30
MIB = 1024 * 1024

eps = 1e-06

NT = (((1,), (1,)), ((), ()))
TN = (((0,), (0,)), ((), ()))
NN = (((1,), (0,)), ((), ()))

ANY = pl.BlockSpec(memory_space=pl.ANY)
SMEM = pl.BlockSpec(memory_space=pltpu.SMEM)
VMEM = pl.BlockSpec(memory_space=pltpu.VMEM)


def dot(left, right, dims):
    return lax.dot_general(left, right, dims, preferred_element_type=jnp.float32)


def params(mib):
    return pltpu.CompilerParams(vmem_limit_bytes=mib * MIB)


def swap_pairs(count, distance):
    return [(index, index ^ distance) for index in range(count)]


def plane_pairs(count, steps):
    return [(index, index + steps) for index in range(count - steps)]


def run(copies):
    for copy in copies:
        copy.start()
    for copy in copies:
        copy.wait()


def split_kernel(group, total, info_ref, *refs):
    x_any, outs = refs[:total], refs[-4 - group : -4]
    held, buf, in_sems, sems = refs[-4:]
    member = info_ref[1]
    loads = [pltpu.make_async_copy(x_any[t], held.at[t], in_sems.at[t]) for t in range(total)]
    for load in loads:
        load.start()
    copies = []
    for t in range(total):
        loads[t].wait()
        buf[:, t] = jnp.swapaxes(held[t], 0, 1)
        for d in range(group):
            source = buf.at[member ^ d, t]
            copies.append(pltpu.make_async_copy(source, outs[d].at[t], sems.at[t, d]))
            copies[-1].start()
    for copy in copies:
        copy.wait()


def split_heads(info, arrays, after=()):
    tok, group, width = arrays[0].shape
    total = len(arrays)
    return pl.pallas_call(
        functools.partial(split_kernel, group, total),
        out_shape=[jax.ShapeDtypeStruct((total, tok, width), jnp.bfloat16)] * group,
        in_specs=[SMEM] + [ANY] * (total + len(after)),
        out_specs=[ANY] * group,
        scratch_shapes=[
            pltpu.VMEM((total, tok, group, width), jnp.bfloat16),
            pltpu.VMEM((group, total, tok, width), jnp.bfloat16),
            pltpu.SemaphoreType.DMA((total,)),
            pltpu.SemaphoreType.DMA((total, group)),
        ],
        compiler_params=params(60),
        name="split_heads",
    )(info, *arrays, *after)


def trade(pieces, count):
    return [
        lax.ppermute(piece, "seq", swap_pairs(count, d)) if d else piece
        for d, piece in enumerate(pieces)
    ]


def grad_kernel(group, tok, first, last, carried, chunks, info_ref, w_ref, *refs):
    pieces = last - first
    piece_any, refs = refs[:pieces], refs[pieces:]
    kvbuf, acc, sems = refs[-3:]
    *outs, last_piece = refs[-4 - chunks : -3] if last == group else (refs[-4], None)
    onward = [last_piece] if last == group else []
    plane, member, first_len = info_ref[0], info_ref[1], info_ref[2]
    copies = [
        pltpu.make_async_copy(piece_any[n], kvbuf.at[n], sems.at[n]) for n in range(pieces)
    ]
    if carried:
        copies.append(pltpu.make_async_copy(refs[0], acc, sems.at[pieces]))
    run(copies)
    leaving = [pltpu.make_async_copy(kvbuf.at[pieces - 1], to, sems.at[0]) for to in onward]
    for copy in leaving:
        copy.start()
    if not carried:
        acc[...] = jnp.zeros_like(acc)
    hidden = w_ref.shape[1]
    part = min(256, hidden)

    def piece(n, carry):
        first_tok = (plane * group + (member ^ (first + n))) * tok

        @pl.when(first_tok < first_len)
        def _():
            keys = kvbuf[n, 0]
            token = first_tok + lax.broadcasted_iota(jnp.int32, (tok, 1), 0)
            values = jnp.where(token < first_len, kvbuf[n, 1].astype(jnp.float32), 0.0)
            values = values.astype(jnp.bfloat16)
            for f in range(0, hidden, part):
                rows = pl.ds(f, part)
                gate = dot(keys, w_ref[0, rows, :], NT)
                up = dot(keys, w_ref[1, rows, :], NT)
                back = dot(values, w_ref[2, rows, :], NT)
                sig = jax.nn.sigmoid(gate)
                silu = gate * sig
                act = (silu * up).astype(jnp.bfloat16)
                grad_up = (back * silu).astype(jnp.bfloat16)
                grad_gate = (back * up * sig * (1.0 + gate * (1.0 - sig))).astype(jnp.bfloat16)
                acc[0, rows, :] += dot(grad_gate, keys, TN)
                acc[1, rows, :] += dot(grad_up, keys, TN)
                acc[2, rows, :] += dot(act, values, TN)

        return carry

    lax.fori_loop(0, pieces, piece, 0)
    rows = hidden // chunks
    for n, out in enumerate(outs):
        at = pl.multiple_of((plane + n) % chunks * rows, rows)
        out[...] = acc[:, pl.ds(at, rows), :].astype(out.dtype)
    for copy in leaving:
        copy.wait()


def weight_sums(info, weights, pairs, first, last, carried=(), after=(), chunks=1):
    group = len(pairs)
    pieces = last - first
    kind = jnp.bfloat16 if last == group else jnp.float32
    return pl.pallas_call(
        functools.partial(grad_kernel, group, pairs[0].shape[1], first, last, len(carried), chunks),
        out_shape=[jax.ShapeDtypeStruct((3, weights.shape[1] // chunks, weights.shape[2]), kind)] * chunks
        + [jax.ShapeDtypeStruct(pairs[0].shape, jnp.bfloat16)] * (last == group),
        in_specs=[SMEM, VMEM] + [ANY] * (pieces + len(carried) + len(after)),
        out_specs=[VMEM] * chunks + [ANY] * (last == group),
        scratch_shapes=[
            pltpu.VMEM((pieces,) + pairs[0].shape, jnp.bfloat16),
            pltpu.VMEM(weights.shape, jnp.float32),
            pltpu.SemaphoreType.DMA((pieces + 1,)),
        ],
        compiler_params=params(60),
        name="weight_sums",
    )(info, weights, *pairs[first:last], *carried, *after)


def lanes_sum(expo):
    total = expo[:, :128]
    for lane in range(128, expo.shape[1], 128):
        total = total + expo[:, lane : lane + 128]
    return total


def soft_steps(parts, scale, fresh, acc, top, norm):
    scores = [
        dot(rows, keys, NT) if mask is None else jnp.where(mask, dot(rows, keys, NT), NEG)
        for _, rows, keys, _, mask in parts
    ]
    done = []
    for (where, _, _, _, _), score in zip(parts, scores):
        peak = jnp.max(score, axis=1, keepdims=True)
        if fresh:
            decay = None
        else:
            before = top[where, :1]
            peak = jnp.maximum(peak, before)
            decay = jnp.exp2((before - peak) * scale)
        expo = jnp.exp2((score - peak) * scale)
        done.append((peak, decay, lanes_sum(expo), expo.astype(jnp.bfloat16)))
    for (where, _, _, values, _), (peak, decay, total, expo) in zip(parts, done):
        mixed = dot(expo, values, NN)
        wide = (peak.shape[0], 128)
        top[where, :] = jnp.broadcast_to(peak, wide)
        if fresh:
            norm[where, :] = total
            acc[where, :] = mixed
        else:
            norm[where, :] = norm[where, :] * decay + total
            acc[where, :] = acc[where, :] * decay + mixed


def soft_close(scale, acc, top, norm, out_ref, level_ref):
    total = jnp.sum(norm[...], axis=1, keepdims=True)
    out_ref[...] = (acc[...] / jnp.maximum(total, 1e-30)).astype(out_ref.dtype)
    level = top[...] * scale + jnp.log2(jnp.maximum(total, 1e-30))
    level_ref[...] = jnp.transpose(level)[:8]


def as_column(rows):
    return jnp.transpose(jnp.concatenate([rows] * 16, axis=0))[:, :1]


def score_scale(width):
    return math.log2(math.e) / math.sqrt(width)


def triangle(rows, cols, first_row, first_col, lower):
    row = first_row + lax.broadcasted_iota(jnp.int32, (rows, cols), 0)
    col = first_col + lax.broadcasted_iota(jnp.int32, (rows, cols), 1)
    return col <= row if lower else col > row


def own_kernel(group, tok, part, first, last, info_ref, *refs):
    count = last - first
    out_ref, level_ref, acc, top, norm, qbuf, kvbuf, sems = refs[-8:]
    member = info_ref[1]
    copies = [
        pltpu.make_async_copy(refs[n], qbuf.at[pl.ds(n, 1)], sems.at[n]) for n in range(count)
    ]
    for d in range(group):
        copies.append(pltpu.make_async_copy(refs[count + d], kvbuf.at[d], sems.at[count + d]))
    run(copies)
    scale = score_scale(qbuf.shape[-1])

    def piece(n, carry):
        d = first + n
        parts = []
        for r in range(0, tok, part):
            where, keys = pl.ds(r, part), pl.ds(0, r + part)
            mask = triangle(part, r + part, r, 0, True)
            parts.append((where, qbuf[n, where], kvbuf[d, 0, keys], kvbuf[d, 1, keys], mask))
        soft_steps(parts, scale, True, acc, top, norm)

        def earlier(other, carry):
            e = member ^ other
            parts = []
            for r in range(0, tok, part):
                where = pl.ds(r, part)
                parts.append((where, qbuf[n, where], kvbuf[e, 0], kvbuf[e, 1], None))
            soft_steps(parts, scale, False, acc, top, norm)
            return carry

        lax.fori_loop(0, member ^ d, earlier, 0)
        soft_close(scale, acc, top, norm, out_ref.at[n], level_ref.at[n])
        return carry

    lax.fori_loop(0, count, piece, 0)


def soft_shapes(group, tok, width):
    return [
        jax.ShapeDtypeStruct((group, tok, width), jnp.bfloat16),
        jax.ShapeDtypeStruct((group, 8, tok), jnp.float32),
    ]


def soft_scratch(tok, width):
    return [
        pltpu.VMEM((tok, width), jnp.float32),
        pltpu.VMEM((tok, 128), jnp.float32),
        pltpu.VMEM((tok, 128), jnp.float32),
    ]


def own_attention(info, asked, pairs, first, last, after=()):
    group = len(asked)
    _, tok, width = asked[0].shape
    count = last - first
    return pl.pallas_call(
        functools.partial(own_kernel, group, tok, min(256, tok), first, last),
        out_shape=soft_shapes(count, tok, width),
        in_specs=[SMEM] + [ANY] * (count + group + len(after)),
        out_specs=[VMEM] * 2,
        scratch_shapes=soft_scratch(tok, width)
        + [
            pltpu.VMEM((count, tok, width), jnp.bfloat16),
            pltpu.VMEM((group, 2, tok, width), jnp.bfloat16),
            pltpu.SemaphoreType.DMA((count + group,)),
        ],
        compiler_params=params(60),
        name="own_attention",
    )(info, *asked[first:last], *pairs, *after)


def renorm_kernel(terms, info_ref, rate_ref, w_ref, *refs):
    out_ref = refs[-1]
    rows = out_ref.shape[1]
    mine = pl.ds(pl.multiple_of(info_ref[0] % (w_ref.shape[1] // rows) * rows, rows), rows)
    step = rate_ref[0] / info_ref[2].astype(jnp.float32)
    for c in range(w_ref.shape[0]):
        previous = w_ref[c, mine, :].astype(jnp.float32)
        summed = refs[0][c].astype(jnp.float32)
        for term in refs[1:terms]:
            summed = summed + term[c].astype(jnp.float32)
        updated = previous + step * summed
        old_norm = jnp.sqrt(jnp.sum(previous * previous, axis=1, keepdims=True) + eps)
        new_norm = jnp.sqrt(jnp.sum(updated * updated, axis=1, keepdims=True) + eps)
        out_ref[c] = (updated * (old_norm / new_norm)).astype(out_ref.dtype)


def renorm(info, rate, weights, sums, after=()):
    return pl.pallas_call(
        functools.partial(renorm_kernel, len(sums)),
        out_shape=jax.ShapeDtypeStruct(sums[0].shape, jnp.bfloat16),
        in_specs=[SMEM] * 2 + [VMEM] * (1 + len(sums)) + [ANY] * len(after),
        out_specs=VMEM,
        compiler_params=params(60),
        name="renorm",
    )(info, rate, weights, *sums, *after)


def cross_kernel(group, tok, behind, part, info_ref, *refs):
    pieces = behind * group
    out_ref, level_ref, acc, top, norm, qbuf, kvbuf, sems = refs[-8:]
    plane, member = info_ref[0], info_ref[1]
    moves = [(refs[d], qbuf.at[pl.ds(d, 1)]) for d in range(group)]
    moves += [(refs[group + at], kvbuf.at[at]) for at in range(pieces)]
    run([pltpu.make_async_copy(*move, sems.at[n]) for n, move in enumerate(moves)])
    scale = score_scale(qbuf.shape[-1])
    valid = jnp.maximum(behind - plane, 0) * group

    def piece(d, carry):
        at = member ^ d

        @pl.when(at >= valid)
        def _():
            parts = []
            for r in range(0, tok, part):
                where, keys = pl.ds(r, part), pl.ds(r, tok - r)
                mask = triangle(part, tok - r, r, r, False)
                parts.append((where, qbuf[d, where], kvbuf[d, 0, keys], kvbuf[d, 1, keys], mask))
            soft_steps(parts, scale, True, acc, top, norm)

        @pl.when(at < valid)
        def _():
            acc[...] = jnp.zeros_like(acc)
            norm[...] = jnp.zeros_like(norm)
            top[...] = jnp.full_like(top, NEG)

        def later(other, carry):
            e = other // group * group + (member ^ (other % group))
            parts = []
            for r in range(0, tok, part):
                where = pl.ds(r, part)
                parts.append((where, qbuf[d, where], kvbuf[e, 0], kvbuf[e, 1], None))
            soft_steps(parts, scale, False, acc, top, norm)
            return carry

        lax.fori_loop(jnp.maximum(at + 1, valid), pieces, later, 0)
        soft_close(scale, acc, top, norm, out_ref.at[d], level_ref.at[d])
        return carry

    lax.fori_loop(0, group, piece, 0)


def cross_attention(info, asked, earlier, after=()):
    group = len(asked)
    _, tok, width = asked[0].shape
    behind = len(earlier) // group
    operands = [*asked, *earlier, *after]
    return pl.pallas_call(
        functools.partial(cross_kernel, group, tok, behind, min(256, tok)),
        out_shape=soft_shapes(group, tok, width),
        in_specs=[SMEM] + [ANY] * len(operands),
        out_specs=[VMEM] * 2,
        scratch_shapes=soft_scratch(tok, width)
        + [
            pltpu.VMEM((group, tok, width), jnp.bfloat16),
            pltpu.VMEM((behind * group, 2, tok, width), jnp.bfloat16),
            pltpu.SemaphoreType.DMA((group + behind * group,)),
        ],
        compiler_params=params(60),
        name="cross_attention",
    )(info, *operands)


def fast_apply(rows, weights):
    gate = dot(rows, weights[0], NT)
    up = dot(rows, weights[1], NT)
    act = (gate * jax.nn.sigmoid(gate) * up).astype(jnp.bfloat16)
    return dot(act, weights[2], NN)


def first_kernel(group, tok, cuts, info_ref, w_any, *refs):
    out_ref, wbuf, qbuf, obuf, xbuf, lbuf, sems = refs[-7:]
    plane, member, first_len = info_ref[0], info_ref[1], info_ref[2]
    moves = [(w_any, wbuf)] + [(refs[d], qbuf.at[pl.ds(d, 1)]) for d in range(group)]
    for n, (first, last) in enumerate(cuts):
        into = pl.ds(first, last - first)
        rows, level = refs[group + 2 * n], refs[group + 2 * n + 1]
        moves += [(rows, obuf.at[into]), (level, lbuf.at[0, into])]
    rows, level = refs[group + 2 * len(cuts)], refs[group + 2 * len(cuts) + 1]
    moves += [(rows, xbuf), (level, lbuf.at[1])]
    run([pltpu.make_async_copy(*move, sems.at[n]) for n, move in enumerate(moves)])

    def piece(d, carry):
        first_tok = (plane * group + (member ^ d)) * tok
        own_log, cross_log = as_column(lbuf[0, d]), as_column(lbuf[1, d])
        own_part = 1.0 / (1.0 + jnp.exp2(cross_log - own_log))
        cross_part = 1.0 / (1.0 + jnp.exp2(own_log - cross_log))
        mixed = obuf[d].astype(jnp.float32) * own_part + xbuf[d].astype(jnp.float32) * cross_part
        out_ref[d] = mixed.astype(out_ref.dtype)

        @pl.when(first_tok < first_len)
        def _():
            token = first_tok + lax.broadcasted_iota(jnp.int32, (tok, 1), 0)
            fast = jnp.where(token < first_len, fast_apply(qbuf[d], wbuf), 0.0)
            out_ref[d] = (out_ref[d].astype(jnp.float32) + fast).astype(out_ref.dtype)

        return carry

    lax.fori_loop(0, group, piece, 0)


def first_rows(info, weights, asked, cuts, parts, after=()):
    group = len(asked)
    _, tok, width = asked[0].shape
    operands = [*asked, *parts]
    whole = pltpu.VMEM((group, tok, width), jnp.bfloat16)
    return pl.pallas_call(
        functools.partial(first_kernel, group, tok, cuts),
        out_shape=jax.ShapeDtypeStruct((group, tok, width), jnp.bfloat16),
        in_specs=[SMEM, ANY] + [ANY] * (len(operands) + len(after)),
        out_specs=VMEM,
        scratch_shapes=[
            pltpu.VMEM(weights.shape, jnp.bfloat16),
            whole,
            whole,
            whole,
            pltpu.VMEM((2, group, 8, tok), jnp.float32),
            pltpu.SemaphoreType.DMA((len(operands) + 1,)),
        ],
        compiler_params=params(60),
        name="first_rows",
    )(info, weights, *operands, *after)


def finish_kernel(group, tok, count, chunks, info_ref, place_ref, base_any, *refs):
    out_ref, wbuf, qbuf, bbuf, sems = refs[-5:]
    plane, member, first_len = info_ref[0], info_ref[1], info_ref[2]

    def base_copy(d):
        return pltpu.make_async_copy(base_any.at[d], bbuf.at[d], sems.at[group + chunks + d])

    moves = [(refs[d], qbuf.at[pl.ds(d, 1)]) for d in range(group)]
    if chunks == 1:
        moves.append((refs[group], wbuf))
    copies = [pltpu.make_async_copy(*move, sems.at[n]) for n, move in enumerate(moves)]
    for copy in copies:
        copy.start()
    for d in range(group):
        base_copy(d).start()
    if chunks > 1:
        own, near, far, near_on, far_on = refs[group : group + chunks]
        rows = own.shape[1]
        halves = [wbuf.at[:, pl.ds(half * rows, rows), :] for half in range(2)]
        for at_plane, pair in ((1, (near, own)), (2, (far, near)), (3, (far_on, near_on))):

            @pl.when(plane == at_plane)
            def _():
                run(
                    [
                        pltpu.make_async_copy(pair[half], halves[half], sems.at[group + half])
                        for half in range(2)
                    ]
                )

    for copy in copies:
        copy.wait()
    seg = tok // count

    def piece(d, carry):
        at = member ^ d
        first_tok = (plane * group + at) * tok
        base_copy(d).wait()

        @pl.when(first_tok + tok > first_len)
        def _():
            token = first_tok + lax.broadcasted_iota(jnp.int32, (tok, 1), 0)
            fast = jnp.where(token < first_len, 0.0, fast_apply(qbuf[d], wbuf))
            bbuf[d] = (bbuf[d].astype(jnp.float32) + fast).astype(bbuf.dtype)

        pick = as_column(place_ref[at]).astype(jnp.int32)
        pick = (pick == lax.broadcasted_iota(jnp.int32, (tok, tok), 1)).astype(jnp.bfloat16)
        sorted_rows = dot(pick, bbuf[d], NN)
        sorted_rows = sorted_rows.reshape(count, seg, sorted_rows.shape[-1])
        out_ref[:, at] = sorted_rows.astype(out_ref.dtype)
        return carry

    lax.fori_loop(0, group, piece, 0)


def finish_rows(info, places, new, base, asked, count):
    group = len(asked)
    _, tok, width = asked[0].shape
    whole = pltpu.VMEM((group, tok, width), jnp.bfloat16)
    return pl.pallas_call(
        functools.partial(finish_kernel, group, tok, count, len(new)),
        out_shape=jax.ShapeDtypeStruct((count, group, tok // count, width), jnp.bfloat16),
        in_specs=[SMEM, VMEM, ANY] + [ANY] * (group + len(new)),
        out_specs=VMEM,
        scratch_shapes=[
            pltpu.VMEM((3, new[0].shape[1] * min(2, len(new)), width), jnp.bfloat16),
            whole,
            whole,
            pltpu.SemaphoreType.DMA((2 * group + len(new),)),
        ],
        compiler_params=params(60),
        name="finish_rows",
    )(info, places, base, *asked, *new)


def norm_kernel(came_ref, scale_ref, gain_ref, out_ref):
    scaled = came_ref[0].astype(jnp.float32) * scale_ref[...] * gain_ref[...]
    out_ref[...] = jnp.swapaxes(scaled.astype(out_ref.dtype), 0, 1)


def norm_rows(came, scale, gain):
    planes, group, rows, width = came.shape
    return pl.pallas_call(
        norm_kernel,
        grid=(planes,),
        out_shape=jax.ShapeDtypeStruct((planes * rows, group, width), jnp.bfloat16),
        in_specs=[
            pl.BlockSpec((1, group, rows, width), lambda z: (z, 0, 0, 0)),
            pl.BlockSpec((1, rows, 1), lambda z: (z, 0, 0)),
            pl.BlockSpec((group, 1, width), lambda z: (0, 0, 0)),
        ],
        out_specs=pl.BlockSpec((rows, group, width), lambda z: (z, 0, 0)),
        compiler_params=params(20),
        name="norm_rows",
    )(came, scale, gain)


def pass_kernel(count, *refs):
    for n in range(count):
        refs[len(refs) - count + n][...] = refs[n][...]


def pass_after(values, after):
    return pl.pallas_call(
        functools.partial(pass_kernel, len(values)),
        out_shape=[jax.ShapeDtypeStruct(value.shape, value.dtype) for value in values],
        in_specs=[VMEM] * len(values) + [ANY] * len(after),
        out_specs=[VMEM] * len(values),
        compiler_params=params(20),
        name="pass_after",
    )(*values, *after)


def as_places(asked, group, tok):
    places = jnp.transpose(asked, (1, 0, 2)).reshape(group, 1, tok).astype(jnp.float32)
    return jnp.broadcast_to(places, (group, 8, tok))


def asked_places(slot_order, group, count):
    tok = slot_order.shape[0]
    seg, planes = tok // count, count // group
    wanted = (slot_order % tok).reshape(planes, 1, group * seg)
    wanted = jnp.broadcast_to(wanted, (planes, group, group * seg))
    wanted = wanted.reshape(count, group * seg)
    asked = lax.all_to_all(wanted, "seq", split_axis=0, concat_axis=0, tiled=True)
    return as_places(asked.reshape(count, group, seg), group, tok)


def per_device(
    queries, token_keys, token_values, fast_weights, learn_rate, out_gain, group_lengths, slot_order
):
    tok, group, width = queries.shape
    count = lax.axis_size("seq")
    seg = tok // count
    planes = count // group
    behind = WINDOW // (group * tok)
    position = lax.axis_index("seq")
    plane, member = position // group, position % group
    info = jnp.stack([plane, member, group_lengths[0]]).astype(jnp.int32)

    weights = lax.dynamic_index_in_dim(fast_weights, member, 1, keepdims=False)
    weights = jnp.transpose(weights, (1, 0, 2))
    rate = lax.dynamic_slice_in_dim(learn_rate, member, 1)
    places = asked_places(slot_order, group, count)

    last = group - 1
    mine = split_heads(info, [token_keys, token_values])
    pairs = list(mine)
    if last:
        pairs = trade(pairs[:last], count)
        (late,) = pass_after(mine[last:], [*pairs[1:], weights, places])
        pairs = pairs + [lax.ppermute(late, "seq", swap_pairs(count, last))]
    carried = [weight_sums(info, weights, pairs, 0, last)[0]] if last else []
    asked = trade(split_heads(info, [queries], carried), count)
    shifts = [back * group for back in range(behind, 0, -1)]
    sources = [plane_pairs(count, shift) for shift in shifts]
    near = [[lax.ppermute(pair, "seq", source) for pair in pairs[:last]] for source in sources]
    waits = [*asked[:3], *near[-1][:2]]
    direct = planes == 4
    chunks = 2 if direct else 1
    *sums, onward = weight_sums(info, weights, pairs, last, group, carried, waits, chunks)
    earlier = []
    for source, arrays in zip(sources, near):
        earlier.extend(arrays + [lax.ppermute(onward, "seq", source)])

    groups = [[z * group + m for z in range(planes)] for m in range(group)]
    cuts = [(0, group)]
    parts = list(own_attention(info, asked, pairs, 0, group))

    def between(value, hops):
        return lax.ppermute(
            value, "seq", [(a * group + m, b * group + m) for a, b in hops for m in range(group)]
        )

    if direct:
        own, other = sums
        sums = [own, between(other, [(0, 1), (1, 0)]), between(own, [(2, 0)]), between(other, [(2, 1)])]
    else:
        sums = [
            lax.psum_scatter(
                sums[0], "seq", scatter_dimension=1, axis_index_groups=groups, tiled=True
            )
        ]
    part = renorm(info, rate, weights, sums, parts[1:] + earlier[min(2, last) :])
    if direct:
        near, far = between(part, [(0, 1), (1, 2)]), between(part, [(0, 2)])
    else:
        new = [lax.all_gather(part, "seq", axis_index_groups=groups, axis=1, tiled=True)]
    parts.extend(cross_attention(info, asked, earlier, [part]))
    base = first_rows(info, weights, asked, cuts, parts)
    if direct:
        (near_on,) = pass_after([near], parts[-1:])
        (far_on,) = pass_after([far], [base])
        new = [part, near, far, between(near_on, [(2, 3)]), between(far_on, [(2, 3)])]
    leaving = finish_rows(info, places, new, base, asked, count)

    came = lax.all_to_all(leaving, "seq", split_axis=0, concat_axis=0, tiled=True)
    came = came.reshape(planes, group, group * seg, width)
    wide = came.astype(jnp.float32)
    power = lax.psum(jnp.sum(wide * wide, axis=(1, 3)), "head")
    scale = lax.rsqrt(power / (group * lax.axis_size("head") * width) + eps)
    return norm_rows(came, scale[:, :, None], out_gain[:, None, :])


def solution(mesh):
    return jax.shard_map(
        per_device,
        mesh=mesh,
        in_specs=(
            P("seq", "head", None),
            P("seq", "head", None),
            P("seq", "head", None),
            P(None, "head", None, None),
            P("head"),
            P("head", None),
            P(),
            P("seq"),
        ),
        out_specs=P("seq", "head", None),
        check_vma=False,
    )
```
